32 devices in a mesh: section: 2 (over x), ctx: 4 (over z), fsdp: 4 (over y, core).
Axes of the slice: x: 2, y: 2, z: 4, core: 2. Of those that a mesh axis runs over, the one named last changes fastest.
Arguments:
- inputs: bfloat16 [4, 2, 1536, 576], P('fsdp', None, 'ctx'), may hold values from -6 to 6
- lengths: int32 [4, 2, 4], P('fsdp'), may hold values from 1 to 1344, 1536 in all within a row
- cotangent: bfloat16 [4, 2, 1536, 576], P('fsdp', None, 'ctx'), may hold values from -6 to 6
- w_query: bfloat16 [2, 576, 576], P('section', ('ctx', 'fsdp')), may hold values from -0.25 to 0.25
- w_key: bfloat16 [2, 576, 192], P('section', ('ctx', 'fsdp')), may hold values from -0.25 to 0.25
- w_value: bfloat16 [2, 576, 192], P('section', ('ctx', 'fsdp')), may hold values from -0.25 to 0.25
- w_out: bfloat16 [2, 576, 576], P('section', ('ctx', 'fsdp')), may hold values from -2.5 to 2.5
- w_gate: bfloat16 [2, 576, 1536], P('section', ('ctx', 'fsdp')), may hold values from -0.25 to 0.25
- w_up: bfloat16 [2, 576, 1536], P('section', ('ctx', 'fsdp')), may hold values from -0.25 to 0.25
- w_down: bfloat16 [2, 1536, 576], P('section', ('ctx', 'fsdp')), may hold values from -0.15625 to 0.15625
- g_attn: bfloat16 [2, 576], P('section', ('ctx', 'fsdp')), may hold values from 0.5 to 1.5
- g_mlp: bfloat16 [2, 576], P('section', ('ctx', 'fsdp')), may hold values from 0.5 to 1.5
Outputs:
- edges: float32 [2, 4, 2, 1536, 576], P('section', 'fsdp', None, 'ctx')
- grad_query: float32 [2, 576, 576], P('section', ('ctx', 'fsdp'))
- grad_key: float32 [2, 576, 192], P('section', ('ctx', 'fsdp'))
- grad_value: float32 [2, 576, 192], P('section', ('ctx', 'fsdp'))
- grad_out: float32 [2, 576, 576], P('section', ('ctx', 'fsdp'))
- grad_gate: float32 [2, 576, 1536], P('section', ('ctx', 'fsdp'))
- grad_up: float32 [2, 576, 1536], P('section', ('ctx', 'fsdp'))
- grad_down: float32 [2, 1536, 576], P('section', ('ctx', 'fsdp'))
- grad_attn_gain: float32 [2, 576], P('section', ('ctx', 'fsdp'))
- grad_mlp_gain: float32 [2, 576], P('section', ('ctx', 'fsdp'))
The draws below stay inside these ranges and needn't reach their ends.
Inputs may be any that keep to these rules, and one draw needn't show every extreme that they name: Each row of 4 lengths sums to 1536; the largest in each row is exactly 1344.
All inputs are finite; a program needn't handle non-finite values.
Results may differ from the reference program's by a relative error of at most 0.035.
Values may be sent and summed in bfloat16 or wider, within the bound.
No kernel may reach another device: no remote copies, remote signals or barrier semaphores. Data moves between devices by JAX's collectives and lax.ppermute only.
A program may use at most 128 MiB of HBM per device.

```python
import math
import jax
import jax.numpy as jnp
import numpy as np
from jax import lax

D = 576
HQ = 9
KV = 3
HD = 64
FF = 1536
LAYERS = 2
DOCS = 4
BLK = 384
MB = 2
SEQ = 1536
NSEQ = 4


def block_levels(rng, dims, split, least, top_value):
    def one(position, shards_of):
        steps = jax.random.uniform(jax.random.fold_in(jax.random.fold_in(rng, 6), position), (shards_of,), jnp.float32, least / len(split), top_value / len(split))
        return jnp.repeat(jnp.exp(steps), dims[position] // shards_of).reshape((-1,) + (1,) * (len(dims) - position - 1))

    level = one(*split[0])
    for cut in split[1:]:
        level = level * one(*cut)
    return level


def length_profile(number_of, total, bound, lean):
    portions = [(1 << 20) // math.isqrt(rank ** lean) + 1 for rank in range(2, number_of + 1)]
    spare, given = total - bound - (number_of - 1), [1] * (number_of - 1)
    while spare > 0:
        free = [i for i in range(number_of - 1) if given[i] < bound]
        pool, budget = sum([portions[i] for i in free]), spare
        for i in free:
            addition = min(bound - given[i], max(1, budget * portions[i] // pool), spare)
            given[i] = given[i] + addition
            spare = spare - addition
    return np.array([bound] + given)


def ragged(stream_key, count, total, bound, skew):
    if count == 2:
        one = jax.random.randint(stream_key, (), max(1, total - bound), min(bound, total - 1) + 1)
        return jnp.stack([one, total - one])
    tallies = jnp.asarray(length_profile(count, total, bound, skew), jnp.int32)
    couples = (count - 1) // 2
    source_of, taker = tallies[1:1 + 2 * couples:2], tallies[2:2 + 2 * couples:2]
    room = jnp.minimum(source_of - 1, bound - taker)
    shifted = jax.random.randint(jax.random.fold_in(stream_key, 1), (couples,), 0, 1 << 20) % (room + 1)
    tallies = tallies.at[1:1 + 2 * couples:2].set(source_of - shifted).at[2:2 + 2 * couples:2].set(taker + shifted)
    return tallies[jax.random.permutation(jax.random.fold_in(stream_key, 2), count)]


def bell_draw(rng, dims, deviation, limit, cuts=(), kind=jnp.bfloat16):
    loudness = block_levels(rng, dims, cuts, -0.22, 0.18) if cuts else 1.0
    array = jax.random.normal(rng, dims, jnp.float32) * deviation * loudness
    return jnp.minimum(jnp.maximum(array, -limit), limit).astype(kind)


def setup_inputs(seed: int = 0) -> dict:
    splits = jax.random.split(jax.random.key(seed), 13)
    return {
        "inputs": bell_draw(splits[0], (NSEQ, MB, SEQ, D), 1.0, 6.0, ((0, 4), (2, 4))),
        "lengths": jax.vmap(lambda own: ragged(own, DOCS, SEQ, SEQ - BLK // 2, 0))(jax.random.split(splits[1], NSEQ * MB)).reshape((NSEQ, MB, DOCS)).astype(jnp.int32),
        "cotangent": bell_draw(splits[2], (NSEQ, MB, SEQ, D), 1.0, 6.0, ((0, 4), (2, 4))),
        "w_query": bell_draw(splits[3], (LAYERS, D, HQ * HD), D ** -0.5, 0.25, ((0, 2), (1, 16))),
        "w_key": bell_draw(splits[4], (LAYERS, D, KV * HD), D ** -0.5, 0.25, ((0, 2), (1, 16))),
        "w_value": bell_draw(splits[5], (LAYERS, D, KV * HD), D ** -0.5, 0.25, ((0, 2), (1, 16))),
        "w_out": bell_draw(splits[6], (LAYERS, HQ * HD, D), (max(1, HQ * HD * 16 // SEQ)) ** -0.5, 2.5, ((0, 2), (1, 16))),
        "w_gate": bell_draw(splits[7], (LAYERS, D, FF), D ** -0.5, 0.25, ((0, 2), (1, 16))),
        "w_up": bell_draw(splits[8], (LAYERS, D, FF), D ** -0.5, 0.25, ((0, 2), (1, 16))),
        "w_down": bell_draw(splits[9], (LAYERS, FF, D), FF ** -0.5, 0.15625, ((0, 2), (1, 16))),
        "g_attn": jnp.clip(1.0 + 0.1 * jax.random.normal(splits[10], (LAYERS, D), jnp.float32), 0.5, 1.5).astype(jnp.bfloat16),
        "g_mlp": jnp.clip(1.0 + 0.1 * jax.random.normal(splits[11], (LAYERS, D), jnp.float32), 0.5, 1.5).astype(jnp.bfloat16),
    }


@jax.custom_vjp
def low(v):
    return lax.optimization_barrier(v.astype(jnp.bfloat16)).astype(jnp.float32)

@jax.custom_vjp
def low_back(v):
    return v

def low_keep(v):
    return (low(v), None)

def low_pass(kept, grad):
    return (grad,)

def back_keep(v):
    return (v, None)

def back_low(kept, grad):
    return (low(grad),)
low.defvjp(low_keep, low_pass)
low_back.defvjp(back_keep, back_low)
EPSILON = 1e-05
THETA = 10000.0
HIGHEST = lax.Precision.HIGHEST

def product(left, right):
    return jnp.dot(left, right, precision=HIGHEST)

def doc_layout(lengths, positions):
    doc_ends = jnp.cumsum(lengths)
    passed = (positions[:, None] >= doc_ends[None, :]).astype(lengths.dtype)
    starts = lax.optimization_barrier(jnp.sum(passed * lengths[None, :], axis=1))
    return (starts, positions - starts)

def rotate_half(values):
    middle = values.shape[-1] // 2
    return jnp.concatenate([-values[..., middle:], values[..., :middle]], axis=-1)

def angle_tables(offsets, head_width):
    middle = head_width // 2
    frequency = THETA ** (-jnp.arange(middle, dtype=jnp.float32) * 2.0 / head_width)
    angles = offsets.astype(jnp.float32)[:, None] * frequency[None, :]
    cosine = jnp.concatenate([jnp.cos(angles), jnp.cos(angles)], axis=-1)[:, None, :]
    sine_table = jnp.concatenate([jnp.sin(angles), jnp.sin(angles)], axis=-1)[:, None, :]
    return (cosine, sine_table)

def rms_scale(layer_input, gain):
    return layer_input * lax.rsqrt(lax.optimization_barrier(jnp.mean(layer_input * layer_input, axis=-1, keepdims=True)) + EPSILON) * gain

def attention(queries, keys_turned, values_all, positions, starts):
    seq_len = queries.shape[0]
    block_rows = 2 * BLK
    keys_full = jnp.repeat(keys_turned, HQ // KV, axis=1)
    values_full = jnp.repeat(values_all, HQ // KV, axis=1)

    def one_block(block_index):
        first_row = block_index * block_rows
        query_rows = lax.dynamic_slice_in_dim(queries, first_row, block_rows, 0)
        query_pos = lax.dynamic_slice_in_dim(positions, first_row, block_rows, 0)
        query_start = lax.dynamic_slice_in_dim(starts, first_row, block_rows, 0)
        scores = low_back(jnp.einsum('qhd,khd->hqk', query_rows, keys_full, precision=HIGHEST)) * HD ** (-0.5)
        allowed = (positions[None, :] <= query_pos[:, None]) & (positions[None, :] >= query_start[:, None])
        scores = jnp.where(allowed[None], scores, -1e+30)
        row_peak = lax.optimization_barrier(jnp.max(scores, axis=-1, keepdims=True))
        weights = jnp.exp(scores - row_peak)
        probabilities = low(weights / lax.optimization_barrier(jnp.sum(weights, axis=-1, keepdims=True)))
        return jnp.einsum('hqk,khd->qhd', probabilities, values_full, precision=HIGHEST).reshape(block_rows, -1)
    blocks = lax.map(jax.checkpoint(one_block), jnp.arange(seq_len // block_rows, dtype=jnp.int32))
    return blocks.reshape(seq_len, -1)

def layer(layer_input, params, lengths):
    w_query, w_key, w_value, w_out, w_gate, w_up, w_down, g_attn, g_mlp = params
    seq_len = layer_input.shape[0]
    positions = jnp.arange(seq_len, dtype=jnp.int32)
    starts, offsets = doc_layout(lengths, positions)
    cosine, sine_table = angle_tables(offsets, HD)
    normed = low(rms_scale(layer_input, g_attn))
    queries = low_back(product(normed, w_query)).reshape(seq_len, HQ, HD)
    queries = low(queries * cosine + rotate_half(queries) * sine_table)
    keys_turned = low_back(product(normed, w_key)).reshape(seq_len, KV, HD)
    keys_turned = low(keys_turned * cosine + rotate_half(keys_turned) * sine_table)
    values_all = low(low_back(product(normed, w_value))).reshape(seq_len, KV, HD)
    attended = attention(queries, keys_turned, values_all, positions, starts)
    middle_state = layer_input + low_back(product(low(low_back(attended)), w_out))
    normed_mlp = low(rms_scale(middle_state, g_mlp))
    gate_value = low_back(product(normed_mlp, w_gate))
    up_value = low_back(product(normed_mlp, w_up))
    hidden = low(jax.nn.silu(gate_value) * up_value)
    return middle_state + low_back(product(hidden, w_down))

def reference(inputs, lengths, cotangent, w_query, w_key, w_value, w_out, w_gate, w_up, w_down, g_attn, g_mlp):
    params = tuple((weight.astype(jnp.float32) for weight in (w_query, w_key, w_value, w_out, w_gate, w_up, w_down, g_attn, g_mlp)))
    flat_inputs = inputs.astype(jnp.float32).reshape(-1, SEQ, D)
    flat_lengths = lengths.reshape(-1, DOCS)

    def forward(sequences, stacked):
        first_layer = tuple((weight[0] for weight in stacked))
        second_layer = tuple((weight[1] for weight in stacked))

        def one_sequence(carry_value, scan_item):
            sequence, sequence_lengths = scan_item
            between = low(low_back(layer(sequence, first_layer, sequence_lengths)))
            return (carry_value, layer(between, second_layer, sequence_lengths))
        _, results = lax.scan(one_sequence, jnp.zeros((), jnp.float32), (sequences, flat_lengths))
        return results
    outputs, pullback = jax.vjp(forward, flat_inputs, params)
    input_grad, param_grads = pullback(cotangent.astype(jnp.float32).reshape(outputs.shape))
    edges = jnp.stack([input_grad, outputs]).reshape((2,) + inputs.shape)
    return (edges, param_grads[0], param_grads[1], param_grads[2], param_grads[3], param_grads[4], param_grads[5], param_grads[6], param_grads[7], param_grads[8])
```

```python
import functools

import jax
import jax.numpy as jnp
from jax import lax
from jax.experimental import pallas as pl
from jax.experimental.pallas import tpu as pltpu
from jax.sharding import PartitionSpec as P

D = 576
HQ = 9
KV = 3
HD = 64
GROUP = HQ // KV
QW = HQ * HD
KW = KV * HD
TURNED = QW + KW
MIXED = 2 * QW + 2 * KW
HALF = MIXED // 2

EPSILON = 1e-05
THETA = 10000.0
BF = jnp.bfloat16
F32 = jnp.float32
I32 = jnp.int32
MIB = 1024 * 1024


def mm(left, right):
    return jnp.dot(left, right, preferred_element_type=F32)


def mm_nt(left, right):
    return lax.dot_general(left, right, (((1,), (1,)), ((), ())), preferred_element_type=F32)


def mm_tn(left, right):
    return lax.dot_general(left, right, (((0,), (0,)), ((), ())), preferred_element_type=F32)


def struct(shape, dtype):
    return jax.ShapeDtypeStruct(shape, dtype)


def flip(count, bit):
    return [(i, i ^ bit) for i in range(count)]


def ring(count, steps):
    return [(i, (i + steps) % count) for i in range(count)]


def swap_core(value):
    return lax.ppermute(value, "fsdp", flip(4, 1))


def swap_y(value):
    return lax.ppermute(value, "fsdp", flip(4, 2))


def swap_zpair(value):
    return lax.ppermute(value, "ctx", flip(4, 1))


def swap_x(value):
    return lax.ppermute(value, "section", flip(2, 1))


def spread_pairs(odd):
    pairs = []
    for z in range(4):
        for f in range(4):
            y, c = f // 2, f % 2
            half = 2 * z + odd
            member = min(half, 7 - half)
            pairs.append((z * 4 + f, (2 * c + member // 2) * 4 + 2 * y + member % 2))
    return pairs


def backwards(pairs):
    return [(target, source) for source, target in pairs]


def turn_tables(offsets):
    middle = HD // 2
    frequency = THETA ** (-jnp.arange(middle, dtype=F32) * 2.0 / HD)
    angles = offsets.astype(F32)[:, None] * frequency[None, :]
    cosine, sine = jnp.cos(angles), jnp.sin(angles)
    return jnp.concatenate([cosine] * 4, axis=1), jnp.concatenate([-sine, sine] * 2, axis=1)


def turn(values, cosine, sine):
    low = lax.broadcasted_iota(I32, (values.shape[0], 128), 1) % HD < HD // 2
    tiles = []
    for first in range(0, values.shape[1], 128):
        tile = values[:, first : first + 128]
        beside = jnp.where(low, pltpu.roll(tile, 128 - HD // 2, 1), pltpu.roll(tile, HD // 2, 1))
        tiles.append(tile * cosine + beside * sine)
    return jnp.concatenate(tiles, axis=1)


def norm(values, gain):
    inverse = lax.rsqrt(jnp.mean(values * values, axis=-1, keepdims=True) + EPSILON)
    scaled = values * inverse
    return inverse, scaled, (scaled * gain).astype(BF)


def norm_back(d_normed, scaled, inverse, gain):
    gain_grad = jnp.sum(d_normed * scaled, axis=0, keepdims=True)
    d_scaled = d_normed * gain
    d_source = inverse * (d_scaled - scaled * jnp.mean(d_scaled * scaled, axis=-1, keepdims=True))
    return d_source, gain_grad


def split_heads(piece_refs, key_scr, value_scr, parts):
    count = sum(ref.shape[0] for ref in piece_refs)
    index = 0
    for ref in piece_refs:
        rows = ref.shape[1] // parts
        for slot in range(ref.shape[0]):
            for part in range(parts):
                block = ref[slot, part * rows : (part + 1) * rows, :]
                at = pl.ds((part * count + index) * rows, rows)
                for group in range(KV):
                    key_scr[group, at, :] = block[:, group * HD : (group + 1) * HD]
                    value_scr[group, at, :] = block[:, KW + group * HD : KW + (group + 1) * HD]
            index += 1


def each_job(jobs, tile, visit):
    if tile is None:
        for first, rows, keys in jobs:
            visit(first, rows, keys)
        return
    _, rows, keys = jobs[0]

    @pl.loop(0, rows // tile)
    def _(step):
        visit(pl.multiple_of(step * tile, tile), tile, keys)


def store(slot, refs, at, value):
    for index, ref in enumerate(refs):

        @pl.when(slot == index)
        def _(ref=ref):
            ref[at] = value


def job_bias(first, rows, keys, position_ref, start_ref, key_position_ref):
    at = key_position_ref[:, :keys]
    allowed = (at <= position_ref[pl.ds(first, rows), :]) & (at >= start_ref[pl.ds(first, rows), :])
    return jnp.where(allowed, 0.0, -1e30)


def project_kernel(source_ref, mixed_ref, gain_ref, cosine_ref, sine_ref, query_ref, pairs_ref):
    _, _, normed = norm(source_ref[...].astype(F32), gain_ref[...])
    both = turn(mm(normed, mixed_ref[:, :TURNED]), cosine_ref[...], sine_ref[...]).astype(BF)
    edge = (2 * QW + KW) // 128 * 128
    values = mm(normed, mixed_ref[:, edge:])[:, 2 * QW + KW - edge :].astype(BF)
    query_ref[...] = both[:, :QW]
    pairs_ref[...] = jnp.concatenate([both[:, QW:], values], axis=1)


def attend_kernel(
    jobs, tile, parts, pieces,
    source_ref, query_ref, position_ref, start_ref, key_position_ref, mixed_ref, *refs,
):
    piece_refs, refs = refs[:pieces], refs[pieces:]
    attended_ref, log_ref, middle_ref = refs[:3]
    query_scr, key_scr, value_scr, out_scr, log_scr = refs[3:]
    split_heads(piece_refs, key_scr, value_scr, parts)
    for head in range(HQ):
        query_scr[head] = query_ref[:, head * HD : (head + 1) * HD] * jnp.asarray(HD**-0.5, BF)

    def visit(first, rows, keys):
        bias = job_bias(first, rows, keys, position_ref, start_ref, key_position_ref)
        at = pl.ds(first, rows)

        @pl.loop(0, KV)
        def _(group):
            key = key_scr[group, :keys, :]
            value = value_scr[group, :keys, :]
            for member in range(GROUP):
                head = group * GROUP + member
                scores = mm_nt(query_scr[head, at, :], key) + bias
                peak = jnp.max(scores, axis=1, keepdims=True)
                weights = jnp.exp(scores - peak)
                total = jnp.sum(weights, axis=1, keepdims=True)
                out_scr[head, at, :] = mm(weights.astype(BF), value) * (1.0 / total)
                log_scr[head, at, :] = peak + jnp.log(total)

    each_job(jobs, tile, visit)
    out = jnp.concatenate([out_scr[head] for head in range(HQ)], axis=1)
    attended_ref[...] = out
    log_ref[...] = jnp.concatenate([log_scr[head] for head in range(HQ)], axis=1)
    added = mm(out.astype(BF), mixed_ref[:, TURNED : TURNED + QW])
    middle_ref[...] = source_ref[...].astype(F32) + added


def mlp_kernel(middle_ref, gate_ref, up_ref, down_ref, gain_ref, result_ref, normed_scr, total_scr):
    middle = middle_ref[...]
    normed_scr[...] = norm(middle, gain_ref[...])[2]
    total_scr[...] = middle
    width = 384

    @pl.loop(0, gate_ref.shape[1] // width)
    def _(step):
        at = pl.ds(pl.multiple_of(step * width, width), width)
        gate = mm(normed_scr[...], gate_ref[:, at])
        up = mm(normed_scr[...], up_ref[:, at])
        hidden = (gate * jax.nn.sigmoid(gate) * up).astype(BF)
        total_scr[...] += mm(hidden, down_ref[at, :])

    result_ref[...] = total_scr[...].astype(BF)


def mlp_back_kernel(
    core_ref, d_result_ref, middle_ref, mixed_ref, gate_ref, up_ref, down_ref, gain_ref, *refs
):
    packed_refs, (gain_grad_ref, d_middle_ref, d_out_ref, normed_scr, total_scr) = refs[:2], refs[2:]
    core = core_ref[0]
    gain = gain_ref[...]
    inverse, scaled, normed = norm(middle_ref[...], gain)
    normed_scr[...] = normed
    total_scr[...] = jnp.zeros_like(total_scr)
    width = 384

    @pl.loop(0, gate_ref.shape[1] // width)
    def _(step):
        at = pl.ds(pl.multiple_of(step * width, width), width)
        low = d_result_ref[...]
        normed = normed_scr[...]
        gate = mm(normed, gate_ref[:, at])
        up = mm(normed, up_ref[:, at])
        d_hidden = mm_nt(low, down_ref[at, :])
        sigmoid = jax.nn.sigmoid(gate)
        silu = gate * sigmoid
        d_gate = (d_hidden * up * sigmoid * (1.0 + gate * (1.0 - sigmoid))).astype(BF)
        d_up = (d_hidden * silu).astype(BF)
        hidden = (silu * up).astype(BF)
        total_scr[...] += mm_nt(d_gate, gate_ref[:, at]) + mm_nt(d_up, up_ref[:, at])
        gate_grad = mm_tn(normed, d_gate)
        up_grad = mm_tn(normed, d_up)
        down_grad = mm_tn(hidden, low)
        slot = (step // 2) ^ core
        columns = pl.ds(pl.multiple_of((step % 2) * width, width), width)
        wide = [
            jnp.concatenate([grad[72 * k : 72 * k + 72] for grad in (gate_grad, up_grad)], axis=0)
            for k in range(8)
        ]
        wide = jnp.stack(wide).astype(BF)
        store(slot, packed_refs, (slice(None), slice(0, 144), columns), wide)
        down_grad = down_grad.reshape(2, 2, 96, D).astype(BF)
        down_grad = jnp.concatenate([down_grad, jnp.zeros((2, 2, 96, HALF - D), BF)], axis=3)
        for side in (0, 1):
            at = (pl.ds(2 * step, 2), slice(144, 240), slice(None))
            store(core ^ side, packed_refs, at, down_grad[:, side])

    d_mlp, gain_grad = norm_back(total_scr[...], scaled, inverse, gain)
    gain_grad_ref[...] = gain_grad
    d_middle = d_result_ref[...].astype(F32) + d_mlp
    d_middle_ref[...] = d_middle
    d_out_ref[...] = mm_nt(d_middle.astype(BF), mixed_ref[:, TURNED : TURNED + QW]).astype(BF)


def attend_back_kernel(
    jobs, tile, parts, pieces,
    d_out_ref, attended_ref, log_ref, query_ref, position_ref, start_ref, key_position_ref, *refs,
):
    piece_refs, refs = refs[:pieces], refs[pieces:]
    d_query_ref, d_pairs_ref = refs[:2]
    (
        query_scr, key_scr, value_scr, d_out_scr, log_scr, delta_scr, d_query_scr,
        d_key_scr, d_value_scr,
    ) = refs[2:]
    d_out = d_out_ref[...]
    split_heads(piece_refs, key_scr, value_scr, parts)
    for head in range(HQ):
        at = slice(head * HD, (head + 1) * HD)
        query_scr[head] = query_ref[:, at] * jnp.asarray(HD**-0.5, BF)
        d_out_scr[head] = d_out[:, at]
        log_scr[head] = log_ref[:, head : head + 1]
        delta_scr[head] = jnp.sum(d_out[:, at].astype(F32) * attended_ref[:, at], 1, keepdims=True)
    d_key_scr[...] = jnp.zeros_like(d_key_scr)
    d_value_scr[...] = jnp.zeros_like(d_value_scr)

    def visit(first, rows, keys):
        bias = job_bias(first, rows, keys, position_ref, start_ref, key_position_ref)
        at = pl.ds(first, rows)

        @pl.loop(0, KV)
        def _(group):
            key = key_scr[group, :keys, :]
            value = value_scr[group, :keys, :]
            for member in range(GROUP):
                head = group * GROUP + member
                query = query_scr[head, at, :]
                d_out = d_out_scr[head, at, :]
                chances = jnp.exp(mm_nt(query, key) + bias - log_scr[head, at, :])
                d_chances = mm_nt(d_out, value)
                d_scores = (chances * (d_chances - delta_scr[head, at, :])).astype(BF)
                d_query_scr[head, at, :] = mm(d_scores, key) * HD**-0.5
                d_value_scr[group, :, :keys] += mm_tn(d_out, chances.astype(BF))
                d_key_scr[group, :, :keys] += mm_tn(query, d_scores)

    each_job(jobs, tile, visit)
    d_query_ref[...] = jnp.concatenate([d_query_scr[head] for head in range(HQ)], axis=1)
    count, rows = d_pairs_ref.shape[0], d_pairs_ref.shape[1] // parts
    for first in range(0, count * parts, parts):
        at = slice(first * rows, (first + parts) * rows)
        grads = [scr[group, :, at].T for scr in (d_key_scr, d_value_scr) for group in range(KV)]
        grads = jnp.concatenate(grads, axis=1).astype(BF)
        for index in range(parts):
            part, piece = divmod(first + index, count)
            d_pairs_ref[piece, part * rows : (part + 1) * rows, :] = grads[
                index * rows : (index + 1) * rows
            ]


def input_kernel(
    adds, core_ref, source_ref, attended_ref, d_middle_ref, d_query_ref, mixed_ref, gain_ref,
    mlp_gain_grad_ref, cosine_ref, sine_ref, *refs,
):
    add_refs, d_source_ref, packed_refs = refs[:adds], refs[adds], refs[adds + 1 :]
    core = core_ref[0]
    gain = gain_ref[...]
    inverse, scaled, normed = norm(source_ref[...].astype(F32), gain)
    d_pairs = sum(ref[...].astype(F32) for ref in add_refs)
    d_both = jnp.concatenate([d_query_ref[...], d_pairs[:, :KW]], axis=1)
    d_both = turn(d_both, cosine_ref[...], -sine_ref[...]).astype(BF)
    d_values = d_pairs[:, KW:].astype(BF)
    d_middle = d_middle_ref[...]
    edge = (2 * QW + KW) // 128 * 128
    lead = 2 * QW + KW - edge
    d_tail = jnp.concatenate([jnp.zeros((d_values.shape[0], lead), BF), d_values], axis=1)
    d_normed = mm_nt(d_both, mixed_ref[:, :TURNED]) + mm_nt(d_tail, mixed_ref[:, edge:])
    d_attn, gain_grad = norm_back(d_normed, scaled, inverse, gain)
    d_source_ref[...] = (d_middle + d_attn).astype(BF)
    first = mm_tn(normed, d_both)
    second = jnp.concatenate(
        [
            mm_tn(attended_ref[...].astype(BF), d_middle.astype(BF)),
            mm_tn(normed, d_values),
        ],
        axis=1,
    )
    gains = (gain_grad, mlp_gain_grad_ref[...])
    for half, grad in enumerate((first, second)):
        blocks = []
        for block in range(8):
            at = 36 * (2 * block + half)
            tail = jnp.concatenate([g[:, at : at + 36] for g in gains] + [jnp.zeros((6, 36), F32)])
            tail = jnp.concatenate([tail, jnp.zeros((8, HALF - 36), F32)], axis=1)
            blocks.append(jnp.concatenate([grad[72 * block : 72 * block + 72], tail], axis=0))
        store(half ^ core, packed_refs, Ellipsis, jnp.stack(blocks).astype(BF))


def join_rows(parts, first):
    return jnp.concatenate([part.astype(F32)[first : first + 72] for part in parts]).astype(BF)


def assemble_kernel(mixed, index_ref, *refs):
    pieces, outs = refs[:16], refs[16:]
    x, z, y, core = (index_ref[i] for i in range(4))
    for place, steps in enumerate((0, 1, 3, 2)):
        row = (z + 4 - steps) % 4
        at = pl.ds(pl.multiple_of(row * 144, 144), 144)
        for cross in (0, 1):
            first = 8 * (place // 2) + 4 * cross
            here, there = (
                [pieces[first + 2 * dx + dy][place % 2] for dy in (0, 1)] for dx in (0, 1)
            )
            here, there = (
                [jnp.where(y == 0, *part), jnp.where(y == 0, *part[::-1])] for part in (here, there)
            )
            sides = [
                jnp.concatenate(
                    [jnp.where(x == 0, a, b), jnp.where(x == 0, b, a)], axis=1
                )
                for a, b in zip(here, there)
            ]
            side = core ^ cross
            columns = pl.ds(pl.multiple_of(side * HALF, HALF), HALF)
            if mixed:
                outs[0][at, columns] = join_rows(sides, 0)
                for beside, part in enumerate(sides):
                    outs[1][4 * row + 2 * beside + side] = part[64:80, :128].astype(F32)
            else:
                outs[0][at, columns] = join_rows(sides, 0)
                outs[1][at, columns] = join_rows(sides, 72)
                for beside, part in enumerate(sides):
                    rows = pl.ds(pl.multiple_of((4 * row + 2 * beside + side) * 96, 96), 96)
                    outs[2][rows, :] = part[144:240, :D]


class Fast:
    parts = 2
    tile = None

    def __init__(self):
        self.section = lax.axis_index("section")
        self.z = lax.axis_index("ctx")
        f = lax.axis_index("fsdp")
        self.y = f // 2
        self.core = f % 2


    def positions_of(self, dz, dc, rows):
        member = 2 * ((self.z % 2) ^ dz) + (self.core ^ dc)
        iota = jnp.arange(rows // 2, dtype=I32)
        return jnp.concatenate([half * (rows // 2) + iota for half in (member, 7 - member)])

    def lengths(self, lengths):
        mine = lax.dynamic_index_in_dim(lengths[0], self.section, 0, keepdims=False)
        other = swap_core(mine)
        return jnp.where(self.z // 2 == self.core, mine, other)

    def spread(self, block):
        half = block.shape[0] // 2
        even, odd = (
            lax.ppermute(block[k * half : (k + 1) * half], ("ctx", "fsdp"), spread_pairs(k))
            for k in (0, 1)
        )
        low = jnp.where(self.core == 0, even, odd)
        return jnp.concatenate([low, jnp.where(self.core == 0, odd, even)], axis=0)

    def unspread(self, block):
        half = block.shape[0] // 2
        low, high = block[:half], block[half:]
        parts = (jnp.where(self.core == 0, low, high), jnp.where(self.core == 0, high, low))
        return jnp.concatenate(
            [
                lax.ppermute(part, ("ctx", "fsdp"), backwards(spread_pairs(k)))
                for k, part in enumerate(parts)
            ],
            axis=0,
        )

    def key_positions(self, rows):
        full = jnp.stack([self.positions_of(dz, dc, rows) for dc in (0, 1) for dz in (0, 1)])
        return full.reshape(4, 2, rows // 2).swapaxes(0, 1).reshape(1, -1)

    def jobs(self, rows, keys):
        return ((0, rows // 2, keys // 2), (rows // 2, rows // 2, keys))

    def share_pairs(self, pairs):
        along = swap_zpair(pairs)
        return [part[None] for part in (pairs, along, swap_core(pairs), swap_core(along))]

    def reduce_pairs(self, grads):
        received = swap_core(grads[2:])
        along = grads[1].astype(F32) + received[1].astype(F32)
        return [grads[0], received[0], swap_zpair(along.astype(BF))]


    def gather(self, wide, down, gains):
        count, rows, width = wide.shape
        mine = lax.dynamic_slice_in_dim(wide, self.core * HALF, HALF, 2)
        other = swap_core(lax.dynamic_slice_in_dim(wide, (1 - self.core) * HALF, HALF, 2))
        joined = jnp.concatenate(
            [jnp.where(self.core == 0, mine, other), jnp.where(self.core == 0, other, mine)], axis=1
        )
        gains = jnp.pad(gains, ((0, 6), (0, HALF - rows)))
        mixed = jnp.concatenate([joined[0], gains], axis=0)
        deep = jnp.concatenate(
            [joined[1], joined[2], jnp.pad(down, ((0, 0), (0, HALF - D)))], axis=0
        )
        index = jnp.stack([self.section, self.z, self.y, self.core])
        packs = []
        for part in (mixed, deep):
            quarter = HALF // 2
            mine, other = (
                lax.dynamic_slice_in_dim(part, x * quarter, quarter, 1)
                for x in (self.section, 1 - self.section)
            )
            packs.append((mine, swap_x(other)))
        layers = []
        for layer in (0, 1):
            weights = []
            for name, (own, theirs) in zip(("mixed", "deep"), packs):
                start = jnp.where(self.section == layer, own, theirs)
                above = lax.ppermute(start, "ctx", ring(4, 1))
                below = lax.ppermute(start, "ctx", ring(4, 3))
                across = lax.ppermute(above, "ctx", ring(4, 1))
                pieces = []
                first = jnp.stack([start, above])
                first_y = swap_y(first)
                square = [first, first_y, swap_x(first), swap_x(first_y)]
                pieces += square + [swap_core(part) for part in square]
                second = jnp.stack([below, across])
                second_x = swap_x(second)
                square = [second, swap_y(second), second_x, swap_y(second_x)]
                pieces += square + [swap_core(part) for part in square]
                weights.append(self.assemble(name == "mixed", index, pieces))
            (mixed, gains), (gate, up, down) = weights
            gains = gains[:, 8:10, :rows].swapaxes(0, 1).reshape(2, 1, D)
            layers.append((mixed, gate, up, down, gains[0], gains[1]))
        return layers

    def assemble(self, mixed, index, pieces):
        if mixed:
            outs = (struct((D, MIXED), BF), struct((16, 16, 128), F32))
        else:
            rows = 16 * (pieces[0].shape[1] - 144)
            outs = (struct((D, MIXED), BF), struct((D, MIXED), BF), struct((rows, D), BF))
        return pl.pallas_call(
            functools.partial(assemble_kernel, mixed),
            out_shape=outs,
            in_specs=[pl.BlockSpec(memory_space=pltpu.SMEM)]
            + [pl.BlockSpec(memory_space=pltpu.VMEM)] * 16,
            compiler_params=pltpu.CompilerParams(vmem_limit_bytes=32 * MIB),
            name="assemble",
        )(index, *pieces)

    def lanes(self, value, x):
        half = value.shape[-1] // 2
        return lax.dynamic_slice_in_dim(value, x * half, half, value.ndim - 1)

    def row(self, value, y):
        return lax.dynamic_index_in_dim(value, y, 1, keepdims=False)

    def reduce_part(self, keep, send):
        held = keep.astype(F32) + swap_core(send).astype(F32)
        held = held.reshape((4, 2) + held.shape[1:])
        x, y = self.section, self.y
        first, second = held[:2], held[2:]
        first_sent = self.lanes(first, 1 - x).astype(BF)
        second_sent = self.row(second, 1 - y).astype(BF)
        first = self.lanes(first, x) + swap_x(first_sent).astype(F32)
        second = self.row(second, y) + swap_y(second_sent).astype(F32)
        first_sent = self.row(first, 1 - y).astype(BF)
        second_sent = self.lanes(second, 1 - x).astype(BF)
        first = self.row(first, y) + swap_y(first_sent).astype(F32)
        second = self.lanes(second, x) + swap_x(second_sent).astype(F32)
        held = jnp.concatenate([first, second])
        low = held.astype(BF)
        total = lax.dynamic_index_in_dim(held, self.z, 0, keepdims=False)
        for steps in (1, 2, 3):
            part = lax.dynamic_index_in_dim(low, (self.z + steps) % 4, 0, keepdims=False)
            total = total + lax.ppermute(part, "ctx", ring(4, steps)).astype(F32)
        return total

    def reduce(self, deep, mixed):
        return self.reduce_part(*mixed), self.reduce_part(*deep)

    def finish(self, first, second, rows):
        joined = []
        for a, b in zip(first, second):
            own = jnp.where(self.section == 0, a, b)
            other = swap_x(jnp.where(self.section == 0, b, a).astype(BF)).astype(F32)
            joined.append(
                jnp.concatenate(
                    [
                        jnp.where(self.section == 0, own, other),
                        jnp.where(self.section == 0, other, own),
                    ],
                    axis=1,
                )
            )
        mixed, deep = joined
        wide = jnp.stack([mixed[: 2 * rows], deep[: 2 * rows], deep[2 * rows : 4 * rows]])
        wide = wide.reshape(3, 2, rows, HALF)
        keep = lax.dynamic_index_in_dim(wide, self.core, 1, keepdims=False)
        sent = lax.dynamic_index_in_dim(wide, 1 - self.core, 1, keepdims=False)
        received = swap_core(sent.astype(BF)).astype(F32)
        left = jnp.where(self.core == 0, keep, received)
        right = jnp.where(self.core == 0, received, keep)
        gains = mixed[2 * rows : 2 * rows + 2, :rows]
        return jnp.concatenate([left, right], axis=2), deep[4 * rows :, :D], gains


class Plain:
    parts = 1
    tile = 16

    def __init__(self):
        self.section = lax.axis_index("section")
        self.ctx = lax.axis_index("ctx")
        self.core = jnp.zeros((), I32)

    def positions_of(self, dz, dc, rows):
        return self.ctx * rows + jnp.arange(rows, dtype=I32)

    def lengths(self, lengths):
        return lax.dynamic_index_in_dim(lengths[0], self.section, 0, keepdims=False)

    def spread(self, block):
        return block

    def unspread(self, block):
        return block

    def key_positions(self, rows):
        return jnp.arange(lax.axis_size("ctx") * rows, dtype=I32)[None]

    def jobs(self, rows, keys):
        return ((0, rows, keys),)

    def share_pairs(self, pairs):
        return [lax.all_gather(pairs, "ctx", axis=0)]

    def reduce_pairs(self, grads):
        return [lax.psum_scatter(grads, "ctx", scatter_dimension=0)]

    def gather(self, wide, down, gains):
        own = (wide, down, gains)
        theirs = tuple(swap_x(part) for part in own)
        layers = []
        for layer in (0, 1):
            w, d, g = (jnp.where(self.section == layer, a, b) for a, b in zip(own, theirs))
            w = lax.all_gather(w, ("ctx", "fsdp"), axis=1, tiled=True)
            d = lax.all_gather(d, ("ctx", "fsdp"), axis=0, tiled=True)
            g = lax.all_gather(g, ("ctx", "fsdp"), axis=1, tiled=True).astype(F32)
            layers.append((w[0], w[1], w[2], d, g[0][None], g[1][None]))
        return layers

    def reduce(self, deep, mixed):
        def columns(pair, first):
            return jnp.concatenate([part[:, first : first + 72] for part in pair], axis=2)

        wide = jnp.stack([columns(mixed, 0), columns(deep, 0), columns(deep, 72)])
        down = jnp.stack([part[:, 144:, :D] for part in deep], axis=1)
        gains = jnp.stack([part[:, 72:74, :36] for part in mixed], axis=1)
        gains = jnp.moveaxis(gains.reshape(16, 2, 36), 1, 0)
        axes = ("ctx", "fsdp")
        return tuple(
            lax.psum_scatter(part, axes, scatter_dimension=axis, tiled=True).astype(F32)
            for part, axis in (
                (wide.reshape(3, D, MIXED), 1),
                (down.reshape(-1, D), 0),
                (gains.reshape(2, D), 1),
            )
        )

    def finish(self, first, second, rows):
        return tuple(
            jnp.where(self.section == 0, a, b) + swap_x(jnp.where(self.section == 0, b, a))
            for a, b in zip(first, second)
        )


def vmem_call(kernel, out_shape, args, scratch=(), scalars=0, limit=56, flops=0, name=None):
    specs = [pl.BlockSpec(memory_space=pltpu.SMEM)] * scalars
    specs += [pl.BlockSpec(memory_space=pltpu.VMEM)] * (len(args) - scalars)
    return pl.pallas_call(
        kernel,
        out_shape=out_shape,
        in_specs=specs,
        scratch_shapes=list(scratch),
        compiler_params=pltpu.CompilerParams(vmem_limit_bytes=limit * MIB),
        cost_estimate=pl.CostEstimate(flops=flops, bytes_accessed=16 * MIB, transcendentals=0),
        name=name,
    )(*args)


def layer_forward(net, source, weights, place):
    mixed, gate, up, down, g_attn, g_mlp = weights
    positions, starts, cosine, sine, key_positions = place
    rows = source.shape[0]
    queries, pairs = vmem_call(
        project_kernel,
        (struct((rows, QW), BF), struct((rows, 2 * KW), BF)),
        (source, mixed, g_attn, cosine, sine),
        flops=2 * rows * D * MIXED,
        name="project",
    )
    pieces = net.share_pairs(pairs)
    keys = key_positions.shape[1]
    attended, log_total, middle = vmem_call(
        functools.partial(
            attend_kernel, net.jobs(rows, keys), net.tile, net.parts, len(pieces)
        ),
        (struct((rows, QW), F32), struct((rows, HQ), F32), struct((rows, D), F32)),
        (source, queries, positions, starts, key_positions, mixed, *pieces),
        [
            pltpu.VMEM((HQ, rows, HD), BF),
            pltpu.VMEM((KV, keys, HD), BF),
            pltpu.VMEM((KV, keys, HD), BF),
            pltpu.VMEM((HQ, rows, HD), F32),
            pltpu.VMEM((HQ, rows, 1), F32),
        ],
        flops=2 * rows * D * QW + 4 * rows * keys * QW,
        name="attend",
    )
    result = vmem_call(
        mlp_kernel,
        struct((rows, D), BF),
        (middle, gate, up, down, g_mlp),
        [pltpu.VMEM((rows, D), BF), pltpu.VMEM((rows, D), F32)],
        flops=6 * rows * D * gate.shape[1],
        name="mlp",
    )
    return result, (source, queries, pieces, attended, log_total, middle)


def layer_backward(net, d_result, kept, weights, place):
    mixed, gate, up, down, g_attn, g_mlp = weights
    source, queries, pieces, attended, log_total, middle = kept
    positions, starts, cosine, sine, key_positions = place
    rows, keys = source.shape[0], key_positions.shape[1]
    core = net.core.reshape(1)
    deep_shape = struct((8, 144 + down.shape[0] // 16, HALF), BF)
    keep, send, gain_grad, d_middle, d_attended = vmem_call(
        mlp_back_kernel,
        (
            deep_shape,
            deep_shape,
            struct((1, D), F32),
            struct((rows, D), F32),
            struct((rows, QW), BF),
        ),
        (core, d_result, middle, mixed, gate, up, down, g_mlp),
        [pltpu.VMEM((rows, D), BF), pltpu.VMEM((rows, D), F32)],
        scalars=1,
        flops=18 * rows * D * gate.shape[1],
        name="mlp_back",
    )
    d_queries, d_pairs = vmem_call(
        functools.partial(
            attend_back_kernel, net.jobs(rows, keys), net.tile, net.parts, len(pieces)
        ),
        (struct((rows, QW), F32), struct((keys // rows, rows, 2 * KW), BF)),
        (d_attended, attended, log_total, queries, positions, starts, key_positions, *pieces),
        [
            pltpu.VMEM((HQ, rows, HD), BF),
            pltpu.VMEM((KV, keys, HD), BF),
            pltpu.VMEM((KV, keys, HD), BF),
            pltpu.VMEM((HQ, rows, HD), BF),
            pltpu.VMEM((HQ, rows, 1), F32),
            pltpu.VMEM((HQ, rows, 1), F32),
            pltpu.VMEM((HQ, rows, HD), F32),
            pltpu.VMEM((KV, HD, keys), F32),
            pltpu.VMEM((KV, HD, keys), F32),
        ],
        flops=10 * rows * keys * QW,
        name="attend_back",
    )
    adds = net.reduce_pairs(d_pairs)
    mixed_shape = struct((8, 80, HALF), BF)
    d_source, mixed_keep, mixed_send = vmem_call(
        functools.partial(input_kernel, len(adds)),
        (struct((rows, D), BF), mixed_shape, mixed_shape),
        (
            core, source, attended, d_middle, d_queries, mixed, g_attn, gain_grad, cosine, sine,
            *adds,
        ),
        scalars=1,
        flops=6 * rows * D * MIXED,
        name="input",
    )
    return d_source, net.reduce((keep, send), (mixed_keep, mixed_send))


def shards(
    inputs, lengths, cotangent, w_query, w_key, w_value, w_out, w_gate, w_up, w_down, g_attn, g_mlp
):
    sizes = tuple(lax.axis_size(axis) for axis in ("section", "ctx", "fsdp"))
    net = Fast() if sizes == (2, 4, 4) else Plain()
    rows = inputs.shape[2]
    wide = jnp.stack(
        [jnp.concatenate([w_query[0], w_key[0], w_out[0], w_value[0]], axis=1), w_gate[0], w_up[0]]
    )
    layers = net.gather(wide, w_down[0], jnp.stack([g_attn[0], g_mlp[0]]))

    source = net.spread(lax.dynamic_index_in_dim(inputs[0], net.section, 0, keepdims=False))
    d_result = net.spread(lax.dynamic_index_in_dim(cotangent[0], net.section, 0, keepdims=False))
    own = net.lengths(lengths)
    positions = net.positions_of(0, 0, rows)
    passed = (positions[:, None] >= jnp.cumsum(own)[None, :]).astype(I32)
    starts = jnp.sum(passed * own[None, :], axis=1)
    cosine, sine = turn_tables(positions - starts)
    place = (positions[:, None], starts[:, None], cosine, sine, net.key_positions(rows))

    first, kept_first = layer_forward(net, source, layers[0], place)
    second, kept_second = layer_forward(net, first, layers[1], place)
    d_first, total_second = layer_backward(net, d_result, kept_second, layers[1], place)
    d_input, total_first = layer_backward(net, d_first, kept_first, layers[0], place)
    wide_grad, down_grad, gain_grads = net.finish(total_first, total_second, w_query.shape[1])
    second = net.unspread(second)
    d_input = net.unspread(d_input)
    kept = jnp.where(net.section == 0, d_input, second)
    crossed = swap_x(jnp.where(net.section == 0, second, d_input))
    edges = jnp.stack(
        [jnp.where(net.section == 0, kept, crossed), jnp.where(net.section == 0, crossed, kept)]
    ).astype(F32)
    mixed = wide_grad[0]
    return (
        edges[None, None],
        mixed[None, :, :QW],
        mixed[None, :, QW:TURNED],
        mixed[None, :, TURNED + QW :],
        mixed[None, :, TURNED : TURNED + QW],
        wide_grad[1][None],
        wide_grad[2][None],
        down_grad[None],
        gain_grads[0][None],
        gain_grads[1][None],
    )


def solution(mesh):
    rows = P("section", ("ctx", "fsdp"), None)
    gains = P("section", ("ctx", "fsdp"))
    blocks = P("fsdp", None, "ctx", None)
    return jax.shard_map(
        shards,
        mesh=mesh,
        in_specs=(blocks, P("fsdp", None, None), blocks) + (rows,) * 7 + (gains,) * 2,
        out_specs=(P("section", "fsdp", None, "ctx", None),) + (rows,) * 7 + (gains,) * 2,
        check_vma=False,
    )
```

```python
import functools

import jax
import jax.numpy as jnp
from jax import lax
from jax.experimental import pallas as pl
from jax.experimental.pallas import tpu as pltpu
from jax.sharding import PartitionSpec as P

D = 576
HQ = 9
KV = 3
HD = 64
GROUP = HQ // KV
QW = HQ * HD
KW = KV * HD
TURNED = QW + KW
MIXED = 2 * QW + 2 * KW
HALF = MIXED // 2

EPSILON = 1e-05
THETA = 10000.0
BF = jnp.bfloat16
F32 = jnp.float32
I32 = jnp.int32
MIB = 1024 * 1024


def mm(left, right):
    return jnp.dot(left, right, preferred_element_type=F32)


def mm_nt(left, right):
    return lax.dot_general(left, right, (((1,), (1,)), ((), ())), preferred_element_type=F32)


def mm_tn(left, right):
    return lax.dot_general(left, right, (((0,), (0,)), ((), ())), preferred_element_type=F32)


def struct(shape, dtype):
    return jax.ShapeDtypeStruct(shape, dtype)


def flip(count, bit):
    return [(i, i ^ bit) for i in range(count)]


def ring(count, steps):
    return [(i, (i + steps) % count) for i in range(count)]


def swap_core(value):
    return lax.ppermute(value, "fsdp", flip(4, 1))


def swap_y(value):
    return lax.ppermute(value, "fsdp", flip(4, 2))


def swap_zpair(value):
    return lax.ppermute(value, "ctx", flip(4, 1))


def swap_x(value):
    return lax.ppermute(value, "section", flip(2, 1))


def swap_corner(value):
    return lax.ppermute(value, ("section", "fsdp"), flip(8, 6))


def tie(value, *others):
    return lax.optimization_barrier((value, others))[0]


def spread_pairs(odd):
    pairs = []
    for z in range(4):
        for f in range(4):
            y, c = f // 2, f % 2
            half = 2 * z + odd
            member = min(half, 7 - half)
            pairs.append((z * 4 + f, (2 * c + member // 2) * 4 + 2 * y + member % 2))
    return pairs


def backwards(pairs):
    return [(target, source) for source, target in pairs]


def turn_tables(offsets):
    middle = HD // 2
    frequency = THETA ** (-jnp.arange(middle, dtype=F32) * 2.0 / HD)
    angles = offsets.astype(F32)[:, None] * frequency[None, :]
    cosine, sine = jnp.cos(angles), jnp.sin(angles)
    return jnp.concatenate([cosine] * 4, axis=1), jnp.concatenate([-sine, sine] * 2, axis=1)


def turn(values, cosine, sine):
    low = lax.broadcasted_iota(I32, (values.shape[0], 128), 1) % HD < HD // 2
    tiles = []
    for first in range(0, values.shape[1], 128):
        tile = values[:, first : first + 128]
        beside = jnp.where(low, pltpu.roll(tile, 128 - HD // 2, 1), pltpu.roll(tile, HD // 2, 1))
        tiles.append(tile * cosine + beside * sine)
    return jnp.concatenate(tiles, axis=1)


def norm(values, gain):
    inverse = lax.rsqrt(jnp.mean(values * values, axis=-1, keepdims=True) + EPSILON)
    scaled = values * inverse
    return inverse, scaled, (scaled * gain).astype(BF)


def norm_back(d_normed, scaled, inverse, gain):
    gain_grad = jnp.sum(d_normed * scaled, axis=0, keepdims=True)
    d_scaled = d_normed * gain
    d_source = inverse * (d_scaled - scaled * jnp.mean(d_scaled * scaled, axis=-1, keepdims=True))
    return d_source, gain_grad


def split_heads(piece_refs, key_scr, value_scr, parts):
    count = sum(ref.shape[0] for ref in piece_refs)
    index = 0
    for ref in piece_refs:
        rows = ref.shape[1] // parts
        for slot in range(ref.shape[0]):
            for part in range(parts):
                block = ref[slot, part * rows : (part + 1) * rows, :]
                at = pl.ds((part * count + index) * rows, rows)
                for group in range(KV):
                    key_scr[group, at, :] = block[:, group * HD : (group + 1) * HD]
                    value_scr[group, at, :] = block[:, KW + group * HD : KW + (group + 1) * HD]
            index += 1


def each_job(jobs, tile, visit):
    if tile is None:
        for first, rows, keys in jobs:
            visit(first, rows, keys)
        return
    _, rows, keys = jobs[0]

    @pl.loop(0, rows // tile)
    def _(step):
        visit(pl.multiple_of(step * tile, tile), tile, keys)


def store(slot, refs, at, value):
    for index, ref in enumerate(refs):

        @pl.when(slot == index)
        def _(ref=ref):
            ref[at] = value


def job_bias(first, rows, keys, position_ref, start_ref, key_position_ref):
    at = key_position_ref[:, :keys]
    allowed = (at <= position_ref[pl.ds(first, rows), :]) & (at >= start_ref[pl.ds(first, rows), :])
    return jnp.where(allowed, 0.0, -1e30)


def project_kernel(source_ref, mixed_ref, gain_ref, cosine_ref, sine_ref, query_ref, pairs_ref):
    _, _, normed = norm(source_ref[...].astype(F32), gain_ref[...])
    both = turn(mm(normed, mixed_ref[:, :TURNED]), cosine_ref[...], sine_ref[...]).astype(BF)
    edge = (2 * QW + KW) // 128 * 128
    values = mm(normed, mixed_ref[:, edge:])[:, 2 * QW + KW - edge :].astype(BF)
    query_ref[...] = both[:, :QW]
    pairs_ref[...] = jnp.concatenate([both[:, QW:], values], axis=1)


def attend_kernel(
    jobs, tile, parts, pieces,
    source_ref, query_ref, position_ref, start_ref, key_position_ref, mixed_ref, *refs,
):
    piece_refs, refs = refs[:pieces], refs[pieces:]
    attended_ref, log_ref, middle_ref = refs[:3]
    query_scr, key_scr, value_scr, out_scr, log_scr = refs[3:]
    split_heads(piece_refs, key_scr, value_scr, parts)
    for head in range(HQ):
        query_scr[head] = query_ref[:, head * HD : (head + 1) * HD] * jnp.asarray(HD**-0.5, BF)

    def visit(first, rows, keys):
        bias = job_bias(first, rows, keys, position_ref, start_ref, key_position_ref)
        at = pl.ds(first, rows)

        @pl.loop(0, KV)
        def _(group):
            key = key_scr[group, :keys, :]
            value = value_scr[group, :keys, :]
            for member in range(GROUP):
                head = group * GROUP + member
                scores = mm_nt(query_scr[head, at, :], key) + bias
                peak = jnp.max(scores, axis=1, keepdims=True)
                weights = jnp.exp(scores - peak)
                total = jnp.sum(weights, axis=1, keepdims=True)
                out_scr[head, at, :] = mm(weights.astype(BF), value) * (1.0 / total)
                log_scr[head, at, :] = peak + jnp.log(total)

    each_job(jobs, tile, visit)
    out = jnp.concatenate([out_scr[head] for head in range(HQ)], axis=1)
    attended_ref[...] = out
    log_ref[...] = jnp.concatenate([log_scr[head] for head in range(HQ)], axis=1)
    added = mm(out.astype(BF), mixed_ref[:, TURNED : TURNED + QW])
    middle_ref[...] = source_ref[...].astype(F32) + added


def mlp_kernel(middle_ref, gate_ref, up_ref, down_ref, gain_ref, result_ref, normed_scr, total_scr):
    middle = middle_ref[...]
    normed_scr[...] = norm(middle, gain_ref[...])[2]
    total_scr[...] = middle
    width = 384

    @pl.loop(0, gate_ref.shape[1] // width)
    def _(step):
        at = pl.ds(pl.multiple_of(step * width, width), width)
        gate = mm(normed_scr[...], gate_ref[:, at])
        up = mm(normed_scr[...], up_ref[:, at])
        hidden = (gate * jax.nn.sigmoid(gate) * up).astype(BF)
        total_scr[...] += mm(hidden, down_ref[at, :])

    result_ref[...] = total_scr[...].astype(BF)


def mlp_back_kernel(
    core_ref, d_result_ref, middle_ref, mixed_ref, gate_ref, up_ref, down_ref, gain_ref, *refs
):
    packed_refs, (gain_grad_ref, d_middle_ref, d_out_ref, normed_scr, total_scr) = refs[:2], refs[2:]
    core = core_ref[0]
    gain = gain_ref[...]
    inverse, scaled, normed = norm(middle_ref[...], gain)
    normed_scr[...] = normed
    total_scr[...] = jnp.zeros_like(total_scr)
    width = 384

    @pl.loop(0, gate_ref.shape[1] // width)
    def _(step):
        at = pl.ds(pl.multiple_of(step * width, width), width)
        low = d_result_ref[...]
        normed = normed_scr[...]
        gate = mm(normed, gate_ref[:, at])
        up = mm(normed, up_ref[:, at])
        d_hidden = mm_nt(low, down_ref[at, :])
        sigmoid = jax.nn.sigmoid(gate)
        silu = gate * sigmoid
        d_gate = (d_hidden * up * sigmoid * (1.0 + gate * (1.0 - sigmoid))).astype(BF)
        d_up = (d_hidden * silu).astype(BF)
        hidden = (silu * up).astype(BF)
        total_scr[...] += mm_nt(d_gate, gate_ref[:, at]) + mm_nt(d_up, up_ref[:, at])
        gate_grad = mm_tn(normed, d_gate)
        up_grad = mm_tn(normed, d_up)
        down_grad = mm_tn(hidden, low)
        slot = (step // 2) ^ core
        columns = pl.ds(pl.multiple_of((step % 2) * width, width), width)
        wide = [
            jnp.concatenate([grad[72 * k : 72 * k + 72] for grad in (gate_grad, up_grad)], axis=0)
            for k in range(8)
        ]
        wide = jnp.stack(wide).astype(BF)
        store(slot, packed_refs, (slice(None), slice(0, 144), columns), wide)
        down_grad = down_grad.reshape(2, 2, 96, D).astype(BF)
        down_grad = jnp.concatenate([down_grad, jnp.zeros((2, 2, 96, HALF - D), BF)], axis=3)
        for side in (0, 1):
            at = (pl.ds(2 * step, 2), slice(144, 240), slice(None))
            store(core ^ side, packed_refs, at, down_grad[:, side])

    d_mlp, gain_grad = norm_back(total_scr[...], scaled, inverse, gain)
    gain_grad_ref[...] = gain_grad
    d_middle = d_result_ref[...].astype(F32) + d_mlp
    d_middle_ref[...] = d_middle
    d_out_ref[...] = mm_nt(d_middle.astype(BF), mixed_ref[:, TURNED : TURNED + QW]).astype(BF)


def attend_back_kernel(
    jobs, tile, parts, pieces,
    d_out_ref, attended_ref, log_ref, query_ref, position_ref, start_ref, key_position_ref, *refs,
):
    piece_refs, refs = refs[:pieces], refs[pieces:]
    d_query_ref, d_pairs_refs = refs[0], refs[1:-9]
    (
        query_scr, key_scr, value_scr, d_out_scr, log_scr, delta_scr, d_query_scr,
        d_key_scr, d_value_scr,
    ) = refs[-9:]
    d_out = d_out_ref[...]
    split_heads(piece_refs, key_scr, value_scr, parts)
    for head in range(HQ):
        at = slice(head * HD, (head + 1) * HD)
        query_scr[head] = query_ref[:, at] * jnp.asarray(HD**-0.5, BF)
        d_out_scr[head] = d_out[:, at]
        log_scr[head] = log_ref[:, head : head + 1]
        delta_scr[head] = jnp.sum(d_out[:, at].astype(F32) * attended_ref[:, at], 1, keepdims=True)
    d_key_scr[...] = jnp.zeros_like(d_key_scr)
    d_value_scr[...] = jnp.zeros_like(d_value_scr)

    def visit(first, rows, keys):
        bias = job_bias(first, rows, keys, position_ref, start_ref, key_position_ref)
        at = pl.ds(first, rows)

        @pl.loop(0, KV)
        def _(group):
            key = key_scr[group, :keys, :]
            value = value_scr[group, :keys, :]
            for member in range(GROUP):
                head = group * GROUP + member
                query = query_scr[head, at, :]
                d_out = d_out_scr[head, at, :]
                chances = jnp.exp(mm_nt(query, key) + bias - log_scr[head, at, :])
                d_chances = mm_nt(d_out, value)
                d_scores = (chances * (d_chances - delta_scr[head, at, :])).astype(BF)
                d_query_scr[head, at, :] = mm(d_scores, key) * HD**-0.5
                d_value_scr[group, :, :keys] += mm_tn(d_out, chances.astype(BF))
                d_key_scr[group, :, :keys] += mm_tn(query, d_scores)

    each_job(jobs, tile, visit)
    d_query_ref[...] = jnp.concatenate([d_query_scr[head] for head in range(HQ)], axis=1)
    near, whole = d_pairs_refs[0].shape[:2]
    count, rows = near * len(d_pairs_refs), whole // parts
    for first in range(0, count * parts, parts):
        at = slice(first * rows, (first + parts) * rows)
        grads = [scr[group, :, at].T for scr in (d_key_scr, d_value_scr) for group in range(KV)]
        grads = jnp.concatenate(grads, axis=1).astype(BF)
        for index in range(parts):
            part, piece = divmod(first + index, count)
            d_pairs_refs[piece // near][piece % near, part * rows : (part + 1) * rows, :] = grads[
                index * rows : (index + 1) * rows
            ]


def input_kernel(
    adds, core_ref, source_ref, attended_ref, d_middle_ref, d_query_ref, mixed_ref, gain_ref,
    mlp_gain_grad_ref, cosine_ref, sine_ref, *refs,
):
    add_refs, d_source_ref, packed_refs = refs[:adds], refs[adds], refs[adds + 1 :]
    core = core_ref[0]
    gain = gain_ref[...]
    inverse, scaled, normed = norm(source_ref[...].astype(F32), gain)
    d_pairs = sum(ref[...].astype(F32) for ref in add_refs)
    d_both = jnp.concatenate([d_query_ref[...], d_pairs[:, :KW]], axis=1)
    d_both = turn(d_both, cosine_ref[...], -sine_ref[...]).astype(BF)
    d_values = d_pairs[:, KW:].astype(BF)
    d_middle = d_middle_ref[...]
    edge = (2 * QW + KW) // 128 * 128
    lead = 2 * QW + KW - edge
    d_tail = jnp.concatenate([jnp.zeros((d_values.shape[0], lead), BF), d_values], axis=1)
    d_normed = mm_nt(d_both, mixed_ref[:, :TURNED]) + mm_nt(d_tail, mixed_ref[:, edge:])
    d_attn, gain_grad = norm_back(d_normed, scaled, inverse, gain)
    d_source_ref[...] = (d_middle + d_attn).astype(BF)
    first = mm_tn(normed, d_both)
    second = jnp.concatenate(
        [
            mm_tn(attended_ref[...].astype(BF), d_middle.astype(BF)),
            mm_tn(normed, d_values),
        ],
        axis=1,
    )
    gains = (gain_grad, mlp_gain_grad_ref[...])
    for half, grad in enumerate((first, second)):
        blocks = []
        for block in range(8):
            at = 36 * (2 * block + half)
            tail = jnp.concatenate([g[:, at : at + 36] for g in gains] + [jnp.zeros((6, 36), F32)])
            tail = jnp.concatenate([tail, jnp.zeros((8, HALF - 36), F32)], axis=1)
            blocks.append(jnp.concatenate([grad[72 * block : 72 * block + 72], tail], axis=0))
        store(half ^ core, packed_refs, Ellipsis, jnp.stack(blocks).astype(BF))


def assemble_kernel(mixed, index_ref, *refs):
    pieces, outs = refs[:8], refs[8:]
    x, z, y, core = (index_ref[i] for i in range(4))

    def ordered(parts):
        rows = [
            [jnp.where(y == 0, a, b), jnp.where(y == 0, b, a)] for a, b in parts
        ]
        return [
            part
            for a, b in zip(*rows)
            for part in (jnp.where(core == 0, a, b), jnp.where(core == 0, b, a))
        ]

    gains = jnp.zeros((8, D), F32)
    owner = lax.broadcasted_iota(I32, (8, D), 1) // 144
    for place, steps in enumerate((0, 1, 3, 2)):
        row = (z + 4 - steps) % 4
        at = pl.ds(pl.multiple_of(row * 144, 144), 144)
        for dx in (0, 1):
            columns = pl.ds(pl.multiple_of((x ^ dx) * HALF, HALF), HALF)
            parts = ordered(
                [
                    [pieces[4 * cross + 2 * dx + dy][place].astype(F32) for dy in (0, 1)]
                    for cross in (0, 1)
                ]
            )
            outs[0][at, columns] = jnp.concatenate([part[:36] for part in parts]).astype(BF)
            if mixed:
                block = jnp.concatenate([part[32:40, :36] for part in parts], axis=1)
                here = (owner == row) & (x == dx)
                gains = jnp.where(here, jnp.concatenate([block] * 4, axis=1), gains)
            else:
                outs[1][at, columns] = jnp.concatenate([part[36:72] for part in parts]).astype(BF)
                for index, part in enumerate(parts):
                    first = (4 * row + index) * 96 + (x ^ dx) * 48
                    rows = pl.ds(pl.multiple_of(first, 16), 48)
                    outs[2][rows, :] = part[72:120, :D].astype(BF)
    if mixed:
        outs[1][...] = gains[4:5]
        outs[2][...] = gains[5:6]


def split_square_kernel(index_ref, keep_ref, received_ref, *out_refs):
    x, y = index_ref[0], index_ref[1]
    half = keep_ref.shape[2] // 2
    for index, ref in enumerate(out_refs):
        dx, dy = divmod(index, 2)
        lanes = pl.ds(pl.multiple_of((x ^ dx) * half, half), half)
        for z in range(4):
            block = 2 * z + (y ^ dy)
            held = keep_ref[block, :, lanes].astype(F32) + received_ref[block, :, lanes].astype(F32)
            ref[z] = held.astype(ref.dtype)


def split_column_kernel(index_ref, *refs):
    parts, out_refs = refs[:4], refs[4:]
    for steps, ref in enumerate(out_refs):
        row = (index_ref[2] + steps) % 4
        ref[...] = sum(part[row].astype(F32) for part in parts).astype(ref.dtype)


class Fast:
    parts = 2
    tile = None
    limit = staticmethod(lambda mib: mib)

    def __init__(self):
        self.section = lax.axis_index("section")
        self.z = lax.axis_index("ctx")
        f = lax.axis_index("fsdp")
        self.y = f // 2
        self.core = f % 2


    def positions_of(self, dz, dc, rows):
        member = 2 * ((self.z % 2) ^ dz) + (self.core ^ dc)
        iota = jnp.arange(rows // 2, dtype=I32)
        return jnp.concatenate([half * (rows // 2) + iota for half in (member, 7 - member)])

    def lengths(self, lengths):
        mine = lax.dynamic_index_in_dim(lengths[0], self.section, 0, keepdims=False)
        other = swap_core(mine)
        return jnp.where(self.z // 2 == self.core, mine, other)

    def spread(self, block):
        half = block.shape[0] // 2
        even, odd = (
            lax.ppermute(block[k * half : (k + 1) * half], ("ctx", "fsdp"), spread_pairs(k))
            for k in (0, 1)
        )
        low = jnp.where(self.core == 0, even, odd)
        return jnp.concatenate([low, jnp.where(self.core == 0, odd, even)], axis=0)

    def unspread(self, block):
        half = block.shape[0] // 2
        low, high = block[:half], block[half:]
        parts = (jnp.where(self.core == 0, low, high), jnp.where(self.core == 0, high, low))
        return jnp.concatenate(
            [
                lax.ppermute(part, ("ctx", "fsdp"), backwards(spread_pairs(k)))
                for k, part in enumerate(parts)
            ],
            axis=0,
        )

    def key_positions(self, rows):
        full = jnp.stack([self.positions_of(dz, dc, rows) for dc in (0, 1) for dz in (0, 1)])
        return full.reshape(4, 2, rows // 2).swapaxes(0, 1).reshape(1, -1)

    def jobs(self, rows, keys):
        return ((0, rows // 2, keys // 2), (rows // 2, rows // 2, keys))

    def share_pairs(self, pairs):
        along = swap_zpair(pairs)
        return [part[None] for part in (pairs, along, swap_core(pairs), swap_core(along))]

    def reduce_pairs(self, grads):
        near, far = grads
        received = swap_core(far)
        along = near[1].astype(F32) + received[1].astype(F32)
        return [near[0], received[0], swap_zpair(along.astype(BF))]


    def pack(self, wide, down, gains):
        rows = wide.shape[1]
        gains = jnp.pad(gains, ((0, 2), (0, MIXED - rows)))
        mixed = jnp.concatenate([wide[0], gains], axis=0)
        half = down.shape[0] // 2
        down = jnp.pad(jnp.stack([down[:half], down[half:]], axis=1), ((0, 0), (0, 0), (0, HALF - D)))
        deep = jnp.concatenate([wide[1], wide[2], down.reshape(half, MIXED)], axis=0)
        return [
            (self.lanes(part, self.section), swap_x(self.lanes(part, 1 - self.section)))
            for part in (mixed, deep)
        ]

    def column(self, pack, layer, *after):
        start = tie(jnp.where(self.section == layer, *pack), *after)
        above = lax.ppermute(start, "ctx", ring(4, 1))
        below = lax.ppermute(start, "ctx", ring(4, 3))
        return start, above, below, lax.ppermute(start, "ctx", ring(4, 2))

    def square(self, column, *after):
        column = jnp.stack(tie(column, *after))
        return column, swap_y(column), swap_x(column), swap_corner(column)

    def assemble(self, square, rows, *after):
        square = tie(square, *after)
        pieces = square + tuple(swap_core(part) for part in square)
        mixed = square[0].shape[1] < 2 * rows
        if mixed:
            outs = (struct((D, MIXED), BF), struct((1, D), F32), struct((1, D), F32))
        else:
            depth = 32 * (square[0].shape[1] - 2 * rows)
            outs = (struct((D, MIXED), BF), struct((D, MIXED), BF), struct((depth, D), BF))
        weights = pl.pallas_call(
            functools.partial(assemble_kernel, mixed),
            out_shape=outs,
            in_specs=[pl.BlockSpec(memory_space=pltpu.SMEM)]
            + [pl.BlockSpec(memory_space=pltpu.VMEM)] * 8,
            compiler_params=pltpu.CompilerParams(vmem_limit_bytes=24 * MIB),
            name="assemble",
        )(jnp.stack([self.section, self.z, self.y, self.core]), *pieces)
        return weights

    def lanes(self, value, x):
        half = value.shape[-1] // 2
        return lax.dynamic_slice_in_dim(value, x * half, half, value.ndim - 1)

    def row(self, value, y):
        return lax.dynamic_index_in_dim(value, y, 1, keepdims=False)

    def reduce_core(self, keep, send):
        return keep, swap_core(send)

    def index(self):
        return jnp.stack([self.section, self.y, self.z])

    def split_square(self, keep, received):
        shape = (4,) + keep.shape[1:2] + (keep.shape[2] // 2,)
        return vmem_call(
            split_square_kernel,
            [struct(shape, F32)] + [struct(shape, BF)] * 3,
            (self.index(), keep, received),
            scalars=1,
            limit=20,
            name="split_square",
        )

    def move_square(self, parts):
        swaps = (swap_y, swap_x, swap_corner)
        return [parts[0]] + [swap(part) for swap, part in zip(swaps, parts[1:])]

    def split_column(self, parts):
        shape = parts[0].shape[1:]
        return vmem_call(
            split_column_kernel,
            [struct(shape, F32)] + [struct(shape, BF)] * 3,
            (self.index(), *parts),
            scalars=1,
            limit=16,
            name="split_column",
        )

    def move_column(self, parts):
        return [parts[0]] + [
            lax.ppermute(part, "ctx", ring(4, steps)) for steps, part in zip((1, 2, 3), parts[1:])
        ]

    def total(self, parts):
        return sum(part.astype(F32) for part in parts)

    def finish(self, first, second, rows):
        joined = []
        for a, b in zip(first, second):
            own = jnp.where(self.section == 0, a, b)
            other = swap_x(jnp.where(self.section == 0, b, a).astype(BF)).astype(F32)
            joined.append(
                jnp.concatenate(
                    [
                        jnp.where(self.section == 0, own, other),
                        jnp.where(self.section == 0, other, own),
                    ],
                    axis=1,
                )
            )
        mixed, deep = joined
        wide = jnp.stack([mixed[: 2 * rows], deep[: 2 * rows], deep[2 * rows : 4 * rows]])
        wide = wide.reshape(3, 2, rows, HALF)
        keep = lax.dynamic_index_in_dim(wide, self.core, 1, keepdims=False)
        sent = lax.dynamic_index_in_dim(wide, 1 - self.core, 1, keepdims=False)
        received = swap_core(sent.astype(BF)).astype(F32)
        left = jnp.where(self.core == 0, keep, received)
        right = jnp.where(self.core == 0, received, keep)
        gains = mixed[2 * rows : 2 * rows + 2, :rows]
        return jnp.concatenate([left, right], axis=2), deep[4 * rows :, :D], gains


class Plain:
    parts = 1
    tile = 16
    limit = staticmethod(lambda mib: 60)

    def __init__(self):
        self.section = lax.axis_index("section")
        self.ctx = lax.axis_index("ctx")
        self.core = jnp.zeros((), I32)

    def positions_of(self, dz, dc, rows):
        return self.ctx * rows + jnp.arange(rows, dtype=I32)

    def lengths(self, lengths):
        return lax.dynamic_index_in_dim(lengths[0], self.section, 0, keepdims=False)

    def spread(self, block):
        return block

    def unspread(self, block):
        return block

    def key_positions(self, rows):
        return jnp.arange(lax.axis_size("ctx") * rows, dtype=I32)[None]

    def jobs(self, rows, keys):
        return ((0, rows, keys),)

    def share_pairs(self, pairs):
        return [lax.all_gather(pairs, "ctx", axis=0)]

    def reduce_pairs(self, grads):
        return [lax.psum_scatter(grads[0], "ctx", scatter_dimension=0)]

    def pack(self, wide, down, gains):
        packs = []
        for own in ((wide[0], gains), (wide[1], wide[2], down)):
            packs.append((own, tuple(swap_x(part) for part in own)))
        return packs

    def column(self, pack, layer, *after):
        return [jnp.where(self.section == layer, a, b) for a, b in zip(*pack)]

    def square(self, column, *after):
        return column

    def assemble(self, square, rows, *after):
        axes = ("ctx", "fsdp")
        weights = [
            lax.all_gather(part, axes, axis=int(part.shape[0] == 2), tiled=True) for part in square
        ]
        if len(weights) == 2:
            gains = weights[1].astype(F32)
            return weights[0], gains[:1], gains[1:]
        return weights

    def reduce_core(self, keep, send):
        return keep, send

    def split_square(self, keep, send):
        return [keep, send]

    def move_square(self, parts):
        return parts

    def split_column(self, parts):
        return parts

    def move_column(self, parts):
        return parts

    def total(self, parts):
        return parts

    def reduce(self, mixed, deep):
        def columns(pair, first):
            return jnp.concatenate([part[:, first : first + 72] for part in pair], axis=2)

        wide = jnp.stack([columns(mixed, 0), columns(deep, 0), columns(deep, 72)])
        down = jnp.stack([part[:, 144:, :D] for part in deep], axis=1)
        gains = jnp.stack([part[:, 72:74, :36] for part in mixed], axis=1)
        gains = jnp.moveaxis(gains.reshape(16, 2, 36), 1, 0)
        axes = ("ctx", "fsdp")
        return tuple(
            lax.psum_scatter(part, axes, scatter_dimension=axis, tiled=True).astype(F32)
            for part, axis in (
                (wide.reshape(3, D, MIXED), 1),
                (down.reshape(-1, D), 0),
                (gains.reshape(2, D), 1),
            )
        )

    def finish(self, first, second, rows):
        first, second = self.reduce(*first), self.reduce(*second)
        return tuple(
            jnp.where(self.section == 0, a, b) + swap_x(jnp.where(self.section == 0, b, a))
            for a, b in zip(first, second)
        )


def vmem_call(kernel, out_shape, args, scratch=(), scalars=0, limit=16, name=None):
    specs = [pl.BlockSpec(memory_space=pltpu.SMEM)] * scalars
    specs += [pl.BlockSpec(memory_space=pltpu.VMEM)] * (len(args) - scalars)
    return pl.pallas_call(
        kernel,
        out_shape=out_shape,
        in_specs=specs,
        scratch_shapes=list(scratch),
        compiler_params=pltpu.CompilerParams(vmem_limit_bytes=limit * MIB),
        name=name,
    )(*args)


def project(net, source, mixed, g_attn, place):
    rows = source.shape[0]
    queries, pairs = vmem_call(
        project_kernel,
        (struct((rows, QW), BF), struct((rows, 2 * KW), BF)),
        (source, mixed, g_attn, place[2], place[3]),
        limit=12,
        name="project",
    )
    return queries, net.share_pairs(pairs)


def attend_forward(net, source, queries, pieces, mixed, place):
    positions, starts, _, _, key_positions = place
    rows, keys = source.shape[0], key_positions.shape[1]
    return vmem_call(
        functools.partial(attend_kernel, net.jobs(rows, keys), net.tile, net.parts, len(pieces)),
        (struct((rows, QW), F32), struct((rows, HQ), F32), struct((rows, D), F32)),
        (source, queries, positions, starts, key_positions, mixed, *pieces),
        [
            pltpu.VMEM((HQ, rows, HD), BF),
            pltpu.VMEM((KV, keys, HD), BF),
            pltpu.VMEM((KV, keys, HD), BF),
            pltpu.VMEM((HQ, rows, HD), F32),
            pltpu.VMEM((HQ, rows, 1), F32),
        ],
        limit=net.limit(28),
        name="attend",
    )


def mlp_forward(middle, gate, up, down, g_mlp):
    rows = middle.shape[0]
    return vmem_call(
        mlp_kernel,
        struct((rows, D), BF),
        (middle, gate, up, down, g_mlp),
        [pltpu.VMEM((rows, D), BF), pltpu.VMEM((rows, D), F32)],
        limit=16,
        name="mlp",
    )


def mlp_backward(net, d_result, middle, mixed, gate, up, down, g_mlp):
    rows = middle.shape[0]
    deep_shape = struct((8, 144 + down.shape[0] // 16, HALF), BF)
    return vmem_call(
        mlp_back_kernel,
        (
            deep_shape,
            deep_shape,
            struct((1, D), F32),
            struct((rows, D), F32),
            struct((rows, QW), BF),
        ),
        (net.core.reshape(1), d_result, middle, mixed, gate, up, down, g_mlp),
        [pltpu.VMEM((rows, D), BF), pltpu.VMEM((rows, D), F32)],
        scalars=1,
        limit=28,
        name="mlp_back",
    )


def attend_backward(net, d_attended, attended, log_total, queries, pieces, place):
    positions, starts, _, _, key_positions = place
    rows, keys = positions.shape[0], key_positions.shape[1]
    return vmem_call(
        functools.partial(
            attend_back_kernel, net.jobs(rows, keys), net.tile, net.parts, len(pieces)
        ),
        [struct((rows, QW), F32)]
        + [struct((keys // rows // net.parts, rows, 2 * KW), BF)] * net.parts,
        (d_attended, attended, log_total, queries, positions, starts, key_positions, *pieces),
        [
            pltpu.VMEM((HQ, rows, HD), BF),
            pltpu.VMEM((KV, keys, HD), BF),
            pltpu.VMEM((KV, keys, HD), BF),
            pltpu.VMEM((HQ, rows, HD), BF),
            pltpu.VMEM((HQ, rows, 1), F32),
            pltpu.VMEM((HQ, rows, 1), F32),
            pltpu.VMEM((HQ, rows, HD), F32),
            pltpu.VMEM((KV, HD, keys), F32),
            pltpu.VMEM((KV, HD, keys), F32),
        ],
        limit=net.limit(32),
        name="attend_back",
    )


def input_backward(
    net, source, attended, d_middle, d_queries, adds, gain_grad, mixed, g_attn, place
):
    rows = source.shape[0]
    mixed_shape = struct((8, 80, HALF), BF)
    return vmem_call(
        functools.partial(input_kernel, len(adds)),
        (struct((rows, D), BF), mixed_shape, mixed_shape),
        (
            net.core.reshape(1), source, attended, d_middle, d_queries, mixed, g_attn, gain_grad,
            place[2], place[3], *adds,
        ),
        scalars=1,
        limit=20,
        name="input",
    )


def shards(
    inputs, lengths, cotangent, w_query, w_key, w_value, w_out, w_gate, w_up, w_down, g_attn, g_mlp
):
    sizes = tuple(lax.axis_size(axis) for axis in ("section", "ctx", "fsdp"))
    net = Fast() if sizes == (2, 4, 4) else Plain()
    rows = inputs.shape[2]
    wide = jnp.stack(
        [jnp.concatenate([w_query[0], w_key[0], w_out[0], w_value[0]], axis=1), w_gate[0], w_up[0]]
    )
    own = net.lengths(lengths)
    positions = net.positions_of(0, 0, rows)
    passed = (positions[:, None] >= jnp.cumsum(own)[None, :]).astype(I32)
    starts = jnp.sum(passed * own[None, :], axis=1)
    cosine, sine = turn_tables(positions - starts)
    place = (positions[:, None], starts[:, None], cosine, sine, net.key_positions(rows))
    shard = w_query.shape[1]

    mixed_pack, deep_pack = net.pack(wide, w_down[0], jnp.stack([g_attn[0], g_mlp[0]]))
    mixed_column = net.column(mixed_pack, 0)
    deep_column = net.column(deep_pack, 0, mixed_column)
    source = lax.dynamic_index_in_dim(inputs[0], net.section, 0, keepdims=False)
    source = net.spread(tie(source, mixed_column))
    d_result = lax.dynamic_index_in_dim(cotangent[0], net.section, 0, keepdims=False)
    mixed_square = net.square(mixed_column)
    deep_square = net.square(deep_column, mixed_square)
    mixed_0, g_attn_0, g_mlp_0 = net.assemble(mixed_square, shard)

    queries_0, pieces_0 = project(net, source, mixed_0, g_attn_0, place)
    mixed_column = net.column(mixed_pack, 1, deep_column, queries_0)
    deep_column = net.column(deep_pack, 1, deep_column, queries_0)
    attended_0, log_0, middle_0 = attend_forward(net, source, queries_0, pieces_0, mixed_0, place)
    mixed_column, deep_column, deep_square = tie((mixed_column, deep_column, deep_square), middle_0)
    mixed_square = net.square(mixed_column, deep_square)
    deep_0 = net.assemble(deep_square, shard, mixed_column, deep_column)
    first = mlp_forward(middle_0, *deep_0, g_mlp_0)
    deep_square = net.square(deep_column, mixed_square, first)
    mixed_1, g_attn_1, g_mlp_1 = net.assemble(mixed_square, shard, first)

    queries_1, pieces_1 = project(net, first, mixed_1, g_attn_1, place)
    d_result = net.spread(tie(d_result, pieces_1))
    attended_1, log_1, middle_1 = attend_forward(net, first, queries_1, pieces_1, mixed_1, place)
    deep_1 = net.assemble(deep_square, shard, middle_1)

    deep_keep, deep_send, gain_grad, d_middle, d_attended = mlp_backward(
        net, d_result, middle_1, mixed_1, *deep_1, g_mlp_1
    )
    deep_sum_1 = net.reduce_core(deep_keep, deep_send)
    d_queries, *d_pairs = attend_backward(
        net, d_attended, attended_1, log_1, queries_1, pieces_1, place
    )
    deep_sum_1 = net.split_square(*tie(deep_sum_1, d_pairs))
    second = mlp_forward(tie(middle_1, deep_sum_1), *deep_1, g_mlp_1)
    adds = tie(net.reduce_pairs(d_pairs), deep_sum_1, second)
    d_first, mixed_keep, mixed_send = input_backward(
        net, first, attended_1, d_middle, d_queries, adds, gain_grad, mixed_1, g_attn_1, place
    )
    deep_sum_1 = net.move_square(deep_sum_1)
    mixed_sum_1 = net.reduce_core(mixed_keep, mixed_send)

    deep_keep, deep_send, gain_grad, d_middle, d_attended = mlp_backward(
        net, d_first, middle_0, mixed_0, *deep_0, g_mlp_0
    )
    deep_sum_0 = net.reduce_core(deep_keep, deep_send)
    mixed_sum_1 = net.split_square(*tie(mixed_sum_1, d_attended))
    deep_sum_1 = net.split_column(tie(deep_sum_1, d_attended))
    d_attended = tie(d_attended, mixed_sum_1, deep_sum_1)
    mixed_sum_1 = net.move_square(mixed_sum_1)
    deep_sum_1 = net.move_column(deep_sum_1)
    d_queries, *d_pairs = attend_backward(
        net, d_attended, attended_0, log_0, queries_0, pieces_0, place
    )
    deep_sum_0 = net.split_square(*tie(deep_sum_0, d_pairs))
    mixed_sum_1 = net.split_column(tie(mixed_sum_1, d_pairs))
    deep_sum_1 = net.total(tie(deep_sum_1, d_pairs))
    second = net.unspread(tie(second, d_pairs))
    adds = tie(net.reduce_pairs(d_pairs), deep_sum_0, mixed_sum_1, deep_sum_1)
    d_input, mixed_keep, mixed_send = input_backward(
        net, source, attended_0, d_middle, d_queries, adds, gain_grad, mixed_0, g_attn_0, place
    )
    deep_sum_0 = net.move_square(deep_sum_0)
    mixed_sum_1 = net.move_column(mixed_sum_1)

    mixed_sum_0 = net.reduce_core(mixed_keep, mixed_send)
    mixed_sum_1 = net.total(tie(mixed_sum_1, d_input))
    deep_sum_0 = tie(deep_sum_0, d_input)
    mixed_sum_0 = net.move_square(tie(net.split_square(*mixed_sum_0), deep_sum_0))
    deep_sum_0 = net.move_column(net.split_column(deep_sum_0))
    deep_sum_0 = net.total(tie(deep_sum_0, mixed_sum_0))
    mixed_sum_0 = net.total(net.move_column(net.split_column(mixed_sum_0)))
    wide_grad, down_grad, gain_grads = net.finish(
        (mixed_sum_0, deep_sum_0), (mixed_sum_1, deep_sum_1), shard
    )
    d_input = net.unspread(d_input)
    kept = jnp.where(net.section == 0, d_input, second)
    crossed = swap_x(jnp.where(net.section == 0, second, d_input))
    edges = jnp.stack(
        [jnp.where(net.section == 0, kept, crossed), jnp.where(net.section == 0, crossed, kept)]
    ).astype(F32)
    mixed = wide_grad[0]
    return (
        edges[None, None],
        mixed[None, :, :QW],
        mixed[None, :, QW:TURNED],
        mixed[None, :, TURNED + QW :],
        mixed[None, :, TURNED : TURNED + QW],
        wide_grad[1][None],
        wide_grad[2][None],
        down_grad[None],
        gain_grads[0][None],
        gain_grads[1][None],
    )


def solution(mesh):
    rows = P("section", ("ctx", "fsdp"), None)
    gains = P("section", ("ctx", "fsdp"))
    blocks = P("fsdp", None, "ctx", None)
    return jax.shard_map(
        shards,
        mesh=mesh,
        in_specs=(blocks, P("fsdp", None, None), blocks) + (rows,) * 7 + (gains,) * 2,
        out_specs=(P("section", "fsdp", None, "ctx", None),) + (rows,) * 7 + (gains,) * 2,
        check_vma=False,
    )
```

```python
import functools

import jax
import jax.numpy as jnp
from jax import lax
from jax.experimental import pallas as pl
from jax.experimental.pallas import tpu as pltpu
from jax.sharding import PartitionSpec as P

D = 576
HQ = 9
KV = 3
HD = 64
GROUP = HQ // KV
QW = HQ * HD
KW = KV * HD
TURNED = QW + KW
MIXED = 2 * QW + 2 * KW
HALF = MIXED // 2

EPSILON = 1e-05
THETA = 10000.0
BF = jnp.bfloat16
F32 = jnp.float32
I32 = jnp.int32
MIB = 1024 * 1024


def mm(left, right):
    return jnp.dot(left, right, preferred_element_type=F32)


def mm_nt(left, right):
    return lax.dot_general(left, right, (((1,), (1,)), ((), ())), preferred_element_type=F32)


def mm_tn(left, right):
    return lax.dot_general(left, right, (((0,), (0,)), ((), ())), preferred_element_type=F32)


def struct(shape, dtype):
    return jax.ShapeDtypeStruct(shape, dtype)


def flip(count, bit):
    return [(i, i ^ bit) for i in range(count)]


def ring(count, steps):
    return [(i, (i + steps) % count) for i in range(count)]


def swap_core(value):
    return lax.ppermute(value, "fsdp", flip(4, 1))


def swap_y(value):
    return lax.ppermute(value, "fsdp", flip(4, 2))


def swap_zpair(value):
    return lax.ppermute(value, "ctx", flip(4, 1))


def swap_x(value):
    return lax.ppermute(value, "section", flip(2, 1))


def swap_corner(value):
    return lax.ppermute(value, ("section", "fsdp"), flip(8, 6))


def tie(value, *others):
    return lax.optimization_barrier((value, others))[0]


def spread_pairs(odd):
    pairs = []
    for z in range(4):
        for f in range(4):
            y, c = f // 2, f % 2
            half = 2 * z + odd
            member = min(half, 7 - half)
            pairs.append((z * 4 + f, (2 * c + member // 2) * 4 + 2 * y + member % 2))
    return pairs


def backwards(pairs):
    return [(target, source) for source, target in pairs]


def turn_tables(offsets):
    middle = HD // 2
    frequency = THETA ** (-jnp.arange(middle, dtype=F32) * 2.0 / HD)
    angles = offsets.astype(F32)[:, None] * frequency[None, :]
    cosine, sine = jnp.cos(angles), jnp.sin(angles)
    return jnp.concatenate([cosine] * 4, axis=1), jnp.concatenate([-sine, sine] * 2, axis=1)


def turn(values, cosine, sine):
    low = lax.broadcasted_iota(I32, (values.shape[0], 128), 1) % HD < HD // 2
    tiles = []
    for first in range(0, values.shape[1], 128):
        tile = values[:, first : first + 128]
        beside = jnp.where(low, pltpu.roll(tile, 128 - HD // 2, 1), pltpu.roll(tile, HD // 2, 1))
        tiles.append(tile * cosine + beside * sine)
    return jnp.concatenate(tiles, axis=1)


def norm(values, gain):
    inverse = lax.rsqrt(jnp.mean(values * values, axis=-1, keepdims=True) + EPSILON)
    scaled = values * inverse
    return inverse, scaled, (scaled * gain).astype(BF)


def norm_back(d_normed, scaled, inverse, gain):
    gain_grad = jnp.sum(d_normed * scaled, axis=0, keepdims=True)
    d_scaled = d_normed * gain
    d_source = inverse * (d_scaled - scaled * jnp.mean(d_scaled * scaled, axis=-1, keepdims=True))
    return d_source, gain_grad


def split_heads(piece_refs, key_scr, value_scr, parts):
    count = sum(ref.shape[0] for ref in piece_refs)
    index = 0
    for ref in piece_refs:
        rows = ref.shape[1] // parts
        for slot in range(ref.shape[0]):
            for part in range(parts):
                block = ref[slot, part * rows : (part + 1) * rows, :]
                at = pl.ds((part * count + index) * rows, rows)
                for group in range(KV):
                    key_scr[group, at, :] = block[:, group * HD : (group + 1) * HD]
                    value_scr[group, at, :] = block[:, KW + group * HD : KW + (group + 1) * HD]
            index += 1


def each_job(jobs, tile, visit):
    if tile is None:
        for first, rows, keys in jobs:
            visit(first, rows, keys)
        return
    _, rows, keys = jobs[0]

    @pl.loop(0, rows // tile)
    def _(step):
        visit(pl.multiple_of(step * tile, tile), tile, keys)


def store(slot, refs, at, value):
    for index, ref in enumerate(refs):

        @pl.when(slot == index)
        def _(ref=ref):
            ref[at] = value


def job_bias(first, rows, keys, position_ref, start_ref, key_position_ref):
    at = key_position_ref[:, :keys]
    allowed = (at <= position_ref[pl.ds(first, rows), :]) & (at >= start_ref[pl.ds(first, rows), :])
    return jnp.where(allowed, 0.0, -1e30)


def project_kernel(source_ref, mixed_ref, gain_ref, cosine_ref, sine_ref, query_ref, pairs_ref):
    _, _, normed = norm(source_ref[...].astype(F32), gain_ref[...])
    both = turn(mm(normed, mixed_ref[:, :TURNED]), cosine_ref[...], sine_ref[...]).astype(BF)
    edge = (2 * QW + KW) // 128 * 128
    values = mm(normed, mixed_ref[:, edge:])[:, 2 * QW + KW - edge :].astype(BF)
    query_ref[...] = both[:, :QW]
    pairs_ref[...] = jnp.concatenate([both[:, QW:], values], axis=1)


def attend_kernel(
    jobs, tile, parts, pieces,
    source_ref, query_ref, position_ref, start_ref, key_position_ref, mixed_ref, *refs,
):
    piece_refs, refs = refs[:pieces], refs[pieces:]
    attended_ref, log_ref, middle_ref = refs[:3]
    query_scr, key_scr, value_scr, out_scr, log_scr = refs[3:]
    split_heads(piece_refs, key_scr, value_scr, parts)
    for head in range(HQ):
        query_scr[head] = query_ref[:, head * HD : (head + 1) * HD] * jnp.asarray(HD**-0.5, BF)

    def visit(first, rows, keys):
        bias = job_bias(first, rows, keys, position_ref, start_ref, key_position_ref)
        at = pl.ds(first, rows)

        @pl.loop(0, KV)
        def _(group):
            key = key_scr[group, :keys, :]
            value = value_scr[group, :keys, :]
            for member in range(GROUP):
                head = group * GROUP + member
                scores = mm_nt(query_scr[head, at, :], key) + bias
                peak = jnp.max(scores, axis=1, keepdims=True)
                weights = jnp.exp(scores - peak)
                total = jnp.sum(weights, axis=1, keepdims=True)
                out_scr[head, at, :] = mm(weights.astype(BF), value) * (1.0 / total)
                log_scr[head, at, :] = peak + jnp.log(total)

    each_job(jobs, tile, visit)
    out = jnp.concatenate([out_scr[head] for head in range(HQ)], axis=1)
    attended_ref[...] = out
    log_ref[...] = jnp.concatenate([log_scr[head] for head in range(HQ)], axis=1)
    added = mm(out.astype(BF), mixed_ref[:, TURNED : TURNED + QW])
    middle_ref[...] = source_ref[...].astype(F32) + added


def mlp_kernel(middle_ref, gate_ref, up_ref, down_ref, gain_ref, result_ref, normed_scr, total_scr):
    middle = middle_ref[...]
    normed_scr[...] = norm(middle, gain_ref[...])[2]
    total_scr[...] = middle
    width = 384

    @pl.loop(0, gate_ref.shape[1] // width)
    def _(step):
        at = pl.ds(pl.multiple_of(step * width, width), width)
        gate = mm(normed_scr[...], gate_ref[:, at])
        up = mm(normed_scr[...], up_ref[:, at])
        hidden = (gate * jax.nn.sigmoid(gate) * up).astype(BF)
        total_scr[...] += mm(hidden, down_ref[at, :])

    result_ref[...] = total_scr[...].astype(BF)


def mlp_back_kernel(
    core_ref, d_result_ref, middle_ref, mixed_ref, gate_ref, up_ref, down_ref, gain_ref, *refs
):
    packed_refs, refs = (refs[:2], refs[2:4]), refs[4:]
    gain_grad_ref, d_middle_ref, d_out_ref, normed_scr, total_scr = refs
    core = core_ref[0]
    gain = gain_ref[...]
    inverse, scaled, normed = norm(middle_ref[...], gain)
    normed_scr[...] = normed
    total_scr[...] = jnp.zeros_like(total_scr)
    width = 384

    for step in range(gate_ref.shape[1] // width):
        at = slice(step * width, (step + 1) * width)
        low = d_result_ref[...]
        normed = normed_scr[...]
        gate = mm(normed, gate_ref[:, at])
        up = mm(normed, up_ref[:, at])
        d_hidden = mm_nt(low, down_ref[at, :])
        sigmoid = jax.nn.sigmoid(gate)
        silu = gate * sigmoid
        d_gate = (d_hidden * up * sigmoid * (1.0 + gate * (1.0 - sigmoid))).astype(BF)
        d_up = (d_hidden * silu).astype(BF)
        hidden = (silu * up).astype(BF)
        total_scr[...] += mm_nt(d_gate, gate_ref[:, at]) + mm_nt(d_up, up_ref[:, at])
        gate_grad = mm_tn(normed, d_gate)
        up_grad = mm_tn(normed, d_up)
        down_grad = mm_tn(hidden, low)
        columns = slice((step % 2) * width, (step % 2 + 1) * width)
        for z in range(4):
            wide = [
                jnp.concatenate([grad[72 * k : 72 * k + 72] for grad in (gate_grad, up_grad)], axis=0)
                for k in (2 * z, 2 * z + 1)
            ]
            refs = [group[z // 2] for group in packed_refs]
            place = (slice(2 * (z % 2), 2 * (z % 2) + 2), slice(0, 144), columns)
            store(core ^ (step // 2), refs, place, jnp.stack(wide).astype(BF))
        down_grad = down_grad.reshape(2, 2, 96, D).astype(BF)
        down_grad = jnp.concatenate([down_grad, jnp.zeros((2, 2, 96, HALF - D), BF)], axis=3)
        for side in (0, 1):
            refs = [group[step // 2] for group in packed_refs]
            place = (slice(2 * (step % 2), 2 * (step % 2) + 2), slice(144, 240), slice(None))
            store(core ^ side, refs, place, down_grad[:, side])

    d_mlp, gain_grad = norm_back(total_scr[...], scaled, inverse, gain)
    gain_grad_ref[...] = gain_grad
    d_middle = d_result_ref[...].astype(F32) + d_mlp
    d_middle_ref[...] = d_middle
    d_out_ref[...] = mm_nt(d_middle.astype(BF), mixed_ref[:, TURNED : TURNED + QW]).astype(BF)


def attend_back_kernel(
    jobs, tile, parts, pieces,
    d_out_ref, attended_ref, log_ref, query_ref, position_ref, start_ref, key_position_ref, *refs,
):
    piece_refs, refs = refs[:pieces], refs[pieces:]
    d_query_ref, d_pairs_refs = refs[0], refs[1:-9]
    (
        query_scr, key_scr, value_scr, d_out_scr, log_scr, delta_scr, d_query_scr,
        d_key_scr, d_value_scr,
    ) = refs[-9:]
    d_out = d_out_ref[...]
    split_heads(piece_refs, key_scr, value_scr, parts)
    for head in range(HQ):
        at = slice(head * HD, (head + 1) * HD)
        query_scr[head] = query_ref[:, at] * jnp.asarray(HD**-0.5, BF)
        d_out_scr[head] = d_out[:, at]
        log_scr[head] = log_ref[:, head : head + 1]
        delta_scr[head] = jnp.sum(d_out[:, at].astype(F32) * attended_ref[:, at], 1, keepdims=True)
    d_key_scr[...] = jnp.zeros_like(d_key_scr)
    d_value_scr[...] = jnp.zeros_like(d_value_scr)

    def visit(first, rows, keys):
        bias = job_bias(first, rows, keys, position_ref, start_ref, key_position_ref)
        at = pl.ds(first, rows)

        @pl.loop(0, KV)
        def _(group):
            key = key_scr[group, :keys, :]
            value = value_scr[group, :keys, :]
            for member in range(GROUP):
                head = group * GROUP + member
                query = query_scr[head, at, :]
                d_out = d_out_scr[head, at, :]
                chances = jnp.exp(mm_nt(query, key) + bias - log_scr[head, at, :])
                d_chances = mm_nt(d_out, value)
                d_scores = (chances * (d_chances - delta_scr[head, at, :])).astype(BF)
                d_query_scr[head, at, :] = mm(d_scores, key) * HD**-0.5
                d_value_scr[group, :, :keys] += mm_tn(d_out, chances.astype(BF))
                d_key_scr[group, :, :keys] += mm_tn(query, d_scores)

    each_job(jobs, tile, visit)
    d_query_ref[...] = jnp.concatenate([d_query_scr[head] for head in range(HQ)], axis=1)
    near, whole = d_pairs_refs[0].shape[:2]
    count, rows = near * len(d_pairs_refs), whole // parts
    for first in range(0, count * parts, parts):
        at = slice(first * rows, (first + parts) * rows)
        grads = [scr[group, :, at].T for scr in (d_key_scr, d_value_scr) for group in range(KV)]
        grads = jnp.concatenate(grads, axis=1).astype(BF)
        for index in range(parts):
            part, piece = divmod(first + index, count)
            d_pairs_refs[piece // near][piece % near, part * rows : (part + 1) * rows, :] = grads[
                index * rows : (index + 1) * rows
            ]


def input_kernel(
    adds, core_ref, source_ref, attended_ref, d_middle_ref, d_query_ref, mixed_ref, gain_ref,
    mlp_gain_grad_ref, cosine_ref, sine_ref, *refs,
):
    add_refs, d_source_ref, packed_refs = refs[:adds], refs[adds], refs[adds + 1 :]
    core = core_ref[0]
    gain = gain_ref[...]
    inverse, scaled, normed = norm(source_ref[...].astype(F32), gain)
    d_pairs = sum(ref[...].astype(F32) for ref in add_refs)
    d_both = jnp.concatenate([d_query_ref[...], d_pairs[:, :KW]], axis=1)
    d_both = turn(d_both, cosine_ref[...], -sine_ref[...]).astype(BF)
    d_values = d_pairs[:, KW:].astype(BF)
    d_middle = d_middle_ref[...]
    edge = (2 * QW + KW) // 128 * 128
    lead = 2 * QW + KW - edge
    d_tail = jnp.concatenate([jnp.zeros((d_values.shape[0], lead), BF), d_values], axis=1)
    d_normed = mm_nt(d_both, mixed_ref[:, :TURNED]) + mm_nt(d_tail, mixed_ref[:, edge:])
    d_attn, gain_grad = norm_back(d_normed, scaled, inverse, gain)
    d_source_ref[...] = (d_middle + d_attn).astype(BF)
    first = mm_tn(normed, d_both)
    second = jnp.concatenate(
        [
            mm_tn(attended_ref[...].astype(BF), d_middle.astype(BF)),
            mm_tn(normed, d_values),
        ],
        axis=1,
    )
    gains = (gain_grad, mlp_gain_grad_ref[...])
    for half, grad in enumerate((first, second)):
        blocks = []
        for block in range(8):
            at = 36 * (2 * block + half)
            tail = jnp.concatenate([g[:, at : at + 36] for g in gains] + [jnp.zeros((6, 36), F32)])
            tail = jnp.concatenate([tail, jnp.zeros((8, HALF - 36), F32)], axis=1)
            blocks.append(jnp.concatenate([grad[72 * block : 72 * block + 72], tail], axis=0))
        store(half ^ core, packed_refs, Ellipsis, jnp.stack(blocks).astype(BF))


def assemble_kernel(mixed, doubled, index_ref, *refs):
    pieces, outs = refs[:-3], refs[-3:]
    x, z, y, core = (index_ref[i] for i in range(4))

    def piece(cross, dx, dy, place):
        if len(pieces) == 2:
            return pieces[cross][2 * dx + dy, place].astype(F32)
        first, second = (dx, dy) if place < 2 else (dy, dx)
        ref = pieces[4 * cross + 2 * (place // 2) + first]
        return ref[2 * second + place % 2].astype(F32)

    def ordered(parts):
        rows = [
            [jnp.where(y == 0, a, b), jnp.where(y == 0, b, a)] for a, b in parts
        ]
        return [
            part
            for a, b in zip(*rows)
            for part in (jnp.where(core == 0, a, b), jnp.where(core == 0, b, a))
        ]

    gains = jnp.zeros((8, D), F32)
    owner = lax.broadcasted_iota(I32, (8, D), 1) // 144
    for place, steps in enumerate((0, 1, 3, 2)):
        row = z ^ place if doubled else (z + 4 - steps) % 4
        at = pl.ds(pl.multiple_of(row * 144, 144), 144)
        for dx in (0, 1):
            columns = pl.ds(pl.multiple_of((x ^ dx) * HALF, HALF), HALF)
            parts = ordered(
                [[piece(cross, dx, dy, place) for dy in (0, 1)] for cross in (0, 1)]
            )
            outs[0][at, columns] = jnp.concatenate([part[:36] for part in parts]).astype(BF)
            if mixed:
                block = jnp.concatenate([part[32:40, :36] for part in parts], axis=1)
                here = (owner == row) & (x == dx)
                gains = jnp.where(here, jnp.concatenate([block] * 4, axis=1), gains)
            else:
                outs[1][at, columns] = jnp.concatenate([part[36:72] for part in parts]).astype(BF)
                for index, part in enumerate(parts):
                    first = (4 * row + index) * 96 + (x ^ dx) * 48
                    rows = pl.ds(pl.multiple_of(first, 16), 48)
                    outs[2][rows, :] = part[72:120, :D].astype(BF)
    if mixed:
        outs[1][...] = gains[4:5]
        outs[2][...] = gains[5:6]


def paired(groups, z, y, lanes):
    sums = []
    for keep_refs, received_refs in groups:
        each = 4 // len(keep_refs)
        at = (2 * (z % each) + y, slice(None), lanes)
        sums.append(keep_refs[z // each][at].astype(F32) + received_refs[z // each][at].astype(F32))
    return jnp.concatenate(sums) if len(sums) > 1 else sums[0]


def read_groups(counts, refs):
    groups = []
    for count in counts:
        groups.append((refs[:count], refs[count : 2 * count]))
        refs = refs[2 * count :]
    return groups, refs


def split_square_kernel(counts, index_ref, *refs):
    x, y = index_ref[0], index_ref[1]
    groups, out_refs = read_groups(counts, refs)
    half = HALF // 2
    for index, ref in enumerate(out_refs):
        dx, dy = divmod(index, 2)
        lanes = pl.ds(pl.multiple_of((x ^ dx) * half, half), half)
        for z in range(4):
            ref[z] = paired(groups, z, y ^ dy, lanes).astype(ref.dtype)


def split_first_kernel(counts, index_ref, *refs):
    x, y = index_ref[0], index_ref[1]
    groups, (own_ref, sent_ref, own_row_ref, sent_row_ref) = read_groups(counts, refs)
    half = HALF // 2
    for dx, ref in enumerate((own_ref, sent_ref)):
        lanes = pl.ds(pl.multiple_of((x ^ dx) * half, half), half)
        for z in (0, 1):
            for row in (0, 1):
                ref[z, row] = paired(groups, z, row, lanes).astype(ref.dtype)
    for dy, ref in enumerate((own_row_ref, sent_row_ref)):
        for z in (0, 1):
            ref[z] = paired(groups, z + 2, y ^ dy, slice(None)).astype(ref.dtype)


def split_second_kernel(index_ref, own_ref, moved_ref, own_row_ref, moved_row_ref, *out_refs):
    x, y = index_ref[0], index_ref[1]
    total_ref, sent_ref, sent_row_ref = out_refs
    half = HALF // 2
    for z in (0, 1):
        for step, ref, at in ((0, total_ref, z), (1, sent_ref, z)):
            part = own_ref[z, y ^ step] + moved_ref[z, y ^ step].astype(F32)
            ref[at] = part.astype(ref.dtype)
        for step, ref, at in ((0, total_ref, z + 2), (1, sent_row_ref, z)):
            lanes = pl.ds(pl.multiple_of((x ^ step) * half, half), half)
            part = own_row_ref[z, :, lanes] + moved_row_ref[z, :, lanes].astype(F32)
            ref[at] = part.astype(ref.dtype)


def split_column_kernel(index_ref, *refs):
    parts, out_refs = refs[:-4], refs[-4:]
    for steps, ref in enumerate(out_refs):
        row = (index_ref[2] + steps) % 4
        total = parts[0][row]
        if len(parts) == 3:
            added = [part[row % 2].astype(F32) for part in parts[1:]]
            total = total + jnp.where(row < 2, *added)
        else:
            total = total + sum(part[row].astype(F32) for part in parts[1:])
        ref[...] = total.astype(ref.dtype)


class Fast:
    parts = 2
    tile = None
    limit = staticmethod(lambda mib: mib)

    def __init__(self):
        self.section = lax.axis_index("section")
        self.z = lax.axis_index("ctx")
        f = lax.axis_index("fsdp")
        self.y = f // 2
        self.core = f % 2


    def positions_of(self, dz, dc, rows):
        member = 2 * ((self.z % 2) ^ dz) + (self.core ^ dc)
        iota = jnp.arange(rows // 2, dtype=I32)
        return jnp.concatenate([half * (rows // 2) + iota for half in (member, 7 - member)])

    def lengths(self, lengths):
        mine = lax.dynamic_index_in_dim(lengths[0], self.section, 0, keepdims=False)
        other = swap_core(mine)
        return jnp.where(self.z // 2 == self.core, mine, other)

    def spread(self, block):
        half = block.shape[0] // 2
        even, odd = (
            lax.ppermute(block[k * half : (k + 1) * half], ("ctx", "fsdp"), spread_pairs(k))
            for k in (0, 1)
        )
        low = jnp.where(self.core == 0, even, odd)
        return jnp.concatenate([low, jnp.where(self.core == 0, odd, even)], axis=0)

    def unspread(self, block):
        half = block.shape[0] // 2
        low, high = block[:half], block[half:]
        parts = (jnp.where(self.core == 0, low, high), jnp.where(self.core == 0, high, low))
        return jnp.concatenate(
            [
                lax.ppermute(part, ("ctx", "fsdp"), backwards(spread_pairs(k)))
                for k, part in enumerate(parts)
            ],
            axis=0,
        )

    def key_positions(self, rows):
        at = lax.broadcasted_iota(I32, (1, 4 * rows), 1)
        half = rows // 2
        piece = at // half % 4
        member = 2 * ((self.z % 2) ^ (piece % 2)) + (self.core ^ (piece // 2))
        return jnp.where(at < 4 * half, member, 7 - member) * half + at % half

    def jobs(self, rows, keys):
        return ((0, rows // 2, keys // 2), (rows // 2, rows // 2, keys))

    def share_pairs(self, pairs):
        along = swap_zpair(pairs)
        return [part[None] for part in (pairs, along, swap_core(pairs), swap_core(along))]

    def reduce_pairs(self, grads):
        near, far = grads
        received = swap_core(far)
        along = near[1].astype(F32) + received[1].astype(F32)
        return [near[0], received[0], swap_zpair(along.astype(BF))]


    def pack(self, wide, down, gains):
        rows = wide.shape[1]
        gains = jnp.pad(gains, ((0, 2), (0, MIXED - rows)))
        mixed = jnp.concatenate([wide[0], gains], axis=0)
        half = down.shape[0] // 2
        down = jnp.pad(jnp.stack([down[:half], down[half:]], axis=1), ((0, 0), (0, 0), (0, HALF - D)))
        deep = jnp.concatenate([wide[1], wide[2], down.reshape(half, MIXED)], axis=0)
        return [
            (self.lanes(part, self.section), swap_x(self.lanes(part, 1 - self.section)))
            for part in (mixed, deep)
        ]

    def start(self, packs, layer, *after):
        start = [jnp.where(self.section == layer, *pack) for pack in packs]
        return tie(jnp.concatenate(start) if len(start) > 1 else start[0], *after)

    def column(self, packs, layer, *after):
        start = self.start(packs, layer, *after)
        return [start] + [lax.ppermute(start, "ctx", ring(4, steps)) for steps in (1, 3, 2)]

    def pair_column(self, packs, layer, *after):
        start = self.start(packs, layer, *after)
        return jnp.stack([start, swap_zpair(start)])

    def double_column(self, pair, *after):
        pair = tie(pair, *after)
        return pair, lax.ppermute(pair, "ctx", flip(4, 2))

    def slices(self, column, rows):
        return [part[rows] for part in column] if len(column) == 4 else [
            part[k, rows] for part in column for k in (0, 1)
        ]

    def square(self, column, *after, rows=slice(None)):
        column = jnp.stack(self.slices(tie(column, *after), rows))
        return column, swap_y(column), swap_x(column), swap_corner(column)

    def gather_square(self, square, *after):
        pieces = jnp.stack(tie(square, *after))
        return [pieces, swap_core(pieces)]

    def first_phase(self, column, *after, rows=slice(None)):
        column = self.slices(tie(column, *after), rows)
        first, second = jnp.stack(column[:2]), jnp.stack(column[2:])
        return first, swap_y(first), second, swap_x(second)

    def second_phase(self, phase, *after):
        phase = tie(phase, *after)
        first, second = jnp.concatenate(phase[:2]), jnp.concatenate(phase[2:])
        return first, swap_x(first), second, swap_y(second)

    def early_core(self, phase):
        return [swap_core(phase[0]), swap_core(phase[2])]

    def gather_phase(self, phase, early, *after):
        phase = tie(phase, *after)
        late = [swap_core(phase[1]), swap_core(phase[3])]
        return [*phase, early[0], late[0], early[1], late[1]]

    def assemble(self, pieces, rows, doubled, *after):
        pieces = tie(pieces, *after)
        mixed = pieces[0].shape[-2] < 2 * rows
        if mixed:
            outs = (struct((D, MIXED), BF), struct((1, D), F32), struct((1, D), F32))
        else:
            depth = 32 * (pieces[0].shape[-2] - 2 * rows)
            outs = (struct((D, MIXED), BF), struct((D, MIXED), BF), struct((depth, D), BF))
        weights = pl.pallas_call(
            functools.partial(assemble_kernel, mixed, doubled),
            out_shape=outs,
            in_specs=[pl.BlockSpec(memory_space=pltpu.SMEM)]
            + [pl.BlockSpec(memory_space=pltpu.VMEM)] * len(pieces),
            compiler_params=pltpu.CompilerParams(vmem_limit_bytes=24 * MIB),
            name="assemble",
        )(jnp.stack([self.section, self.z, self.y, self.core]), *pieces)
        return weights

    def lanes(self, value, x):
        half = value.shape[-1] // 2
        return lax.dynamic_slice_in_dim(value, x * half, half, value.ndim - 1)

    def row(self, value, y):
        return lax.dynamic_index_in_dim(value, y, 1, keepdims=False)

    def reduce_core(self, keep, send):
        return keep, [swap_core(part) for part in send]

    def index(self):
        return jnp.stack([self.section, self.y, self.z])

    def split(self, kernel, shapes, groups, name):
        rows = sum(keep[0].shape[1] for keep, _ in groups)
        args = [part for pair in groups for parts in pair for part in parts]
        return vmem_call(
            functools.partial(kernel, [len(keep) for keep, _ in groups]),
            [struct(shape[:-1] + (rows, shape[-1]), dtype) for shape, dtype in shapes],
            (self.index(), *args),
            scalars=1,
            limit=24,
            name=name,
        )

    def split_square(self, *groups):
        shapes = [((4, HALF // 2), F32)] + [((4, HALF // 2), BF)] * 3
        return self.split(split_square_kernel, shapes, groups, "split_square")

    def move_square(self, parts):
        swaps = (swap_y, swap_x, swap_corner)
        return [parts[0]] + [swap(part) for swap, part in zip(swaps, parts[1:])]

    def split_first(self, *groups):
        shapes = [((2, 2, HALF // 2), F32), ((2, 2, HALF // 2), BF), ((2, HALF), F32), ((2, HALF), BF)]
        return self.split(split_first_kernel, shapes, groups, "split_first")

    def move_first(self, parts):
        return [parts[0], swap_x(parts[1]), parts[2], swap_y(parts[3])]

    def split_second(self, parts):
        rows = parts[0].shape[2]
        return vmem_call(
            split_second_kernel,
            [struct((4, rows, HALF // 2), F32)] + [struct((2, rows, HALF // 2), BF)] * 2,
            (self.index(), *parts),
            scalars=1,
            limit=20,
            name="split_second",
        )

    def move_second(self, parts):
        return [parts[0], swap_y(parts[1]), swap_x(parts[2])]

    def split_column(self, parts):
        shape = parts[0].shape[1:]
        return vmem_call(
            split_column_kernel,
            [struct(shape, F32)] + [struct(shape, BF)] * 3,
            (self.index(), *parts),
            scalars=1,
            limit=20,
            name="split_column",
        )

    def move_column(self, parts):
        return [parts[0]] + [
            lax.ppermute(part, "ctx", ring(4, steps)) for steps, part in zip((1, 2, 3), parts[1:])
        ]

    def total(self, parts, rows=slice(None)):
        return sum(part[rows].astype(F32) for part in parts)

    def finish(self, first, second, rows):
        joined = []
        for a, b in zip(first, second):
            own = jnp.where(self.section == 0, a, b)
            other = swap_x(jnp.where(self.section == 0, b, a).astype(BF)).astype(F32)
            joined.append(
                jnp.concatenate(
                    [
                        jnp.where(self.section == 0, own, other),
                        jnp.where(self.section == 0, other, own),
                    ],
                    axis=1,
                )
            )
        mixed, deep = joined
        wide = jnp.stack([mixed[: 2 * rows], deep[: 2 * rows], deep[2 * rows : 4 * rows]])
        wide = wide.reshape(3, 2, rows, HALF)
        keep = lax.dynamic_index_in_dim(wide, self.core, 1, keepdims=False)
        sent = lax.dynamic_index_in_dim(wide, 1 - self.core, 1, keepdims=False)
        received = swap_core(sent.astype(BF)).astype(F32)
        left = jnp.where(self.core == 0, keep, received)
        right = jnp.where(self.core == 0, received, keep)
        gains = mixed[2 * rows : 2 * rows + 2, :rows]
        return jnp.concatenate([left, right], axis=2), deep[4 * rows :, :D], gains


class Plain:
    parts = 1
    tile = 16
    limit = staticmethod(lambda mib: 60)

    def __init__(self):
        self.section = lax.axis_index("section")
        self.ctx = lax.axis_index("ctx")
        self.core = jnp.zeros((), I32)

    def positions_of(self, dz, dc, rows):
        return self.ctx * rows + jnp.arange(rows, dtype=I32)

    def lengths(self, lengths):
        return lax.dynamic_index_in_dim(lengths[0], self.section, 0, keepdims=False)

    def spread(self, block):
        return block

    def unspread(self, block):
        return block

    def key_positions(self, rows):
        return jnp.arange(lax.axis_size("ctx") * rows, dtype=I32)[None]

    def jobs(self, rows, keys):
        return ((0, rows, keys),)

    def share_pairs(self, pairs):
        return [lax.all_gather(pairs, "ctx", axis=0)]

    def reduce_pairs(self, grads):
        return [lax.psum_scatter(grads[0], "ctx", scatter_dimension=0)]

    def pack(self, wide, down, gains):
        packs = []
        for own in ((wide[0], gains), (wide[1], wide[2], down)):
            packs.append((own, tuple(swap_x(part) for part in own)))
        return packs

    def column(self, packs, layer, *after):
        return [jnp.where(self.section == layer, a, b) for pack in packs for a, b in zip(*pack)]

    def pair_column(self, packs, layer, *after):
        return self.column(packs, layer)

    def double_column(self, pair, *after):
        return pair

    def square(self, column, *after, rows=slice(None)):
        if len(column) == 5:
            return column[:2] if rows.start is None else column[2:]
        return column

    first_phase = square

    def gather_square(self, square, *after):
        return square

    second_phase = gather_square

    def early_core(self, phase):
        return ()

    def gather_phase(self, phase, early, *after):
        return phase

    def assemble(self, square, rows, doubled, *after):
        axes = ("ctx", "fsdp")
        weights = [
            lax.all_gather(part, axes, axis=int(part.shape[0] == 2), tiled=True) for part in square
        ]
        if len(weights) == 2:
            gains = weights[1].astype(F32)
            return weights[0], gains[:1], gains[1:]
        return weights

    def reduce_core(self, keep, send):
        return keep, send

    def split_square(self, *groups):
        return groups

    split_first = split_square

    def move_square(self, groups):
        return groups

    move_first = split_second = move_second = split_column = move_column = move_square

    def total(self, groups, rows=slice(None)):
        return groups[rows.start is not None]

    def reduce(self, mixed, deep):
        mixed, deep = ([jnp.concatenate(part) for part in pair] for pair in (mixed, deep))

        def columns(pair, first):
            return jnp.concatenate([part[:, first : first + 72] for part in pair], axis=2)

        wide = jnp.stack([columns(mixed, 0), columns(deep, 0), columns(deep, 72)])
        down = jnp.stack([part[:, 144:, :D] for part in deep], axis=1)
        gains = jnp.stack([part[:, 72:74, :36] for part in mixed], axis=1)
        gains = jnp.moveaxis(gains.reshape(16, 2, 36), 1, 0)
        axes = ("ctx", "fsdp")
        return tuple(
            lax.psum_scatter(part, axes, scatter_dimension=axis, tiled=True).astype(F32)
            for part, axis in (
                (wide.reshape(3, D, MIXED), 1),
                (down.reshape(-1, D), 0),
                (gains.reshape(2, D), 1),
            )
        )

    def finish(self, first, second, rows):
        first, second = self.reduce(*first), self.reduce(*second)
        return tuple(
            jnp.where(self.section == 0, a, b) + swap_x(jnp.where(self.section == 0, b, a))
            for a, b in zip(first, second)
        )


def vmem_call(kernel, out_shape, args, scratch=(), scalars=0, limit=16, name=None):
    specs = [pl.BlockSpec(memory_space=pltpu.SMEM)] * scalars
    specs += [pl.BlockSpec(memory_space=pltpu.VMEM)] * (len(args) - scalars)
    return pl.pallas_call(
        kernel,
        out_shape=out_shape,
        in_specs=specs,
        scratch_shapes=list(scratch),
        compiler_params=pltpu.CompilerParams(vmem_limit_bytes=limit * MIB),
        name=name,
    )(*args)


def project(net, source, mixed, g_attn, place):
    rows = source.shape[0]
    queries, pairs = vmem_call(
        project_kernel,
        (struct((rows, QW), BF), struct((rows, 2 * KW), BF)),
        (source, mixed, g_attn, place[2], place[3]),
        limit=12,
        name="project",
    )
    return queries, pairs


def attend_forward(net, source, queries, pieces, mixed, place):
    positions, starts, _, _, key_positions = place
    rows, keys = source.shape[0], key_positions.shape[1]
    return vmem_call(
        functools.partial(attend_kernel, net.jobs(rows, keys), net.tile, net.parts, len(pieces)),
        (struct((rows, QW), F32), struct((rows, HQ), F32), struct((rows, D), F32)),
        (source, queries, positions, starts, key_positions, mixed, *pieces),
        [
            pltpu.VMEM((HQ, rows, HD), BF),
            pltpu.VMEM((KV, keys, HD), BF),
            pltpu.VMEM((KV, keys, HD), BF),
            pltpu.VMEM((HQ, rows, HD), F32),
            pltpu.VMEM((HQ, rows, 1), F32),
        ],
        limit=net.limit(28),
        name="attend",
    )


def mlp_forward(middle, gate, up, down, g_mlp):
    rows = middle.shape[0]
    return vmem_call(
        mlp_kernel,
        struct((rows, D), BF),
        (middle, gate, up, down, g_mlp),
        [pltpu.VMEM((rows, D), BF), pltpu.VMEM((rows, D), F32)],
        limit=16,
        name="mlp",
    )


def mlp_backward(net, d_result, middle, mixed, gate, up, down, g_mlp):
    rows = middle.shape[0]
    deep_rows = 144 + down.shape[0] // 16
    shapes = [struct((4, deep_rows, HALF), BF)] * 4
    outs = vmem_call(
        mlp_back_kernel,
        shapes + [struct((1, D), F32), struct((rows, D), F32), struct((rows, QW), BF)],
        (net.core.reshape(1), d_result, middle, mixed, gate, up, down, g_mlp),
        [pltpu.VMEM((rows, D), BF), pltpu.VMEM((rows, D), F32)],
        scalars=1,
        limit=28,
        name="mlp_back",
    )
    return outs[:2], outs[2:4], *outs[4:]


def attend_backward(net, d_attended, attended, log_total, queries, pieces, place):
    positions, starts, _, _, key_positions = place
    rows, keys = positions.shape[0], key_positions.shape[1]
    return vmem_call(
        functools.partial(
            attend_back_kernel, net.jobs(rows, keys), net.tile, net.parts, len(pieces)
        ),
        [struct((rows, QW), F32)]
        + [struct((keys // rows // net.parts, rows, 2 * KW), BF)] * net.parts,
        (d_attended, attended, log_total, queries, positions, starts, key_positions, *pieces),
        [
            pltpu.VMEM((HQ, rows, HD), BF),
            pltpu.VMEM((KV, keys, HD), BF),
            pltpu.VMEM((KV, keys, HD), BF),
            pltpu.VMEM((HQ, rows, HD), BF),
            pltpu.VMEM((HQ, rows, 1), F32),
            pltpu.VMEM((HQ, rows, 1), F32),
            pltpu.VMEM((HQ, rows, HD), F32),
            pltpu.VMEM((KV, HD, keys), F32),
            pltpu.VMEM((KV, HD, keys), F32),
        ],
        limit=net.limit(32),
        name="attend_back",
    )


def input_backward(
    net, source, attended, d_middle, d_queries, adds, gain_grad, mixed, g_attn, place
):
    rows = source.shape[0]
    mixed_shape = struct((8, 80, HALF), BF)
    d_source, keep, send = vmem_call(
        functools.partial(input_kernel, len(adds)),
        (struct((rows, D), BF), mixed_shape, mixed_shape),
        (
            net.core.reshape(1), source, attended, d_middle, d_queries, mixed, g_attn, gain_grad,
            place[2], place[3], *adds,
        ),
        scalars=1,
        limit=20,
        name="input",
    )
    return d_source, [keep], [send]


def shards(
    inputs, lengths, cotangent, w_query, w_key, w_value, w_out, w_gate, w_up, w_down, g_attn, g_mlp
):
    sizes = tuple(lax.axis_size(axis) for axis in ("section", "ctx", "fsdp"))
    net = Fast() if sizes == (2, 4, 4) else Plain()
    rows = inputs.shape[2]
    wide = jnp.stack(
        [jnp.concatenate([w_query[0], w_key[0], w_out[0], w_value[0]], axis=1), w_gate[0], w_up[0]]
    )
    own = net.lengths(lengths)
    positions = net.positions_of(0, 0, rows)
    passed = (positions[:, None] >= jnp.cumsum(own)[None, :]).astype(I32)
    starts = jnp.sum(passed * own[None, :], axis=1)
    cosine, sine = turn_tables(positions - starts)
    place = (positions[:, None], starts[:, None], cosine, sine, net.key_positions(rows))
    shard = w_query.shape[1]

    mixed_pack, deep_pack = net.pack(wide, w_down[0], jnp.stack([g_attn[0], g_mlp[0]]))
    source = lax.dynamic_index_in_dim(inputs[0], net.section, 0, keepdims=False)
    d_result = lax.dynamic_index_in_dim(cotangent[0], net.section, 0, keepdims=False)
    mixed_column = net.column([mixed_pack], 0)
    mixed_square = net.square(mixed_column)
    deep_column = net.column([deep_pack], 0, mixed_column)
    source, d_result, place = tie((source, d_result, place), mixed_column)
    mixed_rows = mixed_square[0].shape[-2]
    mixed_pieces = net.gather_square(mixed_square)
    deep_phase = net.first_phase(deep_column, mixed_square)
    source = net.spread(tie(source, deep_column))
    mixed_0, g_attn_0, g_mlp_0 = net.assemble(mixed_pieces, shard, False)

    queries_0, pairs = project(net, source, mixed_0, g_attn_0, place)
    deep_phase = net.second_phase(deep_phase, source)
    pieces_0 = net.share_pairs(pairs)
    column = net.pair_column([mixed_pack, deep_pack], 1, queries_0)
    early = net.early_core(deep_phase)
    column = net.double_column(column, pieces_0)
    attended_0, log_0, middle_0 = attend_forward(net, source, queries_0, pieces_0, mixed_0, place)
    middle_0, column, deep_phase, early = tie((middle_0, column, deep_phase, early))
    mixed_square = net.square(column, rows=slice(None, mixed_rows))
    deep_0 = net.assemble(net.gather_phase(deep_phase, early), shard, False)
    d_result = net.spread(tie(d_result, deep_0))
    first = mlp_forward(middle_0, *deep_0, g_mlp_0)
    first, mixed_square = tie((first, mixed_square))
    mixed_pieces = net.gather_square(mixed_square)
    deep_phase = net.first_phase(column, mixed_square, rows=slice(mixed_rows, None))
    mixed_1, g_attn_1, g_mlp_1 = net.assemble(mixed_pieces, shard, True)

    queries_1, pairs = project(net, first, mixed_1, g_attn_1, place)
    pairs, d_result = tie((pairs, d_result))
    pieces_1 = net.share_pairs(pairs)
    deep_phase = net.second_phase(deep_phase, queries_1)
    early = net.early_core(deep_phase)
    attended_1, log_1, middle_1 = attend_forward(net, first, queries_1, pieces_1, mixed_1, place)
    middle_1, deep_phase, early = tie((middle_1, deep_phase, early))
    deep_1 = net.assemble(net.gather_phase(deep_phase, early), shard, True)

    deep_keep, deep_send, gain_grad, d_middle, d_attended = mlp_backward(
        net, d_result, middle_1, mixed_1, *deep_1, g_mlp_1
    )
    deep_sum = net.reduce_core(deep_keep, deep_send)
    d_queries, *d_pairs = attend_backward(
        net, d_attended, attended_1, log_1, queries_1, pieces_1, place
    )
    d_queries, d_pairs, deep_sum = tie((d_queries, d_pairs, deep_sum))
    deep_sum = net.split_first(deep_sum)
    d_pairs = tie(d_pairs, deep_sum)
    deep_sum = net.move_first(deep_sum)
    second = mlp_forward(tie(middle_1, d_pairs), *deep_1, g_mlp_1)
    adds, deep_sum = tie((net.reduce_pairs(d_pairs), deep_sum), second)
    deep_sum = net.split_second(deep_sum)
    adds = tie(adds, deep_sum)
    deep_sum = net.move_second(deep_sum)
    d_first, mixed_keep, mixed_send = input_backward(
        net, first, attended_1, d_middle, d_queries, adds, gain_grad, mixed_1, g_attn_1, place
    )
    mixed_sum = net.reduce_core(mixed_keep, mixed_send)
    second = net.unspread(tie(second, d_first))

    outs = mlp_backward(net, d_first, middle_0, mixed_0, *deep_0, g_mlp_0)
    outs, mixed_sum, deep_sum, second = tie((outs, mixed_sum, deep_sum, second))
    deep_keep, deep_send, gain_grad, d_middle, d_attended = outs
    deep_sum = net.split_column(deep_sum)
    d_attended = tie(d_attended, deep_sum)
    deep_sum_1 = net.move_column(deep_sum)
    deep_sum = net.reduce_core(deep_keep, deep_send)
    d_queries, *d_pairs = attend_backward(
        net, d_attended, attended_0, log_0, queries_0, pieces_0, place
    )
    d_queries, d_pairs, deep_sum, deep_sum_1 = tie((d_queries, d_pairs, deep_sum, deep_sum_1))
    sums = net.split_first(mixed_sum, deep_sum)
    d_pairs = tie(d_pairs, sums)
    sums = net.move_first(sums)
    deep_sum_1 = net.total(deep_sum_1)
    adds, sums = tie((net.reduce_pairs(d_pairs), sums), deep_sum_1)
    sums = net.split_second(sums)
    adds = tie(adds, sums)
    sums = net.move_second(sums)
    d_input, mixed_keep, mixed_send = input_backward(
        net, source, attended_0, d_middle, d_queries, adds, gain_grad, mixed_0, g_attn_0, place
    )

    mixed_sum = net.split_square(net.reduce_core(mixed_keep, mixed_send))
    d_input = net.unspread(tie(d_input, mixed_sum))
    mixed_sum, sums = tie((mixed_sum, sums))
    mixed_sum = net.move_square(mixed_sum)
    sums = net.move_column(net.split_column(sums))
    mixed_sum = net.move_column(net.split_column(mixed_sum))
    sums = tie(sums, mixed_sum)
    mixed_sum_1 = net.total(sums, slice(None, 80))
    deep_sum_0 = net.total(sums, slice(80, None))
    mixed_sum_0 = net.total(mixed_sum)
    wide_grad, down_grad, gain_grads = net.finish(
        (mixed_sum_0, deep_sum_0), (mixed_sum_1, deep_sum_1), shard
    )
    kept = jnp.where(net.section == 0, d_input, second)
    crossed = swap_x(jnp.where(net.section == 0, second, d_input))
    edges = jnp.stack(
        [jnp.where(net.section == 0, kept, crossed), jnp.where(net.section == 0, crossed, kept)]
    ).astype(F32)
    mixed = wide_grad[0]
    return (
        edges[None, None],
        mixed[None, :, :QW],
        mixed[None, :, QW:TURNED],
        mixed[None, :, TURNED + QW :],
        mixed[None, :, TURNED : TURNED + QW],
        wide_grad[1][None],
        wide_grad[2][None],
        down_grad[None],
        gain_grads[0][None],
        gain_grads[1][None],
    )


def solution(mesh):
    rows = P("section", ("ctx", "fsdp"), None)
    gains = P("section", ("ctx", "fsdp"))
    blocks = P("fsdp", None, "ctx", None)
    return jax.shard_map(
        shards,
        mesh=mesh,
        in_specs=(blocks, P("fsdp", None, None), blocks) + (rows,) * 7 + (gains,) * 2,
        out_specs=(P("section", "fsdp", None, "ctx", None),) + (rows,) * 7 + (gains,) * 2,
        check_vma=False,
    )
```

```python
import functools

import jax
import jax.numpy as jnp
from jax import lax
from jax.experimental import pallas as pl
from jax.experimental.pallas import tpu as pltpu
from jax.sharding import PartitionSpec as P

D = 576
HQ = 9
KV = 3
HD = 64
GROUP = HQ // KV
QW = HQ * HD
KW = KV * HD
TURNED = QW + KW
MIXED = 2 * QW + 2 * KW
HALF = MIXED // 2

EPSILON = 1e-05
THETA = 10000.0
BF = jnp.bfloat16
F32 = jnp.float32
I32 = jnp.int32
MIB = 1024 * 1024


def mm(left, right):
    return jnp.dot(left, right, preferred_element_type=F32)


def mm_nt(left, right):
    return lax.dot_general(left, right, (((1,), (1,)), ((), ())), preferred_element_type=F32)


def mm_tn(left, right):
    return lax.dot_general(left, right, (((0,), (0,)), ((), ())), preferred_element_type=F32)


def struct(shape, dtype):
    return jax.ShapeDtypeStruct(shape, dtype)


def flip(count, bit):
    return [(i, i ^ bit) for i in range(count)]


def ring(count, steps):
    return [(i, (i + steps) % count) for i in range(count)]


def swap_core(value):
    return lax.ppermute(value, "fsdp", flip(4, 1))


def swap_y(value):
    return lax.ppermute(value, "fsdp", flip(4, 2))


def swap_zpair(value):
    return lax.ppermute(value, "ctx", flip(4, 1))


def swap_x(value):
    return lax.ppermute(value, "section", flip(2, 1))


def swap_corner(value):
    return lax.ppermute(value, ("section", "fsdp"), flip(8, 6))


def tie(value, *others):
    return lax.optimization_barrier((value, others))[0]


def spread_pairs(odd):
    pairs = []
    for z in range(4):
        for f in range(4):
            y, c = f // 2, f % 2
            half = 2 * z + odd
            member = min(half, 7 - half)
            pairs.append((z * 4 + f, (2 * c + member // 2) * 4 + 2 * y + member % 2))
    return pairs


def backwards(pairs):
    return [(target, source) for source, target in pairs]


def turn_tables(offsets):
    middle = HD // 2
    frequency = THETA ** (-jnp.arange(middle, dtype=F32) * 2.0 / HD)
    angles = offsets.astype(F32)[:, None] * frequency[None, :]
    cosine, sine = jnp.cos(angles), jnp.sin(angles)
    return jnp.concatenate([cosine] * 4, axis=1), jnp.concatenate([-sine, sine] * 2, axis=1)


def turn(values, cosine, sine):
    low = lax.broadcasted_iota(I32, (values.shape[0], 128), 1) % HD < HD // 2
    tiles = []
    for first in range(0, values.shape[1], 128):
        tile = values[:, first : first + 128]
        beside = jnp.where(low, pltpu.roll(tile, 128 - HD // 2, 1), pltpu.roll(tile, HD // 2, 1))
        tiles.append(tile * cosine + beside * sine)
    return jnp.concatenate(tiles, axis=1)


def norm(values, gain):
    inverse = lax.rsqrt(jnp.mean(values * values, axis=-1, keepdims=True) + EPSILON)
    scaled = values * inverse
    return inverse, scaled, (scaled * gain).astype(BF)


def norm_back(d_normed, scaled, inverse, gain):
    gain_grad = jnp.sum(d_normed * scaled, axis=0, keepdims=True)
    d_scaled = d_normed * gain
    d_source = inverse * (d_scaled - scaled * jnp.mean(d_scaled * scaled, axis=-1, keepdims=True))
    return d_source, gain_grad


def split_heads(piece_refs, key_scr, value_scr, parts):
    count = sum(ref.shape[0] for ref in piece_refs)
    index = 0
    for ref in piece_refs:
        rows = ref.shape[1] // parts
        for slot in range(ref.shape[0]):
            for part in range(parts):
                block = ref[slot, part * rows : (part + 1) * rows, :]
                at = pl.ds((part * count + index) * rows, rows)
                for group in range(KV):
                    key_scr[group, at, :] = block[:, group * HD : (group + 1) * HD]
                    value_scr[group, at, :] = block[:, KW + group * HD : KW + (group + 1) * HD]
            index += 1


def each_job(jobs, tile, visit):
    if tile is None:
        for first, rows, keys in jobs:
            visit(first, rows, keys)
        return
    _, rows, keys = jobs[0]

    @pl.loop(0, rows // tile)
    def _(step):
        visit(pl.multiple_of(step * tile, tile), tile, keys)


def store(slot, refs, at, value):
    for index, ref in enumerate(refs):

        @pl.when(slot == index)
        def _(ref=ref):
            ref[at] = value


def job_bias(first, rows, keys, position_ref, start_ref, key_position_ref):
    at = key_position_ref[:, :keys]
    allowed = (at <= position_ref[pl.ds(first, rows), :]) & (at >= start_ref[pl.ds(first, rows), :])
    return jnp.where(allowed, 0.0, -1e30)


def project_kernel(source_ref, mixed_ref, gain_ref, cosine_ref, sine_ref, query_ref, pairs_ref):
    _, _, normed = norm(source_ref[...].astype(F32), gain_ref[...])
    both = turn(mm(normed, mixed_ref[:, :TURNED]), cosine_ref[...], sine_ref[...]).astype(BF)
    edge = (2 * QW + KW) // 128 * 128
    values = mm(normed, mixed_ref[:, edge:])[:, 2 * QW + KW - edge :].astype(BF)
    query_ref[...] = both[:, :QW]
    pairs_ref[...] = jnp.concatenate([both[:, QW:], values], axis=1)


def attend_kernel(
    jobs, tile, parts, pieces,
    source_ref, query_ref, position_ref, start_ref, key_position_ref, mixed_ref, *refs,
):
    piece_refs, refs = refs[:pieces], refs[pieces:]
    attended_ref, log_ref, middle_ref = refs[:3]
    query_scr, key_scr, value_scr, out_scr, log_scr = refs[3:]
    split_heads(piece_refs, key_scr, value_scr, parts)
    for head in range(HQ):
        query_scr[head] = query_ref[:, head * HD : (head + 1) * HD] * jnp.asarray(HD**-0.5, BF)

    def visit(first, rows, keys):
        bias = job_bias(first, rows, keys, position_ref, start_ref, key_position_ref)
        at = pl.ds(first, rows)

        @pl.loop(0, KV)
        def _(group):
            key = key_scr[group, :keys, :]
            value = value_scr[group, :keys, :]
            for member in range(GROUP):
                head = group * GROUP + member
                scores = mm_nt(query_scr[head, at, :], key) + bias
                peak = jnp.max(scores, axis=1, keepdims=True)
                weights = jnp.exp(scores - peak)
                total = jnp.sum(weights, axis=1, keepdims=True)
                out_scr[head, at, :] = mm(weights.astype(BF), value) * (1.0 / total)
                log_scr[head, at, :] = peak + jnp.log(total)

    each_job(jobs, tile, visit)
    out = jnp.concatenate([out_scr[head] for head in range(HQ)], axis=1)
    attended_ref[...] = out
    log_ref[...] = jnp.concatenate([log_scr[head] for head in range(HQ)], axis=1)
    added = mm(out.astype(BF), mixed_ref[:, TURNED : TURNED + QW])
    middle_ref[...] = source_ref[...].astype(F32) + added


def mlp_kernel(middle_ref, gate_ref, up_ref, down_ref, gain_ref, result_ref, normed_scr, total_scr):
    middle = middle_ref[...]
    normed_scr[...] = norm(middle, gain_ref[...])[2]
    total_scr[...] = middle
    width = 384

    @pl.loop(0, gate_ref.shape[1] // width)
    def _(step):
        at = pl.ds(pl.multiple_of(step * width, width), width)
        gate = mm(normed_scr[...], gate_ref[:, at])
        up = mm(normed_scr[...], up_ref[:, at])
        hidden = (gate * jax.nn.sigmoid(gate) * up).astype(BF)
        total_scr[...] += mm(hidden, down_ref[at, :])

    result_ref[...] = total_scr[...].astype(BF)


def mlp_back_kernel(
    core_ref, d_result_ref, middle_ref, mixed_ref, gate_ref, up_ref, down_ref, gain_ref, *refs
):
    packed_refs, refs = (refs[:2], refs[2:4]), refs[4:]
    gain_grad_ref, d_middle_ref, d_out_ref, normed_scr, total_scr = refs
    core = core_ref[0]
    gain = gain_ref[...]
    inverse, scaled, normed = norm(middle_ref[...], gain)
    normed_scr[...] = normed
    total_scr[...] = jnp.zeros_like(total_scr)
    width = 384

    for step in range(gate_ref.shape[1] // width):
        at = slice(step * width, (step + 1) * width)
        low = d_result_ref[...]
        normed = normed_scr[...]
        gate = mm(normed, gate_ref[:, at])
        up = mm(normed, up_ref[:, at])
        d_hidden = mm_nt(low, down_ref[at, :])
        sigmoid = jax.nn.sigmoid(gate)
        silu = gate * sigmoid
        d_gate = (d_hidden * up * sigmoid * (1.0 + gate * (1.0 - sigmoid))).astype(BF)
        d_up = (d_hidden * silu).astype(BF)
        hidden = (silu * up).astype(BF)
        total_scr[...] += mm_nt(d_gate, gate_ref[:, at]) + mm_nt(d_up, up_ref[:, at])
        gate_grad = mm_tn(normed, d_gate)
        up_grad = mm_tn(normed, d_up)
        down_grad = mm_tn(hidden, low)
        columns = slice((step % 2) * width, (step % 2 + 1) * width)
        for z in range(4):
            wide = [
                jnp.concatenate([grad[72 * k : 72 * k + 72] for grad in (gate_grad, up_grad)], axis=0)
                for k in (2 * z, 2 * z + 1)
            ]
            refs = [group[z // 2] for group in packed_refs]
            place = (slice(2 * (z % 2), 2 * (z % 2) + 2), slice(0, 144), columns)
            store(core ^ (step // 2), refs, place, jnp.stack(wide).astype(BF))
        down_grad = down_grad.reshape(2, 2, 96, D).astype(BF)
        down_grad = jnp.concatenate([down_grad, jnp.zeros((2, 2, 96, HALF - D), BF)], axis=3)
        for side in (0, 1):
            refs = [group[step // 2] for group in packed_refs]
            place = (slice(2 * (step % 2), 2 * (step % 2) + 2), slice(144, 240), slice(None))
            store(core ^ side, refs, place, down_grad[:, side])

    d_mlp, gain_grad = norm_back(total_scr[...], scaled, inverse, gain)
    gain_grad_ref[...] = gain_grad
    d_middle = d_result_ref[...].astype(F32) + d_mlp
    d_middle_ref[...] = d_middle
    d_out_ref[...] = mm_nt(d_middle.astype(BF), mixed_ref[:, TURNED : TURNED + QW]).astype(BF)


def attend_back_kernel(
    jobs, tile, parts, pieces,
    d_out_ref, attended_ref, log_ref, query_ref, position_ref, start_ref, key_position_ref, *refs,
):
    piece_refs, refs = refs[:pieces], refs[pieces:]
    d_query_ref, d_pairs_refs = refs[0], refs[1:-9]
    (
        query_scr, key_scr, value_scr, d_out_scr, log_scr, delta_scr, d_query_scr,
        d_key_scr, d_value_scr,
    ) = refs[-9:]
    d_out = d_out_ref[...]
    split_heads(piece_refs, key_scr, value_scr, parts)
    for head in range(HQ):
        at = slice(head * HD, (head + 1) * HD)
        query_scr[head] = query_ref[:, at] * jnp.asarray(HD**-0.5, BF)
        d_out_scr[head] = d_out[:, at]
        log_scr[head] = log_ref[:, head : head + 1]
        delta_scr[head] = jnp.sum(d_out[:, at].astype(F32) * attended_ref[:, at], 1, keepdims=True)
    d_key_scr[...] = jnp.zeros_like(d_key_scr)
    d_value_scr[...] = jnp.zeros_like(d_value_scr)

    def visit(first, rows, keys):
        bias = job_bias(first, rows, keys, position_ref, start_ref, key_position_ref)
        at = pl.ds(first, rows)

        @pl.loop(0, KV)
        def _(group):
            key = key_scr[group, :keys, :]
            value = value_scr[group, :keys, :]
            for member in range(GROUP):
                head = group * GROUP + member
                query = query_scr[head, at, :]
                d_out = d_out_scr[head, at, :]
                chances = jnp.exp(mm_nt(query, key) + bias - log_scr[head, at, :])
                d_chances = mm_nt(d_out, value)
                d_scores = (chances * (d_chances - delta_scr[head, at, :])).astype(BF)
                d_query_scr[head, at, :] = mm(d_scores, key) * HD**-0.5
                d_value_scr[group, :, :keys] += mm_tn(d_out, chances.astype(BF))
                d_key_scr[group, :, :keys] += mm_tn(query, d_scores)

    each_job(jobs, tile, visit)
    d_query_ref[...] = jnp.concatenate([d_query_scr[head] for head in range(HQ)], axis=1)
    near, whole = d_pairs_refs[0].shape[:2]
    count, rows = near * len(d_pairs_refs), whole // parts
    for first in range(0, count * parts, parts):
        at = slice(first * rows, (first + parts) * rows)
        grads = [scr[group, :, at].T for scr in (d_key_scr, d_value_scr) for group in range(KV)]
        grads = jnp.concatenate(grads, axis=1).astype(BF)
        for index in range(parts):
            part, piece = divmod(first + index, count)
            d_pairs_refs[piece // near][piece % near, part * rows : (part + 1) * rows, :] = grads[
                index * rows : (index + 1) * rows
            ]


def input_kernel(
    adds, core_ref, source_ref, attended_ref, d_middle_ref, d_query_ref, mixed_ref, gain_ref,
    mlp_gain_grad_ref, cosine_ref, sine_ref, *refs,
):
    add_refs, d_source_ref, packed_refs = refs[:adds], refs[adds], refs[adds + 1 :]
    core = core_ref[0]
    gain = gain_ref[...]
    inverse, scaled, normed = norm(source_ref[...].astype(F32), gain)
    d_pairs = sum(ref[...].astype(F32) for ref in add_refs)
    d_both = jnp.concatenate([d_query_ref[...], d_pairs[:, :KW]], axis=1)
    d_both = turn(d_both, cosine_ref[...], -sine_ref[...]).astype(BF)
    d_values = d_pairs[:, KW:].astype(BF)
    d_middle = d_middle_ref[...]
    edge = (2 * QW + KW) // 128 * 128
    lead = 2 * QW + KW - edge
    d_tail = jnp.concatenate([jnp.zeros((d_values.shape[0], lead), BF), d_values], axis=1)
    d_normed = mm_nt(d_both, mixed_ref[:, :TURNED]) + mm_nt(d_tail, mixed_ref[:, edge:])
    d_attn, gain_grad = norm_back(d_normed, scaled, inverse, gain)
    d_source_ref[...] = (d_middle + d_attn).astype(BF)
    first = mm_tn(normed, d_both)
    second = jnp.concatenate(
        [
            mm_tn(attended_ref[...].astype(BF), d_middle.astype(BF)),
            mm_tn(normed, d_values),
        ],
        axis=1,
    )
    gains = (gain_grad, mlp_gain_grad_ref[...])
    for half, grad in enumerate((first, second)):
        blocks = []
        for block in range(8):
            at = 36 * (2 * block + half)
            tail = jnp.concatenate([g[:, at : at + 36] for g in gains] + [jnp.zeros((6, 36), F32)])
            tail = jnp.concatenate([tail, jnp.zeros((8, HALF - 36), F32)], axis=1)
            blocks.append(jnp.concatenate([grad[72 * block : 72 * block + 72], tail], axis=0))
        store(half ^ core, packed_refs, Ellipsis, jnp.stack(blocks).astype(BF))


def assemble_kernel(mixed, doubled, index_ref, *refs):
    pieces, outs = refs[:-3], refs[-3:]
    x, z, y, core = (index_ref[i] for i in range(4))

    def piece(cross, dx, dy, place):
        if len(pieces) == 2:
            return pieces[cross][2 * dx + dy, place].astype(F32)
        first, second = (dx, dy) if place < 2 else (dy, dx)
        ref = pieces[4 * cross + 2 * (place // 2) + first]
        return ref[2 * second + place % 2].astype(F32)

    def ordered(parts):
        rows = [
            [jnp.where(y == 0, a, b), jnp.where(y == 0, b, a)] for a, b in parts
        ]
        return [
            part
            for a, b in zip(*rows)
            for part in (jnp.where(core == 0, a, b), jnp.where(core == 0, b, a))
        ]

    gains = jnp.zeros((8, D), F32)
    owner = lax.broadcasted_iota(I32, (8, D), 1) // 144
    for place, steps in enumerate((0, 1, 3, 2)):
        row = z ^ place if doubled else (z + 4 - steps) % 4
        at = pl.ds(pl.multiple_of(row * 144, 144), 144)
        for dx in (0, 1):
            columns = pl.ds(pl.multiple_of((x ^ dx) * HALF, HALF), HALF)
            parts = ordered(
                [[piece(cross, dx, dy, place) for dy in (0, 1)] for cross in (0, 1)]
            )
            outs[0][at, columns] = jnp.concatenate([part[:36] for part in parts]).astype(BF)
            if mixed:
                block = jnp.concatenate([part[32:40, :36] for part in parts], axis=1)
                here = (owner == row) & (x == dx)
                gains = jnp.where(here, jnp.concatenate([block] * 4, axis=1), gains)
            else:
                outs[1][at, columns] = jnp.concatenate([part[36:72] for part in parts]).astype(BF)
                for index, part in enumerate(parts):
                    first = (4 * row + index) * 96 + (x ^ dx) * 48
                    rows = pl.ds(pl.multiple_of(first, 16), 48)
                    outs[2][rows, :] = part[72:120, :D].astype(BF)
    if mixed:
        outs[1][...] = gains[4:5]
        outs[2][...] = gains[5:6]


def paired(groups, z, y, lanes):
    sums = []
    for keep_refs, received_refs in groups:
        each = 4 // len(keep_refs)
        at = (2 * (z % each) + y, slice(None), lanes)
        sums.append(keep_refs[z // each][at].astype(F32) + received_refs[z // each][at].astype(F32))
    return jnp.concatenate(sums) if len(sums) > 1 else sums[0]


def read_groups(counts, refs):
    groups = []
    for count in counts:
        groups.append((refs[:count], refs[count : 2 * count]))
        refs = refs[2 * count :]
    return groups, refs


def split_square_kernel(counts, index_ref, *refs):
    x, y = index_ref[0], index_ref[1]
    groups, out_refs = read_groups(counts, refs)
    half = HALF // 2
    for index, ref in enumerate(out_refs):
        dx, dy = divmod(index, 2)
        lanes = pl.ds(pl.multiple_of((x ^ dx) * half, half), half)
        for z in range(4):
            ref[z] = paired(groups, z, y ^ dy, lanes).astype(ref.dtype)


def split_first_kernel(counts, index_ref, *refs):
    x, y = index_ref[0], index_ref[1]
    groups, (own_ref, sent_ref, own_row_ref, sent_row_ref) = read_groups(counts, refs)
    half = HALF // 2
    for dx, ref in enumerate((own_ref, sent_ref)):
        lanes = pl.ds(pl.multiple_of((x ^ dx) * half, half), half)
        for z in (0, 1):
            for row in (0, 1):
                ref[z, row] = paired(groups, z, row, lanes).astype(ref.dtype)
    for dy, ref in enumerate((own_row_ref, sent_row_ref)):
        for z in (0, 1):
            ref[z] = paired(groups, z + 2, y ^ dy, slice(None)).astype(ref.dtype)


def split_second_kernel(index_ref, own_ref, moved_ref, own_row_ref, moved_row_ref, *out_refs):
    x, y = index_ref[0], index_ref[1]
    total_ref, sent_ref, sent_row_ref = out_refs
    half = HALF // 2
    for z in (0, 1):
        for step, ref, at in ((0, total_ref, z), (1, sent_ref, z)):
            part = own_ref[z, y ^ step] + moved_ref[z, y ^ step].astype(F32)
            ref[at] = part.astype(ref.dtype)
        for step, ref, at in ((0, total_ref, z + 2), (1, sent_row_ref, z)):
            lanes = pl.ds(pl.multiple_of((x ^ step) * half, half), half)
            part = own_row_ref[z, :, lanes] + moved_row_ref[z, :, lanes].astype(F32)
            ref[at] = part.astype(ref.dtype)


def split_column_kernel(index_ref, *refs):
    parts, out_refs = refs[:-4], refs[-4:]
    for steps, ref in enumerate(out_refs):
        row = (index_ref[2] + steps) % 4
        total = parts[0][row]
        if len(parts) == 3:
            added = [part[row % 2].astype(F32) for part in parts[1:]]
            total = total + jnp.where(row < 2, *added)
        else:
            total = total + sum(part[row].astype(F32) for part in parts[1:])
        ref[...] = total.astype(ref.dtype)


class Fast:
    parts = 2
    tile = None
    limit = staticmethod(lambda mib: mib)

    def __init__(self):
        self.section = lax.axis_index("section")
        self.z = lax.axis_index("ctx")
        f = lax.axis_index("fsdp")
        self.y = f // 2
        self.core = f % 2


    def positions_of(self, dz, dc, rows):
        member = 2 * ((self.z % 2) ^ dz) + (self.core ^ dc)
        iota = jnp.arange(rows // 2, dtype=I32)
        return jnp.concatenate([half * (rows // 2) + iota for half in (member, 7 - member)])

    def lengths(self, lengths):
        mine = lax.dynamic_index_in_dim(lengths[0], self.section, 0, keepdims=False)
        other = swap_core(mine)
        return jnp.where(self.z // 2 == self.core, mine, other)

    def spread(self, block):
        half = block.shape[0] // 2
        even, odd = (
            lax.ppermute(block[k * half : (k + 1) * half], ("ctx", "fsdp"), spread_pairs(k))
            for k in (0, 1)
        )
        low = jnp.where(self.core == 0, even, odd)
        return jnp.concatenate([low, jnp.where(self.core == 0, odd, even)], axis=0)

    def unspread(self, block):
        half = block.shape[0] // 2
        low, high = block[:half], block[half:]
        parts = (jnp.where(self.core == 0, low, high), jnp.where(self.core == 0, high, low))
        return jnp.concatenate(
            [
                lax.ppermute(part, ("ctx", "fsdp"), backwards(spread_pairs(k)))
                for k, part in enumerate(parts)
            ],
            axis=0,
        )

    def key_positions(self, rows):
        at = lax.broadcasted_iota(I32, (1, 4 * rows), 1)
        half = rows // 2
        piece = at // half % 4
        member = 2 * ((self.z % 2) ^ (piece % 2)) + (self.core ^ (piece // 2))
        return jnp.where(at < 4 * half, member, 7 - member) * half + at % half

    def jobs(self, rows, keys):
        return ((0, rows // 2, keys // 2), (rows // 2, rows // 2, keys))

    def share_pairs(self, pairs):
        along = swap_zpair(pairs)
        return [part[None] for part in (pairs, along, swap_core(pairs), swap_core(along))]

    def reduce_pairs(self, grads):
        near, far = grads
        received = swap_core(far)
        along = near[1].astype(F32) + received[1].astype(F32)
        return [near[0], received[0], swap_zpair(along.astype(BF))]


    def halves(self, part):
        return self.lanes(part, self.section), swap_x(self.lanes(part, 1 - self.section))

    def pack_mixed(self, mixed, gains):
        gains = jnp.pad(gains, ((0, 2), (0, MIXED - mixed.shape[0])))
        return self.halves(jnp.concatenate([mixed, gains], axis=0))

    def pack_deep(self, gate, up, down):
        half = down.shape[0] // 2
        down = jnp.pad(jnp.stack([down[:half], down[half:]], axis=1), ((0, 0), (0, 0), (0, HALF - D)))
        return self.halves(jnp.concatenate([gate, up, down.reshape(half, MIXED)], axis=0))

    def start(self, packs, layer, *after):
        start = [jnp.where(self.section == layer, *pack) for pack in packs]
        return tie(jnp.concatenate(start) if len(start) > 1 else start[0], *after)

    def column(self, packs, layer, *after):
        start = self.start(packs, layer, *after)
        return [start] + [lax.ppermute(start, "ctx", ring(4, steps)) for steps in (1, 3, 2)]

    def pair_column(self, packs, layer, *after):
        start = self.start(packs, layer, *after)
        return jnp.stack([start, swap_zpair(start)])

    def double_column(self, pair, *after):
        pair = tie(pair, *after)
        return pair, lax.ppermute(pair, "ctx", flip(4, 2))

    def slices(self, column, rows):
        return [part[rows] for part in column] if len(column) == 4 else [
            part[k, rows] for part in column for k in (0, 1)
        ]

    def square(self, column, *after, rows=slice(None)):
        column = jnp.stack(self.slices(tie(column, *after), rows))
        return column, swap_y(column), swap_x(column), swap_corner(column)

    def gather_square(self, square, *after):
        pieces = jnp.stack(tie(square, *after))
        return [pieces, swap_core(pieces)]

    def first_phase(self, column, *after, rows=slice(None)):
        column = self.slices(tie(column, *after), rows)
        first, second = jnp.stack(column[:2]), jnp.stack(column[2:])
        return first, swap_y(first), second, swap_x(second)

    def second_phase(self, phase, *after):
        phase = tie(phase, *after)
        first, second = jnp.concatenate(phase[:2]), jnp.concatenate(phase[2:])
        return first, swap_x(first), second, swap_y(second)

    def early_core(self, phase):
        return [swap_core(phase[0]), swap_core(phase[2])]

    def gather_phase(self, phase, early, *after):
        phase = tie(phase, *after)
        late = [swap_core(phase[1]), swap_core(phase[3])]
        return [*phase, early[0], late[0], early[1], late[1]]

    def assemble(self, pieces, rows, doubled, *after):
        pieces = tie(pieces, *after)
        mixed = pieces[0].shape[-2] < 2 * rows
        if mixed:
            outs = (struct((D, MIXED), BF), struct((1, D), F32), struct((1, D), F32))
        else:
            depth = 32 * (pieces[0].shape[-2] - 2 * rows)
            outs = (struct((D, MIXED), BF), struct((D, MIXED), BF), struct((depth, D), BF))
        weights = pl.pallas_call(
            functools.partial(assemble_kernel, mixed, doubled),
            out_shape=outs,
            in_specs=[pl.BlockSpec(memory_space=pltpu.SMEM)]
            + [pl.BlockSpec(memory_space=pltpu.VMEM)] * len(pieces),
            compiler_params=pltpu.CompilerParams(vmem_limit_bytes=20 * MIB),
            name="assemble",
        )(jnp.stack([self.section, self.z, self.y, self.core]), *pieces)
        return weights

    def lanes(self, value, x):
        half = value.shape[-1] // 2
        return lax.dynamic_slice_in_dim(value, x * half, half, value.ndim - 1)

    def row(self, value, y):
        return lax.dynamic_index_in_dim(value, y, 1, keepdims=False)

    def reduce_core(self, keep, send):
        return keep, [swap_core(part) for part in send]

    def index(self):
        return jnp.stack([self.section, self.y, self.z])

    def split(self, kernel, shapes, groups, name):
        rows = sum(keep[0].shape[1] for keep, _ in groups)
        args = [part for pair in groups for parts in pair for part in parts]
        return vmem_call(
            functools.partial(kernel, [len(keep) for keep, _ in groups]),
            [struct(shape[:-1] + (rows, shape[-1]), dtype) for shape, dtype in shapes],
            (self.index(), *args),
            scalars=1,
            limit=20,
            name=name,
        )

    def split_square(self, *groups):
        shapes = [((4, HALF // 2), F32)] + [((4, HALF // 2), BF)] * 3
        return self.split(split_square_kernel, shapes, groups, "split_square")

    def move_square(self, parts):
        swaps = (swap_y, swap_x, swap_corner)
        return [parts[0]] + [swap(part) for swap, part in zip(swaps, parts[1:])]

    def split_first(self, *groups):
        shapes = [((2, 2, HALF // 2), F32), ((2, 2, HALF // 2), BF), ((2, HALF), F32), ((2, HALF), BF)]
        return self.split(split_first_kernel, shapes, groups, "split_first")

    def move_first(self, parts):
        return [parts[0], swap_x(parts[1]), parts[2], swap_y(parts[3])]

    def split_second(self, parts):
        rows = parts[0].shape[2]
        return vmem_call(
            split_second_kernel,
            [struct((4, rows, HALF // 2), F32)] + [struct((2, rows, HALF // 2), BF)] * 2,
            (self.index(), *parts),
            scalars=1,
            limit=20,
            name="split_second",
        )

    def move_second(self, parts):
        return [parts[0], swap_y(parts[1]), swap_x(parts[2])]

    def split_column(self, parts):
        shape = parts[0].shape[1:]
        return vmem_call(
            split_column_kernel,
            [struct(shape, F32)] + [struct(shape, BF)] * 3,
            (self.index(), *parts),
            scalars=1,
            limit=20,
            name="split_column",
        )

    def move_column(self, parts):
        return [parts[0]] + [
            lax.ppermute(part, "ctx", ring(4, steps)) for steps, part in zip((1, 2, 3), parts[1:])
        ]

    def total(self, parts, rows=slice(None)):
        return sum(part[rows].astype(F32) for part in parts)

    def cross(self, first, second):
        own = jnp.where(self.section == 0, first, second)
        other = swap_x(jnp.where(self.section == 0, second, first).astype(BF)).astype(F32)
        left = jnp.where(self.section == 0, own, other)
        return jnp.concatenate([left, jnp.where(self.section == 0, other, own)], axis=1)

    def finish(self, mixed, deep, rows):
        wide = jnp.stack([mixed[: 2 * rows], deep[: 2 * rows], deep[2 * rows : 4 * rows]])
        wide = wide.reshape(3, 2, rows, HALF)
        keep = lax.dynamic_index_in_dim(wide, self.core, 1, keepdims=False)
        sent = lax.dynamic_index_in_dim(wide, 1 - self.core, 1, keepdims=False)
        received = swap_core(sent.astype(BF)).astype(F32)
        left = jnp.where(self.core == 0, keep, received)
        right = jnp.where(self.core == 0, received, keep)
        gains = mixed[2 * rows : 2 * rows + 2, :rows]
        return jnp.concatenate([left, right], axis=2), deep[4 * rows :, :D], gains


class Plain:
    parts = 1
    tile = 16
    limit = staticmethod(lambda mib: 60)

    def __init__(self):
        self.section = lax.axis_index("section")
        self.ctx = lax.axis_index("ctx")
        self.core = jnp.zeros((), I32)

    def positions_of(self, dz, dc, rows):
        return self.ctx * rows + jnp.arange(rows, dtype=I32)

    def lengths(self, lengths):
        return lax.dynamic_index_in_dim(lengths[0], self.section, 0, keepdims=False)

    def spread(self, block):
        return block

    def unspread(self, block):
        return block

    def key_positions(self, rows):
        return jnp.arange(lax.axis_size("ctx") * rows, dtype=I32)[None]

    def jobs(self, rows, keys):
        return ((0, rows, keys),)

    def share_pairs(self, pairs):
        return [lax.all_gather(pairs, "ctx", axis=0)]

    def reduce_pairs(self, grads):
        return [lax.psum_scatter(grads[0], "ctx", scatter_dimension=0)]

    def pack_mixed(self, *own):
        return own, tuple(swap_x(part) for part in own)

    pack_deep = pack_mixed

    def column(self, packs, layer, *after):
        return [jnp.where(self.section == layer, a, b) for pack in packs for a, b in zip(*pack)]

    def pair_column(self, packs, layer, *after):
        return self.column(packs, layer)

    def double_column(self, pair, *after):
        return pair

    def square(self, column, *after, rows=slice(None)):
        if len(column) == 5:
            return column[:2] if rows.start is None else column[2:]
        return column

    first_phase = square

    def gather_square(self, square, *after):
        return square

    second_phase = gather_square

    def early_core(self, phase):
        return ()

    def gather_phase(self, phase, early, *after):
        return phase

    def assemble(self, square, rows, doubled, *after):
        axes = ("ctx", "fsdp")
        weights = [
            lax.all_gather(part, axes, axis=int(part.shape[0] == 2), tiled=True) for part in square
        ]
        if len(weights) == 2:
            gains = weights[1].astype(F32)
            return weights[0], gains[:1], gains[1:]
        return weights

    def reduce_core(self, keep, send):
        return keep, send

    def split_square(self, *groups):
        return groups

    split_first = split_square

    def move_square(self, groups):
        return groups

    move_first = split_second = move_second = split_column = move_column = move_square

    def total(self, groups, rows=slice(None)):
        return groups[rows.start is not None]

    def reduce(self, mixed, deep):
        mixed, deep = ([jnp.concatenate(part) for part in pair] for pair in (mixed, deep))

        def columns(pair, first):
            return jnp.concatenate([part[:, first : first + 72] for part in pair], axis=2)

        wide = jnp.stack([columns(mixed, 0), columns(deep, 0), columns(deep, 72)])
        down = jnp.stack([part[:, 144:, :D] for part in deep], axis=1)
        gains = jnp.stack([part[:, 72:74, :36] for part in mixed], axis=1)
        gains = jnp.moveaxis(gains.reshape(16, 2, 36), 1, 0)
        axes = ("ctx", "fsdp")
        return tuple(
            lax.psum_scatter(part, axes, scatter_dimension=axis, tiled=True).astype(F32)
            for part, axis in (
                (wide.reshape(3, D, MIXED), 1),
                (down.reshape(-1, D), 0),
                (gains.reshape(2, D), 1),
            )
        )

    def cross(self, first, second):
        return first, second

    def finish(self, mixed, deep, rows):
        first, second = (self.reduce(*pair) for pair in zip(mixed, deep))
        return tuple(
            jnp.where(self.section == 0, a, b) + swap_x(jnp.where(self.section == 0, b, a))
            for a, b in zip(first, second)
        )


def vmem_call(kernel, out_shape, args, scratch=(), scalars=0, limit=16, name=None):
    specs = [pl.BlockSpec(memory_space=pltpu.SMEM)] * scalars
    specs += [pl.BlockSpec(memory_space=pltpu.VMEM)] * (len(args) - scalars)
    return pl.pallas_call(
        kernel,
        out_shape=out_shape,
        in_specs=specs,
        scratch_shapes=list(scratch),
        compiler_params=pltpu.CompilerParams(vmem_limit_bytes=limit * MIB),
        name=name,
    )(*args)


def project(net, source, mixed, g_attn, place):
    rows = source.shape[0]
    queries, pairs = vmem_call(
        project_kernel,
        (struct((rows, QW), BF), struct((rows, 2 * KW), BF)),
        (source, mixed, g_attn, place[2], place[3]),
        limit=8,
        name="project",
    )
    return queries, pairs


def attend_forward(net, source, queries, pieces, mixed, place):
    positions, starts, _, _, key_positions = place
    rows, keys = source.shape[0], key_positions.shape[1]
    return vmem_call(
        functools.partial(attend_kernel, net.jobs(rows, keys), net.tile, net.parts, len(pieces)),
        (struct((rows, QW), F32), struct((rows, HQ), F32), struct((rows, D), F32)),
        (source, queries, positions, starts, key_positions, mixed, *pieces),
        [
            pltpu.VMEM((HQ, rows, HD), BF),
            pltpu.VMEM((KV, keys, HD), BF),
            pltpu.VMEM((KV, keys, HD), BF),
            pltpu.VMEM((HQ, rows, HD), F32),
            pltpu.VMEM((HQ, rows, 1), F32),
        ],
        limit=net.limit(16),
        name="attend",
    )


def mlp_forward(middle, gate, up, down, g_mlp):
    rows = middle.shape[0]
    return vmem_call(
        mlp_kernel,
        struct((rows, D), BF),
        (middle, gate, up, down, g_mlp),
        [pltpu.VMEM((rows, D), BF), pltpu.VMEM((rows, D), F32)],
        limit=12,
        name="mlp",
    )


def mlp_backward(net, d_result, middle, mixed, gate, up, down, g_mlp):
    rows = middle.shape[0]
    deep_rows = 144 + down.shape[0] // 16
    shapes = [struct((4, deep_rows, HALF), BF)] * 4
    outs = vmem_call(
        mlp_back_kernel,
        shapes + [struct((1, D), F32), struct((rows, D), F32), struct((rows, QW), BF)],
        (net.core.reshape(1), d_result, middle, mixed, gate, up, down, g_mlp),
        [pltpu.VMEM((rows, D), BF), pltpu.VMEM((rows, D), F32)],
        scalars=1,
        limit=22,
        name="mlp_back",
    )
    return outs[:2], outs[2:4], *outs[4:]


def attend_backward(net, d_attended, attended, log_total, queries, pieces, place):
    positions, starts, _, _, key_positions = place
    rows, keys = positions.shape[0], key_positions.shape[1]
    return vmem_call(
        functools.partial(
            attend_back_kernel, net.jobs(rows, keys), net.tile, net.parts, len(pieces)
        ),
        [struct((rows, QW), F32)]
        + [struct((keys // rows // net.parts, rows, 2 * KW), BF)] * net.parts,
        (d_attended, attended, log_total, queries, positions, starts, key_positions, *pieces),
        [
            pltpu.VMEM((HQ, rows, HD), BF),
            pltpu.VMEM((KV, keys, HD), BF),
            pltpu.VMEM((KV, keys, HD), BF),
            pltpu.VMEM((HQ, rows, HD), BF),
            pltpu.VMEM((HQ, rows, 1), F32),
            pltpu.VMEM((HQ, rows, 1), F32),
            pltpu.VMEM((HQ, rows, HD), F32),
            pltpu.VMEM((KV, HD, keys), F32),
            pltpu.VMEM((KV, HD, keys), F32),
        ],
        limit=net.limit(22),
        name="attend_back",
    )


def input_backward(
    net, source, attended, d_middle, d_queries, adds, gain_grad, mixed, g_attn, place
):
    rows = source.shape[0]
    mixed_shape = struct((8, 80, HALF), BF)
    d_source, keep, send = vmem_call(
        functools.partial(input_kernel, len(adds)),
        (struct((rows, D), BF), mixed_shape, mixed_shape),
        (
            net.core.reshape(1), source, attended, d_middle, d_queries, mixed, g_attn, gain_grad,
            place[2], place[3], *adds,
        ),
        scalars=1,
        limit=12,
        name="input",
    )
    return d_source, [keep], [send]


def shards(
    inputs, lengths, cotangent, w_query, w_key, w_value, w_out, w_gate, w_up, w_down, g_attn, g_mlp
):
    sizes = tuple(lax.axis_size(axis) for axis in ("section", "ctx", "fsdp"))
    net = Fast() if sizes == (2, 4, 4) else Plain()
    rows = inputs.shape[2]
    mixed = jnp.concatenate([w_query[0], w_key[0], w_out[0], w_value[0]], axis=1)
    mixed_pack = net.pack_mixed(mixed, jnp.stack([g_attn[0], g_mlp[0]]))
    shard = w_query.shape[1]
    lengths, gate, up, down, inputs, cotangent = tie(
        (lengths, w_gate[0], w_up[0], w_down[0], inputs, cotangent), mixed_pack[0]
    )
    deep_pack = net.pack_deep(gate, up, down)
    mixed_column = net.column([mixed_pack], 0)
    own = net.lengths(lengths)
    positions = net.positions_of(0, 0, rows)
    passed = (positions[:, None] >= jnp.cumsum(own)[None, :]).astype(I32)
    starts = jnp.sum(passed * own[None, :], axis=1)
    cosine, sine = turn_tables(positions - starts)
    place = (positions[:, None], starts[:, None], cosine, sine, net.key_positions(rows))
    source = lax.dynamic_index_in_dim(inputs[0], net.section, 0, keepdims=False)
    d_result = lax.dynamic_index_in_dim(cotangent[0], net.section, 0, keepdims=False)
    mixed_square = net.square(mixed_column)
    deep_column = net.column([deep_pack], 0, mixed_column)
    source, d_result, place = tie((source, d_result, place), mixed_column)
    mixed_rows = mixed_square[0].shape[-2]
    mixed_pieces = net.gather_square(mixed_square)
    deep_phase = net.first_phase(deep_column, mixed_square)
    source = net.spread(tie(source, deep_column))
    mixed_0, g_attn_0, g_mlp_0 = net.assemble(mixed_pieces, shard, False)

    queries_0, pairs = project(net, source, mixed_0, g_attn_0, place)
    deep_phase = net.second_phase(deep_phase, source)
    pieces_0 = net.share_pairs(pairs)
    column = net.pair_column([mixed_pack, deep_pack], 1, queries_0)
    early = net.early_core(deep_phase)
    column = net.double_column(column, pieces_0)
    attended_0, log_0, middle_0 = attend_forward(net, source, queries_0, pieces_0, mixed_0, place)
    middle_0, column, deep_phase, early = tie((middle_0, column, deep_phase, early))
    mixed_square = net.square(column, rows=slice(None, mixed_rows))
    deep_0 = net.assemble(net.gather_phase(deep_phase, early), shard, False)
    first = mlp_forward(middle_0, *deep_0, g_mlp_0)
    first, mixed_square = tie((first, mixed_square))
    mixed_pieces = net.gather_square(mixed_square)
    deep_phase = net.first_phase(column, mixed_square, rows=slice(mixed_rows, None))
    mixed_1, g_attn_1, g_mlp_1 = net.assemble(mixed_pieces, shard, True)

    queries_1, pairs = project(net, first, mixed_1, g_attn_1, place)
    pieces_1 = net.share_pairs(pairs)
    deep_phase = net.second_phase(deep_phase, queries_1)
    d_result = net.spread(tie(d_result, pieces_1))
    attended_1, log_1, middle_1 = attend_forward(net, first, queries_1, pieces_1, mixed_1, place)
    middle_1, deep_phase, d_result = tie((middle_1, deep_phase, d_result))
    deep_1 = net.assemble(
        net.gather_phase(deep_phase, net.early_core(deep_phase)), shard, True
    )

    deep_keep, deep_send, gain_grad, d_middle, d_attended = mlp_backward(
        net, d_result, middle_1, mixed_1, *deep_1, g_mlp_1
    )
    deep_sum = net.reduce_core(deep_keep, deep_send)
    d_queries, *d_pairs = attend_backward(
        net, d_attended, attended_1, log_1, queries_1, pieces_1, place
    )
    d_queries, d_pairs, deep_sum = tie((d_queries, d_pairs, deep_sum))
    deep_sum = net.split_first(deep_sum)
    d_pairs = tie(d_pairs, deep_sum)
    deep_sum = net.move_first(deep_sum)
    second = mlp_forward(tie(middle_1, d_pairs), *deep_1, g_mlp_1)
    adds = tie(net.reduce_pairs(d_pairs), second)
    outs = input_backward(
        net, first, attended_1, d_middle, d_queries, adds, gain_grad, mixed_1, g_attn_1, place
    )
    (d_first, mixed_keep, mixed_send), deep_sum = tie((outs, deep_sum))
    deep_sum = net.split_second(deep_sum)
    d_first = tie(d_first, deep_sum)
    deep_sum = net.move_second(deep_sum)
    mixed_sum = net.reduce_core(mixed_keep, mixed_send)
    second = net.unspread(tie(second, d_first))

    outs = mlp_backward(net, d_first, middle_0, mixed_0, *deep_0, g_mlp_0)
    outs, mixed_sum, deep_sum, second = tie((outs, mixed_sum, deep_sum, second))
    deep_keep, deep_send, gain_grad, d_middle, d_attended = outs
    deep_sum = net.split_column(deep_sum)
    d_attended = tie(d_attended, deep_sum)
    deep_sum_1 = net.move_column(deep_sum)
    sums = net.split_first(mixed_sum, net.reduce_core(deep_keep, deep_send))
    d_attended = tie(d_attended, sums)
    sums = net.move_first(sums)
    d_queries, *d_pairs = attend_backward(
        net, d_attended, attended_0, log_0, queries_0, pieces_0, place
    )
    d_queries, d_pairs, sums, deep_sum_1 = tie((d_queries, d_pairs, sums, deep_sum_1))
    sums = net.split_second(sums)
    d_pairs = tie(d_pairs, sums)
    sums = net.move_second(sums)
    deep_sum_1 = net.total(deep_sum_1)
    adds, sums = tie((net.reduce_pairs(d_pairs), sums), deep_sum_1)
    sums = net.split_column(sums)
    adds = tie(adds, sums)
    sums = net.move_column(sums)
    d_input, mixed_keep, mixed_send = input_backward(
        net, source, attended_0, d_middle, d_queries, adds, gain_grad, mixed_0, g_attn_0, place
    )
    d_input, mixed_keep, mixed_send = tie((d_input, mixed_keep, mixed_send), sums[1])

    mixed_sum = net.split_square(net.reduce_core(mixed_keep, mixed_send))
    d_input = net.unspread(tie(d_input, mixed_sum))
    mixed_sum = net.move_square(mixed_sum)
    mixed_sum, d_input = tie((mixed_sum, d_input))
    mixed_sum = net.split_column(mixed_sum)
    sums, d_input = tie((sums, d_input), mixed_sum)
    mixed_sum = net.move_column(mixed_sum)
    mixed_sum_1 = net.total(sums, slice(None, 80))
    deep_sum = net.cross(net.total(sums, slice(80, None)), deep_sum_1)
    kept = jnp.where(net.section == 0, d_input, second)
    crossed = swap_x(jnp.where(net.section == 0, second, d_input))
    mixed_sum, crossed, deep_sum = tie((mixed_sum, crossed, deep_sum))
    edges = jnp.stack(
        [jnp.where(net.section == 0, kept, crossed), jnp.where(net.section == 0, crossed, kept)]
    ).astype(F32)
    mixed_sum = net.cross(net.total(mixed_sum), mixed_sum_1)
    mixed_sum, edges = tie((mixed_sum, edges))
    wide_grad, down_grad, gain_grads = net.finish(mixed_sum, deep_sum, shard)
    mixed = wide_grad[0]
    return (
        edges[None, None],
        mixed[None, :, :QW],
        mixed[None, :, QW:TURNED],
        mixed[None, :, TURNED + QW :],
        mixed[None, :, TURNED : TURNED + QW],
        wide_grad[1][None],
        wide_grad[2][None],
        down_grad[None],
        gain_grads[0][None],
        gain_grads[1][None],
    )


def solution(mesh):
    rows = P("section", ("ctx", "fsdp"), None)
    gains = P("section", ("ctx", "fsdp"))
    blocks = P("fsdp", None, "ctx", None)
    return jax.shard_map(
        shards,
        mesh=mesh,
        in_specs=(blocks, P("fsdp", None, None), blocks) + (rows,) * 7 + (gains,) * 2,
        out_specs=(P("section", "fsdp", None, "ctx", None),) + (rows,) * 7 + (gains,) * 2,
        check_vma=False,
    )
```

```python
import functools

import jax
import jax.numpy as jnp
from jax import lax
from jax.experimental import pallas as pl
from jax.experimental.pallas import tpu as pltpu
from jax.sharding import PartitionSpec as P

D = 576
HQ = 9
KV = 3
HD = 64
GROUP = HQ // KV
QW = HQ * HD
KW = KV * HD
TURNED = QW + KW
MIXED = 2 * QW + 2 * KW
HALF = MIXED // 2

EPSILON = 1e-05
THETA = 10000.0
BF = jnp.bfloat16
F32 = jnp.float32
I32 = jnp.int32
MIB = 1024 * 1024


def mm(left, right):
    return jnp.dot(left, right, preferred_element_type=F32)


def mm_nt(left, right):
    return lax.dot_general(left, right, (((1,), (1,)), ((), ())), preferred_element_type=F32)


def mm_tn(left, right):
    return lax.dot_general(left, right, (((0,), (0,)), ((), ())), preferred_element_type=F32)


def struct(shape, dtype):
    return jax.ShapeDtypeStruct(shape, dtype)


def flip(count, bit):
    return [(i, i ^ bit) for i in range(count)]


def ring(count, steps):
    return [(i, (i + steps) % count) for i in range(count)]


def swap_core(value):
    return lax.ppermute(value, "fsdp", flip(4, 1))


def swap_y(value):
    return lax.ppermute(value, "fsdp", flip(4, 2))


def swap_zpair(value):
    return lax.ppermute(value, "ctx", flip(4, 1))


def swap_x(value):
    return lax.ppermute(value, "section", flip(2, 1))


def swap_corner(value):
    return lax.ppermute(value, ("section", "fsdp"), flip(8, 6))


def tie(value, *others):
    return lax.optimization_barrier((value, others))[0]


def spread_pairs(odd):
    pairs = []
    for z in range(4):
        for f in range(4):
            y, c = f // 2, f % 2
            half = 2 * z + odd
            member = min(half, 7 - half)
            pairs.append((z * 4 + f, (2 * c + member // 2) * 4 + 2 * y + member % 2))
    return pairs


def backwards(pairs):
    return [(target, source) for source, target in pairs]


def turn_tables(offsets):
    middle = HD // 2
    frequency = THETA ** (-jnp.arange(middle, dtype=F32) * 2.0 / HD)
    angles = offsets.astype(F32)[:, None] * frequency[None, :]
    cosine, sine = jnp.cos(angles), jnp.sin(angles)
    return jnp.concatenate([cosine] * 4, axis=1), jnp.concatenate([-sine, sine] * 2, axis=1)


def turn(values, cosine, sine):
    low = lax.broadcasted_iota(I32, (values.shape[0], 128), 1) % HD < HD // 2
    tiles = []
    for first in range(0, values.shape[1], 128):
        tile = values[:, first : first + 128]
        beside = jnp.where(low, pltpu.roll(tile, 128 - HD // 2, 1), pltpu.roll(tile, HD // 2, 1))
        tiles.append(tile * cosine + beside * sine)
    return jnp.concatenate(tiles, axis=1)


def norm(values, gain):
    inverse = lax.rsqrt(jnp.mean(values * values, axis=-1, keepdims=True) + EPSILON)
    scaled = values * inverse
    return inverse, scaled, (scaled * gain).astype(BF)


def norm_back(d_normed, scaled, inverse, gain):
    gain_grad = jnp.sum(d_normed * scaled, axis=0, keepdims=True)
    d_scaled = d_normed * gain
    d_source = inverse * (d_scaled - scaled * jnp.mean(d_scaled * scaled, axis=-1, keepdims=True))
    return d_source, gain_grad


def split_heads(piece_refs, key_scr, value_scr, parts):
    count = sum(ref.shape[0] for ref in piece_refs)
    index = 0
    for ref in piece_refs:
        rows = ref.shape[1] // parts
        for slot in range(ref.shape[0]):
            for part in range(parts):
                block = ref[slot, part * rows : (part + 1) * rows, :]
                at = pl.ds((part * count + index) * rows, rows)
                for group in range(KV):
                    key_scr[group, at, :] = block[:, group * HD : (group + 1) * HD]
                    value_scr[group, at, :] = block[:, KW + group * HD : KW + (group + 1) * HD]
            index += 1


def store(slot, refs, at, value):
    for index, ref in enumerate(refs):

        @pl.when(slot == index)
        def _(ref=ref):
            ref[at] = value


def each_job(jobs, tile, visit):
    if tile is None:
        visit(jobs)
        return
    _, rows, first_key, keys = jobs[0]

    @pl.loop(0, rows // tile)
    def _(step):
        visit([(pl.multiple_of(step * tile, tile), tile, first_key, keys)])


def job_bias(job, position_ref, start_ref, key_position_ref):
    first, rows, first_key, keys = job
    at = key_position_ref[:, first_key : first_key + keys]
    allowed = (at <= position_ref[pl.ds(first, rows), :]) & (at >= start_ref[pl.ds(first, rows), :])
    return jnp.where(allowed, 0.0, -1e30)


def project_kernel(source_ref, mixed_ref, gain_ref, cosine_ref, sine_ref, query_ref, pairs_ref):
    _, _, normed = norm(source_ref[...].astype(F32), gain_ref[...])
    both = turn(mm(normed, mixed_ref[:, :TURNED]), cosine_ref[...], sine_ref[...]).astype(BF)
    edge = (2 * QW + KW) // 128 * 128
    values = mm(normed, mixed_ref[:, edge:])[:, 2 * QW + KW - edge :].astype(BF)
    query_ref[...] = both[:, :QW]
    pairs_ref[...] = jnp.concatenate([both[:, QW:], values], axis=1)


def attend_kernel(
    jobs, tile, parts, pieces,
    source_ref, query_ref, position_ref, start_ref, key_position_ref, mixed_ref, *refs,
):
    piece_refs, refs = refs[:pieces], refs[pieces:]
    attended_ref, log_ref, middle_ref = refs[:3]
    query_scr, key_scr, value_scr, out_scr, log_scr = refs[3:]
    split_heads(piece_refs, key_scr, value_scr, parts)
    for head in range(HQ):
        query_scr[head] = query_ref[:, head * HD : (head + 1) * HD] * jnp.asarray(HD**-0.5, BF)

    def visit(jobs):
        for job in jobs:
            visit_one(job)

    def visit_one(job):
        bias = job_bias(job, position_ref, start_ref, key_position_ref)
        at = pl.ds(job[0], job[1])
        among = slice(job[2], job[2] + job[3])

        @pl.loop(0, KV)
        def _(group):
            key = key_scr[group, among, :]
            value = value_scr[group, among, :]
            for member in range(GROUP):
                head = group * GROUP + member
                scores = mm_nt(query_scr[head, at, :], key) + bias
                peak = jnp.max(scores, axis=1, keepdims=True)
                weights = jnp.exp(scores - peak)
                total = jnp.sum(weights, axis=1, keepdims=True)
                out_scr[head, at, :] = mm(weights.astype(BF), value) * (1.0 / total)
                log_scr[head, at, :] = peak + jnp.log(total)

    each_job(jobs, tile, visit)
    out = jnp.concatenate([out_scr[head] for head in range(HQ)], axis=1)
    attended_ref[...] = out
    log_ref[...] = jnp.concatenate([log_scr[head] for head in range(HQ)], axis=1)
    added = mm(out.astype(BF), mixed_ref[:, TURNED : TURNED + QW])
    middle_ref[...] = source_ref[...].astype(F32) + added


def mlp_kernel(middle_ref, gate_ref, up_ref, down_ref, gain_ref, result_ref, normed_scr, total_scr):
    middle = middle_ref[...]
    normed_scr[...] = norm(middle, gain_ref[...])[2]
    total_scr[...] = middle
    width = 384

    @pl.loop(0, gate_ref.shape[1] // width)
    def _(step):
        at = pl.ds(pl.multiple_of(step * width, width), width)
        gate = mm(normed_scr[...], gate_ref[:, at])
        up = mm(normed_scr[...], up_ref[:, at])
        hidden = (gate * jax.nn.sigmoid(gate) * up).astype(BF)
        total_scr[...] += mm(hidden, down_ref[at, :])

    result_ref[...] = total_scr[...].astype(BF)


def mlp_back_kernel(
    core_ref, d_result_ref, middle_ref, mixed_ref, gate_ref, up_ref, down_ref, gain_ref, *refs
):
    packed_refs, refs = (refs[:2], refs[2:4]), refs[4:]
    gain_grad_ref, d_middle_ref, d_out_ref, normed_scr, total_scr = refs
    core = core_ref[0]
    gain = gain_ref[...]
    inverse, scaled, normed = norm(middle_ref[...], gain)
    normed_scr[...] = normed
    total_scr[...] = jnp.zeros_like(total_scr)
    width = 384

    for step in range(gate_ref.shape[1] // width):
        at = slice(step * width, (step + 1) * width)
        low = d_result_ref[...]
        normed = normed_scr[...]
        gate = mm(normed, gate_ref[:, at])
        up = mm(normed, up_ref[:, at])
        d_hidden = mm_nt(low, down_ref[at, :])
        sigmoid = jax.nn.sigmoid(gate)
        silu = gate * sigmoid
        d_gate = (d_hidden * up * sigmoid * (1.0 + gate * (1.0 - sigmoid))).astype(BF)
        d_up = (d_hidden * silu).astype(BF)
        hidden = (silu * up).astype(BF)
        total_scr[...] += mm_nt(d_gate, gate_ref[:, at]) + mm_nt(d_up, up_ref[:, at])
        gate_grad = mm_tn(normed, d_gate)
        up_grad = mm_tn(normed, d_up)
        down_grad = mm_tn(hidden, low)
        columns = slice((step % 2) * width, (step % 2 + 1) * width)
        for z in range(4):
            wide = [
                jnp.concatenate([grad[72 * k : 72 * k + 72] for grad in (gate_grad, up_grad)], axis=0)
                for k in (2 * z, 2 * z + 1)
            ]
            refs = [group[z // 2] for group in packed_refs]
            place = (slice(2 * (z % 2), 2 * (z % 2) + 2), slice(0, 144), columns)
            store(core ^ (step // 2), refs, place, jnp.stack(wide).astype(BF))
        down_grad = down_grad.reshape(2, 2, 96, D).astype(BF)
        down_grad = jnp.concatenate([down_grad, jnp.zeros((2, 2, 96, HALF - D), BF)], axis=3)
        for side in (0, 1):
            refs = [group[step // 2] for group in packed_refs]
            place = (slice(2 * (step % 2), 2 * (step % 2) + 2), slice(144, 240), slice(None))
            store(core ^ side, refs, place, down_grad[:, side])

    d_mlp, gain_grad = norm_back(total_scr[...], scaled, inverse, gain)
    gain_grad_ref[...] = gain_grad
    d_middle = d_result_ref[...].astype(F32) + d_mlp
    d_middle_ref[...] = d_middle
    d_out_ref[...] = mm_nt(d_middle.astype(BF), mixed_ref[:, TURNED : TURNED + QW]).astype(BF)


def attend_back_kernel(
    jobs, tile, parts, pieces,
    d_out_ref, attended_ref, log_ref, query_ref, position_ref, start_ref, key_position_ref, *refs,
):
    piece_refs, refs = refs[:pieces], refs[pieces:]
    d_query_ref, d_pairs_refs = refs[0], refs[1:-9]
    (
        query_scr, key_scr, value_scr, d_out_scr, log_scr, delta_scr, d_query_scr,
        d_key_scr, d_value_scr,
    ) = refs[-9:]
    d_out = d_out_ref[...]
    split_heads(piece_refs, key_scr, value_scr, parts)
    for head in range(HQ):
        at = slice(head * HD, (head + 1) * HD)
        query_scr[head] = query_ref[:, at] * jnp.asarray(HD**-0.5, BF)
        d_out_scr[head] = d_out[:, at]
        log_scr[head] = log_ref[:, head : head + 1]
        delta_scr[head] = jnp.sum(d_out[:, at].astype(F32) * attended_ref[:, at], 1, keepdims=True)
    d_key_scr[...] = jnp.zeros_like(d_key_scr)
    d_value_scr[...] = jnp.zeros_like(d_value_scr)

    def visit(jobs):
        biases = [job_bias(job, position_ref, start_ref, key_position_ref) for job in jobs]

        @pl.loop(0, KV)
        def _(group):
            for index, (job, bias) in enumerate(zip(jobs, biases)):
                at = pl.ds(job[0], job[1])
                among = slice(job[2], job[2] + job[3])
                key = key_scr[group, among, :]
                value = value_scr[group, among, :]
                for member in range(GROUP):
                    head = group * GROUP + member
                    query = query_scr[head, at, :]
                    d_out = d_out_scr[head, at, :]
                    chances = jnp.exp(mm_nt(query, key) + bias - log_scr[head, at, :])
                    d_chances = mm_nt(d_out, value)
                    d_scores = (chances * (d_chances - delta_scr[head, at, :])).astype(BF)
                    d_query = mm(d_scores, key) * HD**-0.5
                    if index:
                        d_query = d_query + d_query_scr[head, at, :]
                    d_query_scr[head, at, :] = d_query
                    d_value_scr[group, :, among] += mm_tn(d_out, chances.astype(BF))
                    d_key_scr[group, :, among] += mm_tn(query, d_scores)

    each_job(jobs, tile, visit)
    d_query_ref[...] = jnp.concatenate([d_query_scr[head] for head in range(HQ)], axis=1)
    near, whole = d_pairs_refs[0].shape[:2]
    count, rows = near * len(d_pairs_refs), whole // parts
    for first in range(0, count * parts, parts):
        at = slice(first * rows, (first + parts) * rows)
        grads = [scr[group, :, at].T for scr in (d_key_scr, d_value_scr) for group in range(KV)]
        grads = jnp.concatenate(grads, axis=1).astype(BF)
        for index in range(parts):
            part, piece = divmod(first + index, count)
            d_pairs_refs[piece // near][piece % near, part * rows : (part + 1) * rows, :] = grads[
                index * rows : (index + 1) * rows
            ]


def input_kernel(
    adds, core_ref, source_ref, attended_ref, d_middle_ref, d_query_ref, mixed_ref, gain_ref,
    mlp_gain_grad_ref, cosine_ref, sine_ref, *refs,
):
    add_refs, d_source_ref, packed_refs = refs[:adds], refs[adds], refs[adds + 1 :]
    core = core_ref[0]
    gain = gain_ref[...]
    inverse, scaled, normed = norm(source_ref[...].astype(F32), gain)
    d_pairs = sum(ref[...].astype(F32) for ref in add_refs)
    d_both = jnp.concatenate([d_query_ref[...], d_pairs[:, :KW]], axis=1)
    d_both = turn(d_both, cosine_ref[...], -sine_ref[...]).astype(BF)
    d_values = d_pairs[:, KW:].astype(BF)
    d_middle = d_middle_ref[...]
    edge = (2 * QW + KW) // 128 * 128
    lead = 2 * QW + KW - edge
    d_tail = jnp.concatenate([jnp.zeros((d_values.shape[0], lead), BF), d_values], axis=1)
    d_normed = mm_nt(d_both, mixed_ref[:, :TURNED]) + mm_nt(d_tail, mixed_ref[:, edge:])
    d_attn, gain_grad = norm_back(d_normed, scaled, inverse, gain)
    d_source_ref[...] = (d_middle + d_attn).astype(BF)
    first = mm_tn(normed, d_both)
    second = jnp.concatenate(
        [
            mm_tn(attended_ref[...].astype(BF), d_middle.astype(BF)),
            mm_tn(normed, d_values),
        ],
        axis=1,
    )
    gains = (gain_grad, mlp_gain_grad_ref[...])
    for half, grad in enumerate((first, second)):
        blocks = []
        for block in range(8):
            at = 36 * (2 * block + half)
            tail = jnp.concatenate([g[:, at : at + 36] for g in gains] + [jnp.zeros((6, 36), F32)])
            tail = jnp.concatenate([tail, jnp.zeros((8, HALF - 36), F32)], axis=1)
            blocks.append(jnp.concatenate([grad[72 * block : 72 * block + 72], tail], axis=0))
        store(half ^ core, packed_refs, Ellipsis, jnp.stack(blocks).astype(BF))


def assemble_kernel(mixed, doubled, index_ref, *refs):
    pieces, outs = refs[:-3], refs[-3:]
    x, z, y, core = (index_ref[i] for i in range(4))

    def piece(cross, dx, dy, place):
        if len(pieces) == 2:
            return pieces[cross][2 * dx + dy, place].astype(F32)
        first, second = (dx, dy) if place < 2 else (dy, dx)
        ref = pieces[4 * cross + 2 * (place // 2) + first]
        return ref[2 * second + place % 2].astype(F32)

    def ordered(parts):
        rows = [
            [jnp.where(y == 0, a, b), jnp.where(y == 0, b, a)] for a, b in parts
        ]
        return [
            part
            for a, b in zip(*rows)
            for part in (jnp.where(core == 0, a, b), jnp.where(core == 0, b, a))
        ]

    gains = jnp.zeros((8, D), F32)
    owner = lax.broadcasted_iota(I32, (8, D), 1) // 144
    for place, steps in enumerate((0, 1, 3, 2)):
        row = z ^ place if doubled else (z + 4 - steps) % 4
        at = pl.ds(pl.multiple_of(row * 144, 144), 144)
        for dx in (0, 1):
            columns = pl.ds(pl.multiple_of((x ^ dx) * HALF, HALF), HALF)
            parts = ordered(
                [[piece(cross, dx, dy, place) for dy in (0, 1)] for cross in (0, 1)]
            )
            outs[0][at, columns] = jnp.concatenate([part[:36] for part in parts]).astype(BF)
            if mixed:
                block = jnp.concatenate([part[32:40, :36] for part in parts], axis=1)
                here = (owner == row) & (x == dx)
                gains = jnp.where(here, jnp.concatenate([block] * 4, axis=1), gains)
            else:
                outs[1][at, columns] = jnp.concatenate([part[36:72] for part in parts]).astype(BF)
                for index, part in enumerate(parts):
                    first = (4 * row + index) * 96 + (x ^ dx) * 48
                    rows = pl.ds(pl.multiple_of(first, 16), 48)
                    outs[2][rows, :] = part[72:120, :D].astype(BF)
    if mixed:
        outs[1][...] = gains[4:5]
        outs[2][...] = gains[5:6]


def paired(groups, z, y, lanes):
    sums = []
    for keep_refs, received_refs in groups:
        each = 4 // len(keep_refs)
        at = (2 * (z % each) + y, slice(None), lanes)
        sums.append(keep_refs[z // each][at].astype(F32) + received_refs[z // each][at].astype(F32))
    return jnp.concatenate(sums) if len(sums) > 1 else sums[0]


def read_groups(counts, refs):
    groups = []
    for count in counts:
        groups.append((refs[:count], refs[count : 2 * count]))
        refs = refs[2 * count :]
    return groups, refs


def split_square_kernel(counts, index_ref, *refs):
    x, y = index_ref[0], index_ref[1]
    groups, out_refs = read_groups(counts, refs)
    half = HALF // 2
    for index, ref in enumerate(out_refs):
        dx, dy = divmod(index, 2)
        lanes = pl.ds(pl.multiple_of((x ^ dx) * half, half), half)
        for z in range(4):
            ref[z] = paired(groups, z, y ^ dy, lanes).astype(ref.dtype)


def split_first_kernel(counts, index_ref, *refs):
    x, y = index_ref[0], index_ref[1]
    groups, (own_ref, sent_ref, own_row_ref, sent_row_ref) = read_groups(counts, refs)
    half = HALF // 2
    for dx, ref in enumerate((own_ref, sent_ref)):
        lanes = pl.ds(pl.multiple_of((x ^ dx) * half, half), half)
        for z in (0, 1):
            for row in (0, 1):
                ref[z, row] = paired(groups, z, row, lanes).astype(ref.dtype)
    for dy, ref in enumerate((own_row_ref, sent_row_ref)):
        for z in (0, 1):
            ref[z] = paired(groups, z + 2, y ^ dy, slice(None)).astype(ref.dtype)


def split_second_kernel(index_ref, own_ref, moved_ref, own_row_ref, moved_row_ref, *out_refs):
    x, y = index_ref[0], index_ref[1]
    total_ref, sent_ref, sent_row_ref = out_refs
    half = HALF // 2
    for z in (0, 1):
        for step, ref, at in ((0, total_ref, z), (1, sent_ref, z)):
            part = own_ref[z, y ^ step] + moved_ref[z, y ^ step].astype(F32)
            ref[at] = part.astype(ref.dtype)
        for step, ref, at in ((0, total_ref, z + 2), (1, sent_row_ref, z)):
            lanes = pl.ds(pl.multiple_of((x ^ step) * half, half), half)
            part = own_row_ref[z, :, lanes] + moved_row_ref[z, :, lanes].astype(F32)
            ref[at] = part.astype(ref.dtype)


def split_column_kernel(index_ref, *refs):
    parts, out_refs = refs[:-4], refs[-4:]
    for steps, ref in enumerate(out_refs):
        row = (index_ref[2] + steps) % 4
        total = parts[0][row]
        if len(parts) == 3:
            added = [part[row % 2].astype(F32) for part in parts[1:]]
            total = total + jnp.where(row < 2, *added)
        else:
            total = total + sum(part[row].astype(F32) for part in parts[1:])
        ref[...] = total.astype(ref.dtype)


class Fast:
    parts = 2
    tile = None
    limit = staticmethod(lambda mib: mib)

    def __init__(self):
        self.section = lax.axis_index("section")
        self.z = lax.axis_index("ctx")
        f = lax.axis_index("fsdp")
        self.y = f // 2
        self.core = f % 2


    def positions_of(self, dz, dc, rows):
        member = 2 * ((self.z % 2) ^ dz) + (self.core ^ dc)
        iota = jnp.arange(rows // 2, dtype=I32)
        return jnp.concatenate([half * (rows // 2) + iota for half in (member, 7 - member)])

    def lengths(self, lengths):
        mine = lax.dynamic_index_in_dim(lengths[0], self.section, 0, keepdims=False)
        other = swap_core(mine)
        return jnp.where(self.z // 2 == self.core, mine, other)

    def spread(self, block):
        half = block.shape[0] // 2
        even, odd = (
            lax.ppermute(block[k * half : (k + 1) * half], ("ctx", "fsdp"), spread_pairs(k))
            for k in (0, 1)
        )
        low = jnp.where(self.core == 0, even, odd)
        return jnp.concatenate([low, jnp.where(self.core == 0, odd, even)], axis=0)

    def unspread(self, block):
        half = block.shape[0] // 2
        low, high = block[:half], block[half:]
        parts = (jnp.where(self.core == 0, low, high), jnp.where(self.core == 0, high, low))
        return jnp.concatenate(
            [
                lax.ppermute(part, ("ctx", "fsdp"), backwards(spread_pairs(k)))
                for k, part in enumerate(parts)
            ],
            axis=0,
        )

    def key_positions(self, rows):
        at = lax.broadcasted_iota(I32, (1, 4 * rows), 1)
        half = rows // 2
        piece = at // half % 4
        member = 2 * ((self.z % 2) ^ (piece % 2)) + (self.core ^ (piece // 2))
        return jnp.where(at < 4 * half, member, 7 - member) * half + at % half

    def jobs(self, rows, keys):
        half = rows // 2
        return ((0, half, 0, keys // 2), (half, half, 0, keys))

    def back_jobs(self, rows, keys):
        return ((0, rows, 0, keys // 2), (rows // 2, rows // 2, keys // 2, keys // 2))

    def share_pairs(self, pairs):
        along = swap_zpair(pairs)
        return [part[None] for part in (pairs, along, swap_core(pairs), swap_core(along))]

    def reduce_pairs(self, grads):
        near, far = grads
        received = swap_core(far)
        along = near[1].astype(F32) + received[1].astype(F32)
        return [near[0], received[0], swap_zpair(along.astype(BF))]


    def halves(self, part):
        return self.lanes(part, self.section), swap_x(self.lanes(part, 1 - self.section))

    def pack_mixed(self, mixed, gains):
        gains = jnp.pad(gains, ((0, 2), (0, MIXED - mixed.shape[0])))
        return self.halves(jnp.concatenate([mixed, gains], axis=0))

    def pack_deep(self, gate, up, down):
        half = down.shape[0] // 2
        down = jnp.pad(jnp.stack([down[:half], down[half:]], axis=1), ((0, 0), (0, 0), (0, HALF - D)))
        return self.halves(jnp.concatenate([gate, up, down.reshape(half, MIXED)], axis=0))

    def start(self, packs, layer, *after):
        start = [jnp.where(self.section == layer, *pack) for pack in packs]
        return tie(jnp.concatenate(start) if len(start) > 1 else start[0], *after)

    def column(self, packs, layer, *after):
        start = self.start(packs, layer, *after)
        return [start] + [lax.ppermute(start, "ctx", ring(4, steps)) for steps in (1, 3, 2)]

    def pair_column(self, packs, layer, *after):
        start = self.start(packs, layer, *after)
        return jnp.stack([start, swap_zpair(start)])

    def double_column(self, pair, *after):
        pair = tie(pair, *after)
        return pair, lax.ppermute(pair, "ctx", flip(4, 2))

    def slices(self, column, rows):
        return [part[rows] for part in column] if len(column) == 4 else [
            part[k, rows] for part in column for k in (0, 1)
        ]

    def square(self, column, *after, rows=slice(None)):
        column = jnp.stack(self.slices(tie(column, *after), rows))
        return column, swap_y(column), swap_x(column), swap_corner(column)

    def gather_square(self, square, *after):
        pieces = jnp.stack(tie(square, *after))
        return [pieces, swap_core(pieces)]

    def first_phase(self, column, *after, rows=slice(None)):
        column = self.slices(tie(column, *after), rows)
        first, second = jnp.stack(column[:2]), jnp.stack(column[2:])
        return first, swap_y(first), second, swap_x(second)

    def second_phase(self, phase, *after):
        phase = tie(phase, *after)
        first, second = jnp.concatenate(phase[:2]), jnp.concatenate(phase[2:])
        return first, swap_x(first), second, swap_y(second)

    def early_core(self, phase):
        return [swap_core(phase[0]), swap_core(phase[2])]

    def gather_phase(self, phase, early, *after):
        phase = tie(phase, *after)
        late = [swap_core(phase[1]), swap_core(phase[3])]
        return [*phase, early[0], late[0], early[1], late[1]]

    def assemble(self, pieces, rows, doubled, *after):
        pieces = tie(pieces, *after)
        mixed = pieces[0].shape[-2] < 2 * rows
        if mixed:
            outs = (struct((D, MIXED), BF), struct((1, D), F32), struct((1, D), F32))
        else:
            depth = 32 * (pieces[0].shape[-2] - 2 * rows)
            outs = (struct((D, MIXED), BF), struct((D, MIXED), BF), struct((depth, D), BF))
        weights = pl.pallas_call(
            functools.partial(assemble_kernel, mixed, doubled),
            out_shape=outs,
            in_specs=[pl.BlockSpec(memory_space=pltpu.SMEM)]
            + [pl.BlockSpec(memory_space=pltpu.VMEM)] * len(pieces),
            compiler_params=pltpu.CompilerParams(vmem_limit_bytes=20 * MIB),
            name="assemble",
        )(jnp.stack([self.section, self.z, self.y, self.core]), *pieces)
        return weights

    def lanes(self, value, x):
        half = value.shape[-1] // 2
        return lax.dynamic_slice_in_dim(value, x * half, half, value.ndim - 1)

    def row(self, value, y):
        return lax.dynamic_index_in_dim(value, y, 1, keepdims=False)

    def reduce_core(self, keep, send):
        return keep, [swap_core(part) for part in send]

    def index(self):
        return jnp.stack([self.section, self.y, self.z])

    def split(self, kernel, shapes, groups, name):
        rows = sum(keep[0].shape[1] for keep, _ in groups)
        args = [part for pair in groups for parts in pair for part in parts]
        return vmem_call(
            functools.partial(kernel, [len(keep) for keep, _ in groups]),
            [struct(shape[:-1] + (rows, shape[-1]), dtype) for shape, dtype in shapes],
            (self.index(), *args),
            scalars=1,
            limit=20,
            name=name,
        )

    def split_square(self, *groups):
        shapes = [((4, HALF // 2), F32)] + [((4, HALF // 2), BF)] * 3
        return self.split(split_square_kernel, shapes, groups, "split_square")

    def move_square(self, parts):
        swaps = (swap_y, swap_x, swap_corner)
        return [parts[0]] + [swap(part) for swap, part in zip(swaps, parts[1:])]

    def split_first(self, *groups):
        shapes = [((2, 2, HALF // 2), F32), ((2, 2, HALF // 2), BF), ((2, HALF), F32), ((2, HALF), BF)]
        return self.split(split_first_kernel, shapes, groups, "split_first")

    def move_first(self, parts):
        return [parts[0], swap_x(parts[1]), parts[2], swap_y(parts[3])]

    def split_second(self, parts):
        rows = parts[0].shape[2]
        return vmem_call(
            split_second_kernel,
            [struct((4, rows, HALF // 2), F32)] + [struct((2, rows, HALF // 2), BF)] * 2,
            (self.index(), *parts),
            scalars=1,
            limit=20,
            name="split_second",
        )

    def move_second(self, parts):
        return [parts[0], swap_y(parts[1]), swap_x(parts[2])]

    def split_column(self, parts):
        shape = parts[0].shape[1:]
        return vmem_call(
            split_column_kernel,
            [struct(shape, F32)] + [struct(shape, BF)] * 3,
            (self.index(), *parts),
            scalars=1,
            limit=20,
            name="split_column",
        )

    def move_column(self, parts):
        return [parts[0]] + [
            lax.ppermute(part, "ctx", ring(4, steps)) for steps, part in zip((1, 2, 3), parts[1:])
        ]

    def total(self, parts, rows=slice(None)):
        return sum(part[rows].astype(F32) for part in parts)

    def cross(self, first, second):
        own = jnp.where(self.section == 0, first, second)
        other = swap_x(jnp.where(self.section == 0, second, first).astype(BF)).astype(F32)
        left = jnp.where(self.section == 0, own, other)
        return jnp.concatenate([left, jnp.where(self.section == 0, other, own)], axis=1)

    def finish(self, mixed, deep, rows):
        wide = jnp.stack([mixed[: 2 * rows], deep[: 2 * rows], deep[2 * rows : 4 * rows]])
        wide = wide.reshape(3, 2, rows, HALF)
        keep = lax.dynamic_index_in_dim(wide, self.core, 1, keepdims=False)
        sent = lax.dynamic_index_in_dim(wide, 1 - self.core, 1, keepdims=False)
        received = swap_core(sent.astype(BF)).astype(F32)
        left = jnp.where(self.core == 0, keep, received)
        right = jnp.where(self.core == 0, received, keep)
        gains = mixed[2 * rows : 2 * rows + 2, :rows]
        return jnp.concatenate([left, right], axis=2), deep[4 * rows :, :D], gains


class Plain:
    parts = 1
    tile = 16
    limit = staticmethod(lambda mib: 60)

    def __init__(self):
        self.section = lax.axis_index("section")
        self.ctx = lax.axis_index("ctx")
        self.core = jnp.zeros((), I32)

    def positions_of(self, dz, dc, rows):
        return self.ctx * rows + jnp.arange(rows, dtype=I32)

    def lengths(self, lengths):
        return lax.dynamic_index_in_dim(lengths[0], self.section, 0, keepdims=False)

    def spread(self, block):
        return block

    def unspread(self, block):
        return block

    def key_positions(self, rows):
        return jnp.arange(lax.axis_size("ctx") * rows, dtype=I32)[None]

    def jobs(self, rows, keys):
        return ((0, rows, 0, keys),)

    back_jobs = jobs

    def share_pairs(self, pairs):
        return [lax.all_gather(pairs, "ctx", axis=0)]

    def reduce_pairs(self, grads):
        return [lax.psum_scatter(grads[0], "ctx", scatter_dimension=0)]

    def pack_mixed(self, *own):
        return own, tuple(swap_x(part) for part in own)

    pack_deep = pack_mixed

    def column(self, packs, layer, *after):
        return [jnp.where(self.section == layer, a, b) for pack in packs for a, b in zip(*pack)]

    def pair_column(self, packs, layer, *after):
        return self.column(packs, layer)

    def double_column(self, pair, *after):
        return pair

    def square(self, column, *after, rows=slice(None)):
        if len(column) == 5:
            return column[:2] if rows.start is None else column[2:]
        return column

    first_phase = square

    def gather_square(self, square, *after):
        return square

    second_phase = gather_square

    def early_core(self, phase):
        return ()

    def gather_phase(self, phase, early, *after):
        return phase

    def assemble(self, square, rows, doubled, *after):
        axes = ("ctx", "fsdp")
        weights = [
            lax.all_gather(part, axes, axis=int(part.shape[0] == 2), tiled=True) for part in square
        ]
        if len(weights) == 2:
            gains = weights[1].astype(F32)
            return weights[0], gains[:1], gains[1:]
        return weights

    def reduce_core(self, keep, send):
        return keep, send

    def split_square(self, *groups):
        return groups

    split_first = split_square

    def move_square(self, groups):
        return groups

    move_first = split_second = move_second = split_column = move_column = move_square

    def total(self, groups, rows=slice(None)):
        return groups[rows.start is not None]

    def reduce(self, mixed, deep):
        mixed, deep = ([jnp.concatenate(part) for part in pair] for pair in (mixed, deep))

        def columns(pair, first):
            return jnp.concatenate([part[:, first : first + 72] for part in pair], axis=2)

        wide = jnp.stack([columns(mixed, 0), columns(deep, 0), columns(deep, 72)])
        down = jnp.stack([part[:, 144:, :D] for part in deep], axis=1)
        gains = jnp.stack([part[:, 72:74, :36] for part in mixed], axis=1)
        gains = jnp.moveaxis(gains.reshape(16, 2, 36), 1, 0)
        axes = ("ctx", "fsdp")
        return tuple(
            lax.psum_scatter(part, axes, scatter_dimension=axis, tiled=True).astype(F32)
            for part, axis in (
                (wide.reshape(3, D, MIXED), 1),
                (down.reshape(-1, D), 0),
                (gains.reshape(2, D), 1),
            )
        )

    def cross(self, first, second):
        return first, second

    def finish(self, mixed, deep, rows):
        first, second = (self.reduce(*pair) for pair in zip(mixed, deep))
        return tuple(
            jnp.where(self.section == 0, a, b) + swap_x(jnp.where(self.section == 0, b, a))
            for a, b in zip(first, second)
        )


def vmem_call(kernel, out_shape, args, scratch=(), scalars=0, limit=16, name=None):
    specs = [pl.BlockSpec(memory_space=pltpu.SMEM)] * scalars
    specs += [pl.BlockSpec(memory_space=pltpu.VMEM)] * (len(args) - scalars)
    return pl.pallas_call(
        kernel,
        out_shape=out_shape,
        in_specs=specs,
        scratch_shapes=list(scratch),
        compiler_params=pltpu.CompilerParams(vmem_limit_bytes=limit * MIB),
        name=name,
    )(*args)


def project(net, source, mixed, g_attn, place):
    rows = source.shape[0]
    queries, pairs = vmem_call(
        project_kernel,
        (struct((rows, QW), BF), struct((rows, 2 * KW), BF)),
        (source, mixed, g_attn, place[2], place[3]),
        limit=8,
        name="project",
    )
    return queries, pairs


def attend_forward(net, source, queries, pieces, mixed, place):
    positions, starts, _, _, key_positions = place
    rows, keys = source.shape[0], key_positions.shape[1]
    return vmem_call(
        functools.partial(attend_kernel, net.jobs(rows, keys), net.tile, net.parts, len(pieces)),
        (struct((rows, QW), F32), struct((rows, HQ), F32), struct((rows, D), F32)),
        (source, queries, positions, starts, key_positions, mixed, *pieces),
        [
            pltpu.VMEM((HQ, rows, HD), BF),
            pltpu.VMEM((KV, keys, HD), BF),
            pltpu.VMEM((KV, keys, HD), BF),
            pltpu.VMEM((HQ, rows, HD), F32),
            pltpu.VMEM((HQ, rows, 1), F32),
        ],
        limit=net.limit(16),
        name="attend",
    )


def mlp_forward(middle, gate, up, down, g_mlp):
    rows = middle.shape[0]
    return vmem_call(
        mlp_kernel,
        struct((rows, D), BF),
        (middle, gate, up, down, g_mlp),
        [pltpu.VMEM((rows, D), BF), pltpu.VMEM((rows, D), F32)],
        limit=12,
        name="mlp",
    )


def mlp_backward(net, d_result, middle, mixed, gate, up, down, g_mlp):
    rows = middle.shape[0]
    deep_rows = 144 + down.shape[0] // 16
    shapes = [struct((4, deep_rows, HALF), BF)] * 4
    outs = vmem_call(
        mlp_back_kernel,
        shapes + [struct((1, D), F32), struct((rows, D), F32), struct((rows, QW), BF)],
        (net.core.reshape(1), d_result, middle, mixed, gate, up, down, g_mlp),
        [pltpu.VMEM((rows, D), BF), pltpu.VMEM((rows, D), F32)],
        scalars=1,
        limit=22,
        name="mlp_back",
    )
    return outs[:2], outs[2:4], *outs[4:]


def attend_backward(net, d_attended, attended, log_total, queries, pieces, place):
    positions, starts, _, _, key_positions = place
    rows, keys = positions.shape[0], key_positions.shape[1]
    return vmem_call(
        functools.partial(
            attend_back_kernel, net.back_jobs(rows, keys), net.tile, net.parts, len(pieces)
        ),
        [struct((rows, QW), F32)]
        + [struct((keys // rows // net.parts, rows, 2 * KW), BF)] * net.parts,
        (d_attended, attended, log_total, queries, positions, starts, key_positions, *pieces),
        [
            pltpu.VMEM((HQ, rows, HD), BF),
            pltpu.VMEM((KV, keys, HD), BF),
            pltpu.VMEM((KV, keys, HD), BF),
            pltpu.VMEM((HQ, rows, HD), BF),
            pltpu.VMEM((HQ, rows, 1), F32),
            pltpu.VMEM((HQ, rows, 1), F32),
            pltpu.VMEM((HQ, rows, HD), F32),
            pltpu.VMEM((KV, HD, keys), F32),
            pltpu.VMEM((KV, HD, keys), F32),
        ],
        limit=net.limit(22),
        name="attend_back",
    )


def input_backward(
    net, source, attended, d_middle, d_queries, adds, gain_grad, mixed, g_attn, place
):
    rows = source.shape[0]
    mixed_shape = struct((8, 80, HALF), BF)
    d_source, keep, send = vmem_call(
        functools.partial(input_kernel, len(adds)),
        (struct((rows, D), BF), mixed_shape, mixed_shape),
        (
            net.core.reshape(1), source, attended, d_middle, d_queries, mixed, g_attn, gain_grad,
            place[2], place[3], *adds,
        ),
        scalars=1,
        limit=12,
        name="input",
    )
    return d_source, [keep], [send]


def shards(
    inputs, lengths, cotangent, w_query, w_key, w_value, w_out, w_gate, w_up, w_down, g_attn, g_mlp
):
    sizes = tuple(lax.axis_size(axis) for axis in ("section", "ctx", "fsdp"))
    net = Fast() if sizes == (2, 4, 4) else Plain()
    rows = inputs.shape[2]
    mixed = jnp.concatenate([w_query[0], w_key[0], w_out[0], w_value[0]], axis=1)
    mixed_pack = net.pack_mixed(mixed, jnp.stack([g_attn[0], g_mlp[0]]))
    shard = w_query.shape[1]
    lengths, gate, up, down, inputs, cotangent = tie(
        (lengths, w_gate[0], w_up[0], w_down[0], inputs, cotangent), mixed_pack[0]
    )
    deep_pack = net.pack_deep(gate, up, down)
    mixed_column = net.column([mixed_pack], 0)
    own = net.lengths(lengths)
    positions = net.positions_of(0, 0, rows)
    passed = (positions[:, None] >= jnp.cumsum(own)[None, :]).astype(I32)
    starts = jnp.sum(passed * own[None, :], axis=1)
    cosine, sine = turn_tables(positions - starts)
    place = (positions[:, None], starts[:, None], cosine, sine, net.key_positions(rows))
    source = lax.dynamic_index_in_dim(inputs[0], net.section, 0, keepdims=False)
    d_result = lax.dynamic_index_in_dim(cotangent[0], net.section, 0, keepdims=False)
    mixed_square = net.square(mixed_column)
    deep_column = net.column([deep_pack], 0, mixed_column)
    source, d_result, place = tie((source, d_result, place), mixed_column)
    mixed_rows = mixed_square[0].shape[-2]
    mixed_pieces = net.gather_square(mixed_square)
    deep_phase = net.first_phase(deep_column, mixed_square)
    source = net.spread(tie(source, deep_column))
    mixed_0, g_attn_0, g_mlp_0 = net.assemble(mixed_pieces, shard, False)

    queries_0, pairs = project(net, source, mixed_0, g_attn_0, place)
    deep_phase = net.second_phase(deep_phase, source)
    pieces_0 = net.share_pairs(pairs)
    column = net.pair_column([mixed_pack, deep_pack], 1, queries_0)
    early = net.early_core(deep_phase)
    column = net.double_column(column, pieces_0)
    attended_0, log_0, middle_0 = attend_forward(net, source, queries_0, pieces_0, mixed_0, place)
    middle_0, column, deep_phase, early = tie((middle_0, column, deep_phase, early))
    mixed_square = net.square(column, rows=slice(None, mixed_rows))
    deep_0 = net.assemble(net.gather_phase(deep_phase, early), shard, False)
    first = mlp_forward(middle_0, *deep_0, g_mlp_0)
    first, mixed_square = tie((first, mixed_square))
    mixed_pieces = net.gather_square(mixed_square)
    deep_phase = net.first_phase(column, mixed_square, rows=slice(mixed_rows, None))
    mixed_1, g_attn_1, g_mlp_1 = net.assemble(mixed_pieces, shard, True)

    queries_1, pairs = project(net, first, mixed_1, g_attn_1, place)
    pieces_1 = net.share_pairs(pairs)
    deep_phase = net.second_phase(deep_phase, queries_1)
    d_result = net.spread(tie(d_result, pieces_1))
    attended_1, log_1, middle_1 = attend_forward(net, first, queries_1, pieces_1, mixed_1, place)
    middle_1, deep_phase, d_result = tie((middle_1, deep_phase, d_result))
    deep_1 = net.assemble(
        net.gather_phase(deep_phase, net.early_core(deep_phase)), shard, True
    )

    deep_keep, deep_send, gain_grad, d_middle, d_attended = mlp_backward(
        net, d_result, middle_1, mixed_1, *deep_1, g_mlp_1
    )
    deep_sum = net.reduce_core(deep_keep, deep_send)
    d_queries, *d_pairs = attend_backward(
        net, d_attended, attended_1, log_1, queries_1, pieces_1, place
    )
    d_queries, d_pairs, deep_sum = tie((d_queries, d_pairs, deep_sum))
    deep_sum = net.split_first(deep_sum)
    d_pairs = tie(d_pairs, deep_sum)
    deep_sum = net.move_first(deep_sum)
    second = mlp_forward(tie(middle_1, d_pairs), *deep_1, g_mlp_1)
    adds = tie(net.reduce_pairs(d_pairs), second)
    outs = input_backward(
        net, first, attended_1, d_middle, d_queries, adds, gain_grad, mixed_1, g_attn_1, place
    )
    (d_first, mixed_keep, mixed_send), deep_sum = tie((outs, deep_sum))
    deep_sum = net.split_second(deep_sum)
    d_first = tie(d_first, deep_sum)
    deep_sum = net.move_second(deep_sum)
    mixed_sum = net.reduce_core(mixed_keep, mixed_send)
    second = net.unspread(tie(second, d_first))

    outs = mlp_backward(net, d_first, middle_0, mixed_0, *deep_0, g_mlp_0)
    outs, mixed_sum, deep_sum, second = tie((outs, mixed_sum, deep_sum, second))
    deep_keep, deep_send, gain_grad, d_middle, d_attended = outs
    deep_sum = net.split_column(deep_sum)
    d_attended = tie(d_attended, deep_sum)
    deep_sum_1 = net.move_column(deep_sum)
    sums = net.split_first(mixed_sum, net.reduce_core(deep_keep, deep_send))
    d_attended = tie(d_attended, sums)
    sums = net.move_first(sums)
    d_queries, *d_pairs = attend_backward(
        net, d_attended, attended_0, log_0, queries_0, pieces_0, place
    )
    d_queries, d_pairs, sums, deep_sum_1 = tie((d_queries, d_pairs, sums, deep_sum_1))
    sums = net.split_second(sums)
    d_pairs = tie(d_pairs, sums)
    sums = net.move_second(sums)
    deep_sum_1 = net.total(deep_sum_1)
    adds = tie(net.reduce_pairs(d_pairs), deep_sum_1)
    d_input, mixed_keep, mixed_send = input_backward(
        net, source, attended_0, d_middle, d_queries, adds, gain_grad, mixed_0, g_attn_0, place
    )
    d_input, mixed_keep, mixed_send, sums = tie((d_input, mixed_keep, mixed_send, sums))
    sums = net.move_column(net.split_column(sums))

    mixed_sum = net.split_square(net.reduce_core(mixed_keep, mixed_send))
    d_input = net.unspread(tie(d_input, mixed_sum))
    mixed_sum = net.move_square(mixed_sum)
    mixed_sum, d_input = tie((mixed_sum, d_input))
    mixed_sum = net.split_column(mixed_sum)
    sums, d_input = tie((sums, d_input), mixed_sum)
    mixed_sum = net.move_column(mixed_sum)
    mixed_sum_1 = net.total(sums, slice(None, 80))
    deep_sum = net.cross(net.total(sums, slice(80, None)), deep_sum_1)
    kept = jnp.where(net.section == 0, d_input, second)
    crossed = swap_x(jnp.where(net.section == 0, second, d_input))
    mixed_sum, crossed, deep_sum = tie((mixed_sum, crossed, deep_sum))
    edges = jnp.stack(
        [jnp.where(net.section == 0, kept, crossed), jnp.where(net.section == 0, crossed, kept)]
    ).astype(F32)
    mixed_sum = net.cross(net.total(mixed_sum), mixed_sum_1)
    mixed_sum, edges = tie((mixed_sum, edges))
    wide_grad, down_grad, gain_grads = net.finish(mixed_sum, deep_sum, shard)
    mixed = wide_grad[0]
    return (
        edges[None, None],
        mixed[None, :, :QW],
        mixed[None, :, QW:TURNED],
        mixed[None, :, TURNED + QW :],
        mixed[None, :, TURNED : TURNED + QW],
        wide_grad[1][None],
        wide_grad[2][None],
        down_grad[None],
        gain_grads[0][None],
        gain_grads[1][None],
    )


def solution(mesh):
    rows = P("section", ("ctx", "fsdp"), None)
    gains = P("section", ("ctx", "fsdp"))
    blocks = P("fsdp", None, "ctx", None)
    return jax.shard_map(
        shards,
        mesh=mesh,
        in_specs=(blocks, P("fsdp", None, None), blocks) + (rows,) * 7 + (gains,) * 2,
        out_specs=(P("section", "fsdp", None, "ctx", None),) + (rows,) * 7 + (gains,) * 2,
        check_vma=False,
    )
```

```python
import functools

import jax
import jax.numpy as jnp
from jax import lax
from jax.experimental import pallas as pl
from jax.experimental.pallas import tpu as pltpu
from jax.sharding import PartitionSpec as P

D = 576
HQ = 9
KV = 3
HD = 64
GROUP = HQ // KV
QW = HQ * HD
KW = KV * HD
TURNED = QW + KW
MIXED = 2 * QW + 2 * KW
HALF = MIXED // 2

EPSILON = 1e-05
THETA = 10000.0
BF = jnp.bfloat16
F32 = jnp.float32
I32 = jnp.int32
MIB = 1024 * 1024


def mm(left, right):
    return jnp.dot(left, right, preferred_element_type=F32)


def mm_nt(left, right):
    return lax.dot_general(left, right, (((1,), (1,)), ((), ())), preferred_element_type=F32)


def mm_tn(left, right):
    return lax.dot_general(left, right, (((0,), (0,)), ((), ())), preferred_element_type=F32)


def struct(shape, dtype):
    return jax.ShapeDtypeStruct(shape, dtype)


def flip(count, bit):
    return [(i, i ^ bit) for i in range(count)]


def ring(count, steps):
    return [(i, (i + steps) % count) for i in range(count)]


def swap_core(value):
    return lax.ppermute(value, "fsdp", flip(4, 1))


def swap_y(value):
    return lax.ppermute(value, "fsdp", flip(4, 2))


def swap_zpair(value):
    return lax.ppermute(value, "ctx", flip(4, 1))


def swap_x(value):
    return lax.ppermute(value, "section", flip(2, 1))


def swap_corner(value):
    return lax.ppermute(value, ("section", "fsdp"), flip(8, 6))


def tie(value, *others):
    return lax.optimization_barrier((value, others))[0]


def spread_pairs(odd):
    pairs = []
    for z in range(4):
        for f in range(4):
            y, c = f // 2, f % 2
            half = 2 * z + odd
            member = min(half, 7 - half)
            pairs.append((z * 4 + f, (2 * c + member // 2) * 4 + 2 * y + member % 2))
    return pairs


def backwards(pairs):
    return [(target, source) for source, target in pairs]


def turn_tables(offsets):
    middle = HD // 2
    frequency = THETA ** (-jnp.arange(middle, dtype=F32) * 2.0 / HD)
    angles = offsets.astype(F32)[:, None] * frequency[None, :]
    cosine, sine = jnp.cos(angles), jnp.sin(angles)
    return jnp.concatenate([cosine] * 4, axis=1), jnp.concatenate([-sine, sine] * 2, axis=1)


def turn(values, cosine, sine):
    low = lax.broadcasted_iota(I32, (values.shape[0], 128), 1) % HD < HD // 2
    tiles = []
    for first in range(0, values.shape[1], 128):
        tile = values[:, first : first + 128]
        beside = jnp.where(low, pltpu.roll(tile, 128 - HD // 2, 1), pltpu.roll(tile, HD // 2, 1))
        tiles.append(tile * cosine + beside * sine)
    return jnp.concatenate(tiles, axis=1)


def norm(values, gain):
    inverse = lax.rsqrt(jnp.mean(values * values, axis=-1, keepdims=True) + EPSILON)
    scaled = values * inverse
    return inverse, scaled, (scaled * gain).astype(BF)


def norm_back(d_normed, scaled, inverse, gain):
    gain_grad = jnp.sum(d_normed * scaled, axis=0, keepdims=True)
    d_scaled = d_normed * gain
    d_source = inverse * (d_scaled - scaled * jnp.mean(d_scaled * scaled, axis=-1, keepdims=True))
    return d_source, gain_grad


def split_heads(piece_refs, key_scr, value_scr, parts):
    count = sum(ref.shape[0] for ref in piece_refs)
    index = 0
    for ref in piece_refs:
        rows = ref.shape[1] // parts
        for slot in range(ref.shape[0]):
            for part in range(parts):
                block = ref[slot, part * rows : (part + 1) * rows, :]
                at = pl.ds((part * count + index) * rows, rows)
                for group in range(KV):
                    key_scr[group, at, :] = block[:, group * HD : (group + 1) * HD]
                    value_scr[group, at, :] = block[:, KW + group * HD : KW + (group + 1) * HD]
            index += 1


def store(slot, refs, at, value):
    for index, ref in enumerate(refs):

        @pl.when(slot == index)
        def _(ref=ref):
            ref[at] = value


def each_job(jobs, tile, visit):
    if tile is None:
        visit(jobs)
        return
    _, rows, first_key, keys = jobs[0]

    @pl.loop(0, rows // tile)
    def _(step):
        visit([(pl.multiple_of(step * tile, tile), tile, first_key, keys)])


def job_bias(job, position_ref, start_ref, key_position_ref):
    first, rows, first_key, keys = job
    at = key_position_ref[:, first_key : first_key + keys]
    allowed = (at <= position_ref[pl.ds(first, rows), :]) & (at >= start_ref[pl.ds(first, rows), :])
    return jnp.where(allowed, 0.0, -1e30)


def project_kernel(source_ref, mixed_ref, gain_ref, cosine_ref, sine_ref, query_ref, pairs_ref):
    _, _, normed = norm(source_ref[...].astype(F32), gain_ref[...])
    both = turn(mm(normed, mixed_ref[:, :TURNED]), cosine_ref[...], sine_ref[...]).astype(BF)
    edge = (2 * QW + KW) // 128 * 128
    values = mm(normed, mixed_ref[:, edge:])[:, 2 * QW + KW - edge :].astype(BF)
    query_ref[...] = both[:, :QW]
    pairs_ref[...] = jnp.concatenate([both[:, QW:], values], axis=1)


def attend_kernel(
    jobs, tile, parts, pieces,
    source_ref, query_ref, position_ref, start_ref, key_position_ref, mixed_ref, *refs,
):
    piece_refs, refs = refs[:pieces], refs[pieces:]
    attended_ref, log_ref, middle_ref = refs[:3]
    query_scr, key_scr, value_scr, out_scr, log_scr = refs[3:]
    split_heads(piece_refs, key_scr, value_scr, parts)
    for head in range(HQ):
        query_scr[head] = query_ref[:, head * HD : (head + 1) * HD] * jnp.asarray(HD**-0.5, BF)

    def visit(jobs):
        for job in jobs:
            visit_one(job)

    def visit_one(job):
        bias = job_bias(job, position_ref, start_ref, key_position_ref)
        at = pl.ds(job[0], job[1])
        among = slice(job[2], job[2] + job[3])

        @pl.loop(0, KV)
        def _(group):
            key = key_scr[group, among, :]
            value = value_scr[group, among, :]
            for member in range(GROUP):
                head = group * GROUP + member
                scores = mm_nt(query_scr[head, at, :], key) + bias
                peak = jnp.max(scores, axis=1, keepdims=True)
                weights = jnp.exp(scores - peak)
                total = jnp.sum(weights, axis=1, keepdims=True)
                out_scr[head, at, :] = mm(weights.astype(BF), value) * (1.0 / total)
                log_scr[head, at, :] = peak + jnp.log(total)

    each_job(jobs, tile, visit)
    out = jnp.concatenate([out_scr[head] for head in range(HQ)], axis=1)
    attended_ref[...] = out
    log_ref[...] = jnp.concatenate([log_scr[head] for head in range(HQ)], axis=1)
    added = mm(out.astype(BF), mixed_ref[:, TURNED : TURNED + QW])
    middle_ref[...] = source_ref[...].astype(F32) + added


def mlp_kernel(middle_ref, gate_ref, up_ref, down_ref, gain_ref, result_ref, normed_scr, total_scr):
    middle = middle_ref[...]
    normed_scr[...] = norm(middle, gain_ref[...])[2]
    total_scr[...] = middle
    width = 384

    @pl.loop(0, gate_ref.shape[1] // width)
    def _(step):
        at = pl.ds(pl.multiple_of(step * width, width), width)
        gate = mm(normed_scr[...], gate_ref[:, at])
        up = mm(normed_scr[...], up_ref[:, at])
        hidden = (gate * jax.nn.sigmoid(gate) * up).astype(BF)
        total_scr[...] += mm(hidden, down_ref[at, :])

    result_ref[...] = total_scr[...].astype(BF)


def mlp_back_kernel(
    core_ref, d_result_ref, middle_ref, mixed_ref, gate_ref, up_ref, down_ref, gain_ref, *refs
):
    packed_refs, refs = (refs[:2], refs[2:4]), refs[4:]
    gain_grad_ref, d_middle_ref, d_out_ref, normed_scr, total_scr = refs
    core = core_ref[0]
    gain = gain_ref[...]
    inverse, scaled, normed = norm(middle_ref[...], gain)
    normed_scr[...] = normed
    total_scr[...] = jnp.zeros_like(total_scr)
    width = 384

    for step in range(gate_ref.shape[1] // width):
        at = slice(step * width, (step + 1) * width)
        low = d_result_ref[...]
        normed = normed_scr[...]
        gate = mm(normed, gate_ref[:, at])
        up = mm(normed, up_ref[:, at])
        d_hidden = mm_nt(low, down_ref[at, :])
        sigmoid = jax.nn.sigmoid(gate)
        silu = gate * sigmoid
        d_gate = (d_hidden * up * sigmoid * (1.0 + gate * (1.0 - sigmoid))).astype(BF)
        d_up = (d_hidden * silu).astype(BF)
        hidden = (silu * up).astype(BF)
        total_scr[...] += mm_nt(d_gate, gate_ref[:, at]) + mm_nt(d_up, up_ref[:, at])
        gate_grad = mm_tn(normed, d_gate)
        up_grad = mm_tn(normed, d_up)
        down_grad = mm_tn(hidden, low)
        columns = slice((step % 2) * width, (step % 2 + 1) * width)
        for z in range(4):
            wide = [
                jnp.concatenate([grad[72 * k : 72 * k + 72] for grad in (gate_grad, up_grad)], axis=0)
                for k in (2 * z, 2 * z + 1)
            ]
            refs = [group[z // 2] for group in packed_refs]
            place = (slice(2 * (z % 2), 2 * (z % 2) + 2), slice(0, 144), columns)
            store(core ^ (step // 2), refs, place, jnp.stack(wide).astype(BF))
        down_grad = down_grad.reshape(2, 2, 96, D).astype(BF)
        down_grad = jnp.concatenate([down_grad, jnp.zeros((2, 2, 96, HALF - D), BF)], axis=3)
        for side in (0, 1):
            refs = [group[step // 2] for group in packed_refs]
            place = (slice(2 * (step % 2), 2 * (step % 2) + 2), slice(144, 240), slice(None))
            store(core ^ side, refs, place, down_grad[:, side])

    d_mlp, gain_grad = norm_back(total_scr[...], scaled, inverse, gain)
    gain_grad_ref[...] = gain_grad
    d_middle = d_result_ref[...].astype(F32) + d_mlp
    d_middle_ref[...] = d_middle
    d_out_ref[...] = mm_nt(d_middle.astype(BF), mixed_ref[:, TURNED : TURNED + QW]).astype(BF)


def attend_back_kernel(
    jobs, tile, parts, pieces,
    d_out_ref, attended_ref, log_ref, query_ref, position_ref, start_ref, key_position_ref, *refs,
):
    piece_refs, refs = refs[:pieces], refs[pieces:]
    d_query_ref, d_pairs_refs = refs[0], refs[1:-9]
    (
        query_scr, key_scr, value_scr, d_out_scr, log_scr, delta_scr, d_query_scr,
        d_key_scr, d_value_scr,
    ) = refs[-9:]
    d_out = d_out_ref[...]
    split_heads(piece_refs, key_scr, value_scr, parts)
    for head in range(HQ):
        at = slice(head * HD, (head + 1) * HD)
        query_scr[head] = query_ref[:, at] * jnp.asarray(HD**-0.5, BF)
        d_out_scr[head] = d_out[:, at]
        log_scr[head] = log_ref[:, head : head + 1]
        delta_scr[head] = jnp.sum(d_out[:, at].astype(F32) * attended_ref[:, at], 1, keepdims=True)
    d_key_scr[...] = jnp.zeros_like(d_key_scr)
    d_value_scr[...] = jnp.zeros_like(d_value_scr)

    def visit(jobs):
        biases = [job_bias(job, position_ref, start_ref, key_position_ref) for job in jobs]

        @pl.loop(0, KV)
        def _(group):
            for index, (job, bias) in enumerate(zip(jobs, biases)):
                at = pl.ds(job[0], job[1])
                among = slice(job[2], job[2] + job[3])
                key = key_scr[group, among, :]
                value = value_scr[group, among, :]
                for member in range(GROUP):
                    head = group * GROUP + member
                    query = query_scr[head, at, :]
                    d_out = d_out_scr[head, at, :]
                    chances = jnp.exp(mm_nt(query, key) + bias - log_scr[head, at, :])
                    d_chances = mm_nt(d_out, value)
                    d_scores = (chances * (d_chances - delta_scr[head, at, :])).astype(BF)
                    d_query = mm(d_scores, key) * HD**-0.5
                    if index:
                        d_query = d_query + d_query_scr[head, at, :]
                    d_query_scr[head, at, :] = d_query
                    d_value_scr[group, :, among] += mm_tn(d_out, chances.astype(BF))
                    d_key_scr[group, :, among] += mm_tn(query, d_scores)

    each_job(jobs, tile, visit)
    d_query_ref[...] = jnp.concatenate([d_query_scr[head] for head in range(HQ)], axis=1)
    near, whole = d_pairs_refs[0].shape[:2]
    count, rows = near * len(d_pairs_refs), whole // parts
    for first in range(0, count * parts, parts):
        at = slice(first * rows, (first + parts) * rows)
        grads = [scr[group, :, at].T for scr in (d_key_scr, d_value_scr) for group in range(KV)]
        grads = jnp.concatenate(grads, axis=1).astype(BF)
        for index in range(parts):
            part, piece = divmod(first + index, count)
            d_pairs_refs[piece // near][piece % near, part * rows : (part + 1) * rows, :] = grads[
                index * rows : (index + 1) * rows
            ]


def input_kernel(
    adds, core_ref, source_ref, attended_ref, d_middle_ref, d_query_ref, mixed_ref, gain_ref,
    mlp_gain_grad_ref, cosine_ref, sine_ref, *refs,
):
    add_refs, d_source_ref, packed_refs = refs[:adds], refs[adds], refs[adds + 1 :]
    core = core_ref[0]
    gain = gain_ref[...]
    inverse, scaled, normed = norm(source_ref[...].astype(F32), gain)
    d_pairs = sum(ref[...].astype(F32) for ref in add_refs)
    d_both = jnp.concatenate([d_query_ref[...], d_pairs[:, :KW]], axis=1)
    d_both = turn(d_both, cosine_ref[...], -sine_ref[...]).astype(BF)
    d_values = d_pairs[:, KW:].astype(BF)
    d_middle = d_middle_ref[...]
    edge = (2 * QW + KW) // 128 * 128
    lead = 2 * QW + KW - edge
    d_tail = jnp.concatenate([jnp.zeros((d_values.shape[0], lead), BF), d_values], axis=1)
    d_normed = mm_nt(d_both, mixed_ref[:, :TURNED]) + mm_nt(d_tail, mixed_ref[:, edge:])
    d_attn, gain_grad = norm_back(d_normed, scaled, inverse, gain)
    d_source_ref[...] = (d_middle + d_attn).astype(BF)
    first = mm_tn(normed, d_both)
    second = jnp.concatenate(
        [
            mm_tn(attended_ref[...].astype(BF), d_middle.astype(BF)),
            mm_tn(normed, d_values),
        ],
        axis=1,
    )
    gains = (gain_grad, mlp_gain_grad_ref[...])
    for half, grad in enumerate((first, second)):
        blocks = []
        for block in range(8):
            at = 36 * (2 * block + half)
            tail = jnp.concatenate([g[:, at : at + 36] for g in gains] + [jnp.zeros((6, 36), F32)])
            tail = jnp.concatenate([tail, jnp.zeros((8, HALF - 36), F32)], axis=1)
            blocks.append(jnp.concatenate([grad[72 * block : 72 * block + 72], tail], axis=0))
        store(half ^ core, packed_refs, Ellipsis, jnp.stack(blocks).astype(BF))


def assemble_kernel(mixed, doubled, index_ref, *refs):
    pieces, outs = refs[:-3], refs[-3:]
    x, z, y, core = (index_ref[i] for i in range(4))

    def piece(cross, dx, dy, place):
        if len(pieces) == 2:
            return pieces[cross][2 * dx + dy, place].astype(F32)
        first, second = (dx, dy) if place < 2 else (dy, dx)
        ref = pieces[4 * cross + 2 * (place // 2) + first]
        return ref[2 * second + place % 2].astype(F32)

    def ordered(parts):
        rows = [
            [jnp.where(y == 0, a, b), jnp.where(y == 0, b, a)] for a, b in parts
        ]
        return [
            part
            for a, b in zip(*rows)
            for part in (jnp.where(core == 0, a, b), jnp.where(core == 0, b, a))
        ]

    gains = jnp.zeros((8, D), F32)
    owner = lax.broadcasted_iota(I32, (8, D), 1) // 144
    for place, steps in enumerate((0, 1, 3, 2)):
        row = z ^ place if doubled else (z + 4 - steps) % 4
        at = pl.ds(pl.multiple_of(row * 144, 144), 144)
        for dx in (0, 1):
            columns = pl.ds(pl.multiple_of((x ^ dx) * HALF, HALF), HALF)
            parts = ordered(
                [[piece(cross, dx, dy, place) for dy in (0, 1)] for cross in (0, 1)]
            )
            outs[0][at, columns] = jnp.concatenate([part[:36] for part in parts]).astype(BF)
            if mixed:
                block = jnp.concatenate([part[32:40, :36] for part in parts], axis=1)
                here = (owner == row) & (x == dx)
                gains = jnp.where(here, jnp.concatenate([block] * 4, axis=1), gains)
            else:
                outs[1][at, columns] = jnp.concatenate([part[36:72] for part in parts]).astype(BF)
                for index, part in enumerate(parts):
                    first = (4 * row + index) * 96 + (x ^ dx) * 48
                    rows = pl.ds(pl.multiple_of(first, 16), 48)
                    outs[2][rows, :] = part[72:120, :D].astype(BF)
    if mixed:
        outs[1][...] = gains[4:5]
        outs[2][...] = gains[5:6]


def paired(groups, z, y, lanes):
    sums = []
    for keep_refs, received_refs in groups:
        each = 4 // len(keep_refs)
        at = (2 * (z % each) + y, slice(None), lanes)
        sums.append(keep_refs[z // each][at].astype(F32) + received_refs[z // each][at].astype(F32))
    return jnp.concatenate(sums) if len(sums) > 1 else sums[0]


def read_groups(counts, refs):
    groups = []
    for count in counts:
        groups.append((refs[:count], refs[count : 2 * count]))
        refs = refs[2 * count :]
    return groups, refs


def split_square_kernel(counts, index_ref, *refs):
    x, y = index_ref[0], index_ref[1]
    groups, out_refs = read_groups(counts, refs)
    half = HALF // 2
    for index, ref in enumerate(out_refs):
        dx, dy = divmod(index, 2)
        lanes = pl.ds(pl.multiple_of((x ^ dx) * half, half), half)
        for z in range(4):
            ref[z] = paired(groups, z, y ^ dy, lanes).astype(ref.dtype)


def split_first_kernel(counts, index_ref, *refs):
    x, y = index_ref[0], index_ref[1]
    groups, (own_ref, sent_ref, own_row_ref, sent_row_ref) = read_groups(counts, refs)
    half = HALF // 2
    for dx, ref in enumerate((own_ref, sent_ref)):
        lanes = pl.ds(pl.multiple_of((x ^ dx) * half, half), half)
        for z in (0, 1):
            for row in (0, 1):
                ref[z, row] = paired(groups, z, row, lanes).astype(ref.dtype)
    for dy, ref in enumerate((own_row_ref, sent_row_ref)):
        for z in (0, 1):
            ref[z] = paired(groups, z + 2, y ^ dy, slice(None)).astype(ref.dtype)


def split_second_kernel(index_ref, own_ref, moved_ref, own_row_ref, moved_row_ref, *out_refs):
    x, y = index_ref[0], index_ref[1]
    total_ref, sent_ref, sent_row_ref = out_refs
    half = HALF // 2
    for z in (0, 1):
        for step, ref, at in ((0, total_ref, z), (1, sent_ref, z)):
            part = own_ref[z, y ^ step] + moved_ref[z, y ^ step].astype(F32)
            ref[at] = part.astype(ref.dtype)
        for step, ref, at in ((0, total_ref, z + 2), (1, sent_row_ref, z)):
            lanes = pl.ds(pl.multiple_of((x ^ step) * half, half), half)
            part = own_row_ref[z, :, lanes] + moved_row_ref[z, :, lanes].astype(F32)
            ref[at] = part.astype(ref.dtype)


def split_column_kernel(index_ref, *refs):
    parts, out_refs = refs[:-4], refs[-4:]
    for steps, ref in enumerate(out_refs):
        row = (index_ref[2] + steps) % 4
        total = parts[0][row]
        if len(parts) == 3:
            added = [part[row % 2].astype(F32) for part in parts[1:]]
            total = total + jnp.where(row < 2, *added)
        else:
            total = total + sum(part[row].astype(F32) for part in parts[1:])
        ref[...] = total.astype(ref.dtype)


class Fast:
    parts = 2
    tile = None
    limit = staticmethod(lambda mib: mib)

    def __init__(self):
        self.section = lax.axis_index("section")
        self.z = lax.axis_index("ctx")
        f = lax.axis_index("fsdp")
        self.y = f // 2
        self.core = f % 2


    def positions_of(self, dz, dc, rows):
        member = 2 * ((self.z % 2) ^ dz) + (self.core ^ dc)
        iota = jnp.arange(rows // 2, dtype=I32)
        return jnp.concatenate([half * (rows // 2) + iota for half in (member, 7 - member)])

    def lengths(self, lengths):
        mine = lax.dynamic_index_in_dim(lengths[0], self.section, 0, keepdims=False)
        other = swap_core(mine)
        return jnp.where(self.z // 2 == self.core, mine, other)

    def spread(self, block):
        half = block.shape[0] // 2
        even, odd = (
            lax.ppermute(block[k * half : (k + 1) * half], ("ctx", "fsdp"), spread_pairs(k))
            for k in (0, 1)
        )
        low = jnp.where(self.core == 0, even, odd)
        return jnp.concatenate([low, jnp.where(self.core == 0, odd, even)], axis=0)

    def unspread(self, block):
        half = block.shape[0] // 2
        low, high = block[:half], block[half:]
        parts = (jnp.where(self.core == 0, low, high), jnp.where(self.core == 0, high, low))
        return jnp.concatenate(
            [
                lax.ppermute(part, ("ctx", "fsdp"), backwards(spread_pairs(k)))
                for k, part in enumerate(parts)
            ],
            axis=0,
        )

    def key_positions(self, rows):
        at = lax.broadcasted_iota(I32, (1, 4 * rows), 1)
        half = rows // 2
        piece = at // half % 4
        member = 2 * ((self.z % 2) ^ (piece % 2)) + (self.core ^ (piece // 2))
        return jnp.where(at < 4 * half, member, 7 - member) * half + at % half

    def jobs(self, rows, keys):
        half = rows // 2
        return ((0, half, 0, keys // 2), (half, half, 0, keys))

    def back_jobs(self, rows, keys):
        return ((0, rows, 0, keys // 2), (rows // 2, rows // 2, keys // 2, keys // 2))

    def share_pairs(self, pairs):
        along = swap_zpair(pairs)
        return [part[None] for part in (pairs, along, swap_core(pairs), swap_core(along))]

    def reduce_pairs(self, grads):
        near, far = grads
        received = swap_core(far)
        along = near[1].astype(F32) + received[1].astype(F32)
        return [near[0], received[0], swap_zpair(along.astype(BF))]


    def halves(self, part):
        return self.lanes(part, self.section), swap_x(self.lanes(part, 1 - self.section))

    def pack_mixed(self, mixed, gains):
        gains = jnp.pad(gains, ((0, 2), (0, MIXED - mixed.shape[0])))
        return self.halves(jnp.concatenate([mixed, gains], axis=0))

    def pack_deep(self, gate, up, down):
        half = down.shape[0] // 2
        down = jnp.pad(jnp.stack([down[:half], down[half:]], axis=1), ((0, 0), (0, 0), (0, HALF - D)))
        return self.halves(jnp.concatenate([gate, up, down.reshape(half, MIXED)], axis=0))

    def start(self, packs, layer, *after):
        start = [jnp.where(self.section == layer, *pack) for pack in packs]
        return tie(jnp.concatenate(start) if len(start) > 1 else start[0], *after)

    def column(self, packs, layer, *after):
        start = self.start(packs, layer, *after)
        return [start] + [lax.ppermute(start, "ctx", ring(4, steps)) for steps in (1, 3, 2)]

    def pair_column(self, packs, layer, *after):
        start = self.start(packs, layer, *after)
        return jnp.stack([start, swap_zpair(start)])

    def double_column(self, pair, *after):
        pair = tie(pair, *after)
        return pair, lax.ppermute(pair, "ctx", flip(4, 2))

    def slices(self, column, rows):
        return [part[rows] for part in column] if len(column) == 4 else [
            part[k, rows] for part in column for k in (0, 1)
        ]

    def square(self, column, *after, rows=slice(None)):
        column = jnp.stack(self.slices(tie(column, *after), rows))
        return column, swap_y(column), swap_x(column), swap_corner(column)

    def gather_square(self, square, *after):
        pieces = jnp.stack(tie(square, *after))
        return [pieces, swap_core(pieces)]

    def first_phase(self, column, *after, rows=slice(None)):
        column = self.slices(tie(column, *after), rows)
        first, second = jnp.stack(column[:2]), jnp.stack(column[2:])
        return first, swap_y(first), second, swap_x(second)

    def second_phase(self, phase, *after):
        phase = tie(phase, *after)
        first, second = jnp.concatenate(phase[:2]), jnp.concatenate(phase[2:])
        return first, swap_x(first), second, swap_y(second)

    def early_core(self, phase):
        return [swap_core(phase[0]), swap_core(phase[2])]

    def gather_phase(self, phase, early, *after):
        phase = tie(phase, *after)
        late = [swap_core(phase[1]), swap_core(phase[3])]
        return [*phase, early[0], late[0], early[1], late[1]]

    def assemble(self, pieces, rows, doubled, *after):
        pieces = tie(pieces, *after)
        mixed = pieces[0].shape[-2] < 2 * rows
        if mixed:
            outs = (struct((D, MIXED), BF), struct((1, D), F32), struct((1, D), F32))
        else:
            depth = 32 * (pieces[0].shape[-2] - 2 * rows)
            outs = (struct((D, MIXED), BF), struct((D, MIXED), BF), struct((depth, D), BF))
        weights = pl.pallas_call(
            functools.partial(assemble_kernel, mixed, doubled),
            out_shape=outs,
            in_specs=[pl.BlockSpec(memory_space=pltpu.SMEM)]
            + [pl.BlockSpec(memory_space=pltpu.VMEM)] * len(pieces),
            compiler_params=pltpu.CompilerParams(vmem_limit_bytes=20 * MIB),
            name="assemble",
        )(jnp.stack([self.section, self.z, self.y, self.core]), *pieces)
        return weights

    def lanes(self, value, x):
        half = value.shape[-1] // 2
        return lax.dynamic_slice_in_dim(value, x * half, half, value.ndim - 1)

    def row(self, value, y):
        return lax.dynamic_index_in_dim(value, y, 1, keepdims=False)

    def reduce_core(self, keep, send):
        return keep, [swap_core(part) for part in send]

    def index(self):
        return jnp.stack([self.section, self.y, self.z])

    def split(self, kernel, shapes, groups, name):
        rows = sum(keep[0].shape[1] for keep, _ in groups)
        args = [part for pair in groups for parts in pair for part in parts]
        return vmem_call(
            functools.partial(kernel, [len(keep) for keep, _ in groups]),
            [struct(shape[:-1] + (rows, shape[-1]), dtype) for shape, dtype in shapes],
            (self.index(), *args),
            scalars=1,
            limit=20,
            name=name,
        )

    def split_square(self, *groups):
        shapes = [((4, HALF // 2), F32)] + [((4, HALF // 2), BF)] * 3
        return self.split(split_square_kernel, shapes, groups, "split_square")

    def move_square(self, parts):
        swaps = (swap_y, swap_x, swap_corner)
        return [parts[0]] + [swap(part) for swap, part in zip(swaps, parts[1:])]

    def split_first(self, *groups):
        shapes = [((2, 2, HALF // 2), F32), ((2, 2, HALF // 2), BF), ((2, HALF), F32), ((2, HALF), BF)]
        return self.split(split_first_kernel, shapes, groups, "split_first")

    def move_first(self, parts):
        return [parts[0], swap_x(parts[1]), parts[2], swap_y(parts[3])]

    def split_second(self, parts):
        rows = parts[0].shape[2]
        return vmem_call(
            split_second_kernel,
            [struct((4, rows, HALF // 2), F32)] + [struct((2, rows, HALF // 2), BF)] * 2,
            (self.index(), *parts),
            scalars=1,
            limit=20,
            name="split_second",
        )

    def move_second(self, parts):
        return [parts[0], swap_y(parts[1]), swap_x(parts[2])]

    def split_column(self, parts):
        shape = parts[0].shape[1:]
        return vmem_call(
            split_column_kernel,
            [struct(shape, F32)] + [struct(shape, BF)] * 3,
            (self.index(), *parts),
            scalars=1,
            limit=20,
            name="split_column",
        )

    def move_column(self, parts):
        return [parts[0]] + [
            lax.ppermute(part, "ctx", ring(4, steps)) for steps, part in zip((1, 2, 3), parts[1:])
        ]

    def total(self, parts, rows=slice(None)):
        return sum(part[rows].astype(F32) for part in parts)

    def cross(self, first, second):
        own = jnp.where(self.section == 0, first, second)
        other = swap_x(jnp.where(self.section == 0, second, first).astype(BF)).astype(F32)
        left = jnp.where(self.section == 0, own, other)
        return jnp.concatenate([left, jnp.where(self.section == 0, other, own)], axis=1)

    def own_rows(self, parts, rows):
        wide = jnp.stack(parts).reshape(len(parts), 2, rows, HALF)
        keep = lax.dynamic_index_in_dim(wide, self.core, 1, keepdims=False)
        sent = lax.dynamic_index_in_dim(wide, 1 - self.core, 1, keepdims=False)
        received = swap_core(sent.astype(BF)).astype(F32)
        left = jnp.where(self.core == 0, keep, received)
        right = jnp.where(self.core == 0, received, keep)
        return jnp.concatenate([left, right], axis=2)

    def finish_deep(self, deep, rows):
        wide = self.own_rows([deep[: 2 * rows], deep[2 * rows : 4 * rows]], rows)
        return wide[0], wide[1], deep[4 * rows :, :D]

    def finish(self, mixed, deep, rows):
        gains = mixed[2 * rows : 2 * rows + 2, :rows]
        wide = self.own_rows([mixed[: 2 * rows]], rows)
        return (wide[0], deep[0], deep[1]), deep[2], gains


class Plain:
    parts = 1
    tile = 16
    limit = staticmethod(lambda mib: 60)

    def __init__(self):
        self.section = lax.axis_index("section")
        self.ctx = lax.axis_index("ctx")
        self.core = jnp.zeros((), I32)

    def positions_of(self, dz, dc, rows):
        return self.ctx * rows + jnp.arange(rows, dtype=I32)

    def lengths(self, lengths):
        return lax.dynamic_index_in_dim(lengths[0], self.section, 0, keepdims=False)

    def spread(self, block):
        return block

    def unspread(self, block):
        return block

    def key_positions(self, rows):
        return jnp.arange(lax.axis_size("ctx") * rows, dtype=I32)[None]

    def jobs(self, rows, keys):
        return ((0, rows, 0, keys),)

    back_jobs = jobs

    def share_pairs(self, pairs):
        return [lax.all_gather(pairs, "ctx", axis=0)]

    def reduce_pairs(self, grads):
        return [lax.psum_scatter(grads[0], "ctx", scatter_dimension=0)]

    def pack_mixed(self, *own):
        return own, tuple(swap_x(part) for part in own)

    pack_deep = pack_mixed

    def column(self, packs, layer, *after):
        return [jnp.where(self.section == layer, a, b) for pack in packs for a, b in zip(*pack)]

    def pair_column(self, packs, layer, *after):
        return self.column(packs, layer)

    def double_column(self, pair, *after):
        return pair

    def square(self, column, *after, rows=slice(None)):
        if len(column) == 5:
            return column[:2] if rows.start is None else column[2:]
        return column

    first_phase = square

    def gather_square(self, square, *after):
        return square

    second_phase = gather_square

    def early_core(self, phase):
        return ()

    def gather_phase(self, phase, early, *after):
        return phase

    def assemble(self, square, rows, doubled, *after):
        axes = ("ctx", "fsdp")
        weights = [
            lax.all_gather(part, axes, axis=int(part.shape[0] == 2), tiled=True) for part in square
        ]
        if len(weights) == 2:
            gains = weights[1].astype(F32)
            return weights[0], gains[:1], gains[1:]
        return weights

    def reduce_core(self, keep, send):
        return keep, send

    def split_square(self, *groups):
        return groups

    split_first = split_square

    def move_square(self, groups):
        return groups

    move_first = split_second = move_second = split_column = move_column = move_square

    def total(self, groups, rows=slice(None)):
        return groups[rows.start is not None]

    def reduce(self, mixed, deep):
        mixed, deep = ([jnp.concatenate(part) for part in pair] for pair in (mixed, deep))

        def columns(pair, first):
            return jnp.concatenate([part[:, first : first + 72] for part in pair], axis=2)

        wide = jnp.stack([columns(mixed, 0), columns(deep, 0), columns(deep, 72)])
        down = jnp.stack([part[:, 144:, :D] for part in deep], axis=1)
        gains = jnp.stack([part[:, 72:74, :36] for part in mixed], axis=1)
        gains = jnp.moveaxis(gains.reshape(16, 2, 36), 1, 0)
        axes = ("ctx", "fsdp")
        return tuple(
            lax.psum_scatter(part, axes, scatter_dimension=axis, tiled=True).astype(F32)
            for part, axis in (
                (wide.reshape(3, D, MIXED), 1),
                (down.reshape(-1, D), 0),
                (gains.reshape(2, D), 1),
            )
        )

    def cross(self, first, second):
        return first, second

    def finish_deep(self, deep, rows):
        return deep

    def finish(self, mixed, deep, rows):
        first, second = (self.reduce(*pair) for pair in zip(mixed, deep))
        return tuple(
            jnp.where(self.section == 0, a, b) + swap_x(jnp.where(self.section == 0, b, a))
            for a, b in zip(first, second)
        )


def vmem_call(kernel, out_shape, args, scratch=(), scalars=0, limit=16, name=None):
    specs = [pl.BlockSpec(memory_space=pltpu.SMEM)] * scalars
    specs += [pl.BlockSpec(memory_space=pltpu.VMEM)] * (len(args) - scalars)
    return pl.pallas_call(
        kernel,
        out_shape=out_shape,
        in_specs=specs,
        scratch_shapes=list(scratch),
        compiler_params=pltpu.CompilerParams(vmem_limit_bytes=limit * MIB),
        name=name,
    )(*args)


def project(net, source, mixed, g_attn, place):
    rows = source.shape[0]
    queries, pairs = vmem_call(
        project_kernel,
        (struct((rows, QW), BF), struct((rows, 2 * KW), BF)),
        (source, mixed, g_attn, place[2], place[3]),
        limit=8,
        name="project",
    )
    return queries, pairs


def attend_forward(net, source, queries, pieces, mixed, place):
    positions, starts, _, _, key_positions = place
    rows, keys = source.shape[0], key_positions.shape[1]
    return vmem_call(
        functools.partial(attend_kernel, net.jobs(rows, keys), net.tile, net.parts, len(pieces)),
        (struct((rows, QW), F32), struct((rows, HQ), F32), struct((rows, D), F32)),
        (source, queries, positions, starts, key_positions, mixed, *pieces),
        [
            pltpu.VMEM((HQ, rows, HD), BF),
            pltpu.VMEM((KV, keys, HD), BF),
            pltpu.VMEM((KV, keys, HD), BF),
            pltpu.VMEM((HQ, rows, HD), F32),
            pltpu.VMEM((HQ, rows, 1), F32),
        ],
        limit=net.limit(16),
        name="attend",
    )


def mlp_forward(middle, gate, up, down, g_mlp):
    rows = middle.shape[0]
    return vmem_call(
        mlp_kernel,
        struct((rows, D), BF),
        (middle, gate, up, down, g_mlp),
        [pltpu.VMEM((rows, D), BF), pltpu.VMEM((rows, D), F32)],
        limit=12,
        name="mlp",
    )


def mlp_backward(net, d_result, middle, mixed, gate, up, down, g_mlp):
    rows = middle.shape[0]
    deep_rows = 144 + down.shape[0] // 16
    shapes = [struct((4, deep_rows, HALF), BF)] * 4
    outs = vmem_call(
        mlp_back_kernel,
        shapes + [struct((1, D), F32), struct((rows, D), F32), struct((rows, QW), BF)],
        (net.core.reshape(1), d_result, middle, mixed, gate, up, down, g_mlp),
        [pltpu.VMEM((rows, D), BF), pltpu.VMEM((rows, D), F32)],
        scalars=1,
        limit=22,
        name="mlp_back",
    )
    return outs[:2], outs[2:4], *outs[4:]


def attend_backward(net, d_attended, attended, log_total, queries, pieces, place):
    positions, starts, _, _, key_positions = place
    rows, keys = positions.shape[0], key_positions.shape[1]
    return vmem_call(
        functools.partial(
            attend_back_kernel, net.back_jobs(rows, keys), net.tile, net.parts, len(pieces)
        ),
        [struct((rows, QW), F32)]
        + [struct((keys // rows // net.parts, rows, 2 * KW), BF)] * net.parts,
        (d_attended, attended, log_total, queries, positions, starts, key_positions, *pieces),
        [
            pltpu.VMEM((HQ, rows, HD), BF),
            pltpu.VMEM((KV, keys, HD), BF),
            pltpu.VMEM((KV, keys, HD), BF),
            pltpu.VMEM((HQ, rows, HD), BF),
            pltpu.VMEM((HQ, rows, 1), F32),
            pltpu.VMEM((HQ, rows, 1), F32),
            pltpu.VMEM((HQ, rows, HD), F32),
            pltpu.VMEM((KV, HD, keys), F32),
            pltpu.VMEM((KV, HD, keys), F32),
        ],
        limit=net.limit(22),
        name="attend_back",
    )


def input_backward(
    net, source, attended, d_middle, d_queries, adds, gain_grad, mixed, g_attn, place
):
    rows = source.shape[0]
    mixed_shape = struct((8, 80, HALF), BF)
    d_source, keep, send = vmem_call(
        functools.partial(input_kernel, len(adds)),
        (struct((rows, D), BF), mixed_shape, mixed_shape),
        (
            net.core.reshape(1), source, attended, d_middle, d_queries, mixed, g_attn, gain_grad,
            place[2], place[3], *adds,
        ),
        scalars=1,
        limit=12,
        name="input",
    )
    return d_source, [keep], [send]


def shards(
    inputs, lengths, cotangent, w_query, w_key, w_value, w_out, w_gate, w_up, w_down, g_attn, g_mlp
):
    sizes = tuple(lax.axis_size(axis) for axis in ("section", "ctx", "fsdp"))
    net = Fast() if sizes == (2, 4, 4) else Plain()
    rows = inputs.shape[2]
    mixed = jnp.concatenate([w_query[0], w_key[0], w_out[0], w_value[0]], axis=1)
    mixed_pack = net.pack_mixed(mixed, jnp.stack([g_attn[0], g_mlp[0]]))
    shard = w_query.shape[1]
    lengths, gate, up, down, inputs, cotangent = tie(
        (lengths, w_gate[0], w_up[0], w_down[0], inputs, cotangent), mixed_pack[0]
    )
    deep_pack = net.pack_deep(gate, up, down)
    mixed_column = net.column([mixed_pack], 0)
    own = net.lengths(lengths)
    positions = net.positions_of(0, 0, rows)
    passed = (positions[:, None] >= jnp.cumsum(own)[None, :]).astype(I32)
    starts = jnp.sum(passed * own[None, :], axis=1)
    cosine, sine = turn_tables(positions - starts)
    place = (positions[:, None], starts[:, None], cosine, sine, net.key_positions(rows))
    source = lax.dynamic_index_in_dim(inputs[0], net.section, 0, keepdims=False)
    d_result = lax.dynamic_index_in_dim(cotangent[0], net.section, 0, keepdims=False)
    mixed_square = net.square(mixed_column)
    deep_column = net.column([deep_pack], 0, mixed_column)
    source, d_result, place = tie((source, d_result, place), mixed_column)
    mixed_rows = mixed_square[0].shape[-2]
    mixed_pieces = net.gather_square(mixed_square)
    deep_phase = net.first_phase(deep_column, mixed_square)
    source = net.spread(tie(source, deep_column))
    mixed_0, g_attn_0, g_mlp_0 = net.assemble(mixed_pieces, shard, False)

    queries_0, pairs = project(net, source, mixed_0, g_attn_0, place)
    deep_phase = net.second_phase(deep_phase, source)
    pieces_0 = net.share_pairs(pairs)
    column = net.pair_column([mixed_pack, deep_pack], 1, queries_0)
    early = net.early_core(deep_phase)
    column = net.double_column(column, pieces_0)
    attended_0, log_0, middle_0 = attend_forward(net, source, queries_0, pieces_0, mixed_0, place)
    middle_0, column, deep_phase, early = tie((middle_0, column, deep_phase, early))
    mixed_square = net.square(column, rows=slice(None, mixed_rows))
    deep_0 = net.assemble(net.gather_phase(deep_phase, early), shard, False)
    first = mlp_forward(middle_0, *deep_0, g_mlp_0)
    first, mixed_square = tie((first, mixed_square))
    mixed_pieces = net.gather_square(mixed_square)
    deep_phase = net.first_phase(column, mixed_square, rows=slice(mixed_rows, None))
    mixed_1, g_attn_1, g_mlp_1 = net.assemble(mixed_pieces, shard, True)

    queries_1, pairs = project(net, first, mixed_1, g_attn_1, place)
    pieces_1 = net.share_pairs(pairs)
    deep_phase = net.second_phase(deep_phase, queries_1)
    d_result = net.spread(tie(d_result, pieces_1))
    attended_1, log_1, middle_1 = attend_forward(net, first, queries_1, pieces_1, mixed_1, place)
    middle_1, deep_phase, d_result = tie((middle_1, deep_phase, d_result))
    deep_1 = net.assemble(
        net.gather_phase(deep_phase, net.early_core(deep_phase)), shard, True
    )

    deep_keep, deep_send, gain_grad, d_middle, d_attended = mlp_backward(
        net, d_result, middle_1, mixed_1, *deep_1, g_mlp_1
    )
    deep_sum = net.reduce_core(deep_keep, deep_send)
    d_queries, *d_pairs = attend_backward(
        net, d_attended, attended_1, log_1, queries_1, pieces_1, place
    )
    d_queries, d_pairs, deep_sum = tie((d_queries, d_pairs, deep_sum))
    deep_sum = net.split_first(deep_sum)
    d_pairs = tie(d_pairs, deep_sum)
    deep_sum = net.move_first(deep_sum)
    second = mlp_forward(tie(middle_1, d_pairs), *deep_1, g_mlp_1)
    adds = tie(net.reduce_pairs(d_pairs), second)
    outs = input_backward(
        net, first, attended_1, d_middle, d_queries, adds, gain_grad, mixed_1, g_attn_1, place
    )
    (d_first, mixed_keep, mixed_send), deep_sum = tie((outs, deep_sum))
    deep_sum = net.split_second(deep_sum)
    d_first = tie(d_first, deep_sum)
    deep_sum = net.move_second(deep_sum)
    mixed_sum = net.reduce_core(mixed_keep, mixed_send)
    second = net.unspread(tie(second, d_first))

    outs = mlp_backward(net, d_first, middle_0, mixed_0, *deep_0, g_mlp_0)
    outs, mixed_sum, deep_sum, second = tie((outs, mixed_sum, deep_sum, second))
    deep_keep, deep_send, gain_grad, d_middle, d_attended = outs
    deep_sum = net.split_column(deep_sum)
    d_attended = tie(d_attended, deep_sum)
    deep_sum_1 = net.move_column(deep_sum)
    sums = net.split_first(mixed_sum, net.reduce_core(deep_keep, deep_send))
    d_attended = tie(d_attended, sums)
    sums = net.move_first(sums)
    d_queries, *d_pairs = attend_backward(
        net, d_attended, attended_0, log_0, queries_0, pieces_0, place
    )
    d_queries, d_pairs, sums, deep_sum_1 = tie((d_queries, d_pairs, sums, deep_sum_1))
    sums = net.split_second(sums)
    d_pairs = tie(d_pairs, sums)
    sums = net.move_second(sums)
    deep_sum_1 = net.total(deep_sum_1)
    adds = tie(net.reduce_pairs(d_pairs), deep_sum_1)
    d_input, mixed_keep, mixed_send = input_backward(
        net, source, attended_0, d_middle, d_queries, adds, gain_grad, mixed_0, g_attn_0, place
    )
    d_input, mixed_keep, mixed_send, sums = tie((d_input, mixed_keep, mixed_send, sums))
    sums = net.move_column(net.split_column(sums))

    mixed_sum = net.split_square(net.reduce_core(mixed_keep, mixed_send))
    d_input = net.unspread(tie(d_input, mixed_sum))
    mixed_sum = net.move_square(mixed_sum)
    mixed_sum, d_input = tie((mixed_sum, d_input))
    mixed_sum = net.split_column(mixed_sum)
    sums, d_input = tie((sums, d_input), mixed_sum)
    mixed_sum = net.move_column(mixed_sum)
    mixed_sum_1 = net.total(sums, slice(None, 80))
    deep_sum = net.cross(net.total(sums, slice(80, None)), deep_sum_1)
    kept = jnp.where(net.section == 0, d_input, second)
    crossed = swap_x(jnp.where(net.section == 0, second, d_input))
    mixed_sum, crossed, deep_sum = tie((mixed_sum, crossed, deep_sum))
    edges = jnp.stack(
        [jnp.where(net.section == 0, kept, crossed), jnp.where(net.section == 0, crossed, kept)]
    ).astype(F32)
    mixed_sum = net.cross(net.total(mixed_sum), mixed_sum_1)
    deep_sum = net.finish_deep(deep_sum, shard)
    mixed_sum, edges, deep_sum = tie((mixed_sum, edges, deep_sum))
    wide_grad, down_grad, gain_grads = net.finish(mixed_sum, deep_sum, shard)
    mixed = wide_grad[0]
    return (
        edges[None, None],
        mixed[None, :, :QW],
        mixed[None, :, QW:TURNED],
        mixed[None, :, TURNED + QW :],
        mixed[None, :, TURNED : TURNED + QW],
        wide_grad[1][None],
        wide_grad[2][None],
        down_grad[None],
        gain_grads[0][None],
        gain_grads[1][None],
    )


def solution(mesh):
    rows = P("section", ("ctx", "fsdp"), None)
    gains = P("section", ("ctx", "fsdp"))
    blocks = P("fsdp", None, "ctx", None)
    return jax.shard_map(
        shards,
        mesh=mesh,
        in_specs=(blocks, P("fsdp", None, None), blocks) + (rows,) * 7 + (gains,) * 2,
        out_specs=(P("section", "fsdp", None, "ctx", None),) + (rows,) * 7 + (gains,) * 2,
        check_vma=False,
    )
```
